256 devices in a mesh: nodes: 32 (over x, z), feat: 8 (over y, core).
Axes of the slice: x: 4, y: 4, z: 8, core: 2. Of those that a mesh axis runs over, the one named last changes fastest.
Arguments:
- features: bfloat16 [65536, 768], P('nodes', 'feat'), may hold values from -6 to 6
- w_self: bfloat16 [768, 1024], replicated, may hold values from -0.21875 to 0.21875
- w_neigh: bfloat16 [768, 1024], replicated, may hold values from -0.21875 to 0.21875
- src_tiles: int32 [256, 64], P('nodes'), may hold values from 0 to 255
- counts: int32 [256], P('nodes'), may hold values from 1 to 64, as said below
- edge_rows: int32 [256, 64, 256], P('nodes'), may hold values from 0 to 255
- cotangent: bfloat16 [65536, 1024], P(('nodes', 'feat')), may hold values from -24 to 24
Outputs:
- activations: bfloat16 [65536, 1024], P(('nodes', 'feat'))
- weight_grads: float32 [768, 2048], P('feat', 'nodes')
The draws below stay inside these ranges and needn't reach their ends.
Inputs may be any that keep to these rules, and one draw needn't show every extreme that they name: Slots from counts[t] on are ignored; some tile uses all 64 slots.
All inputs are finite; a program needn't handle non-finite values.
Results may differ from the reference program's by a relative error of at most 0.0033.
Values may be sent and summed in bfloat16 or wider, within the bound.
A program may use at most 128 MiB of HBM per device.

```python
from functools import partial
import jax
import jax.numpy as jnp
from jax import lax

F = 768
H = 1024
TILE = 256
SLOTS = 64
ROWS = 2048
NODES = 65536
NTILES = 256


def draw_counts(key, part):
    key = jax.random.fold_in(key, 7)
    key_level, key_base, key_full = jax.random.split(key, 3)
    per_block = ROWS // TILE
    levels = jax.random.randint(key_level, (NTILES // per_block,), 1, SLOTS + 1)
    level_rows = jnp.repeat(levels, per_block)
    base = jax.random.randint(key_base, (NTILES,), 0, SLOTS) % level_rows + 1
    full_tile = jax.random.randint(key_full, (), 0, NTILES)
    return jnp.where(jnp.arange(NTILES) == full_tile, SLOTS, base).astype(jnp.int32)


def touch_ends(array, rng, least, largest):
    place = [jax.random.randint(jax.random.fold_in(rng, axis), (), 0, length) for axis, length in enumerate(array.shape)]
    main_axis = array.shape.index(max(array.shape))
    next_to = place[:main_axis] + [(place[main_axis] + 1) % array.shape[main_axis]] + place[main_axis + 1:]
    return array.at[tuple(place)].set(least).at[tuple(next_to)].set(largest)


def spiked(values, stream_key, source, target, shards_of, factor):
    owner, partner = [(jnp.arange(values.shape[position]) // (values.shape[position] // shards_of)).reshape([-1 if axis == position else 1 for axis in range(values.ndim)]) for position in (source, target)]
    chosen = jax.random.permutation(stream_key, shards_of)[partner]
    strong = (owner == chosen) | (owner == (partner + shards_of // 2) % shards_of)
    return jnp.where(strong, factor * values, values)


def shard_levels(stream_key, dims, shards, smallest, largest):
    def one(dim, shards_of):
        heights = jax.random.uniform(jax.random.fold_in(jax.random.fold_in(stream_key, 6), dim), (shards_of,), jnp.float32, smallest / len(shards), largest / len(shards))
        return jnp.repeat(jnp.exp(heights), dims[dim] // shards_of).reshape((-1,) + (1,) * (len(dims) - dim - 1))

    loudness = one(*shards[0])
    for cut in shards[1:]:
        loudness = loudness * one(*cut)
    return loudness


def centred(key, shape, spread, limit, pieces=(), kind=jnp.bfloat16):
    gain = shard_levels(key, shape, pieces, -0.22, 0.18) if pieces else 1.0
    array = jax.random.normal(key, shape, jnp.float32) * spread * gain
    return jnp.minimum(jnp.maximum(array, -limit), limit).astype(kind)


def noise_with(rng, extent, deviation, limit, cuts, heavy, kind=jnp.bfloat16):
    values = deviation * jax.random.normal(rng, extent, jnp.float32)
    if cuts:
        values = values * shard_levels(rng, extent, cuts, -0.22, 0.18)
    return jnp.clip(spiked(values, jax.random.fold_in(rng, 3), *heavy), -limit, limit).astype(kind)


def setup_inputs(seed: int = 0) -> dict:
    splits = jax.random.split(jax.random.key(seed), 8)
    features = centred(splits[0], (NODES, F), 1.0, 6.0, ((0, 32), (1, 8)))
    w_self = centred(splits[1], (F, H), F ** -0.5, 0.21875)
    w_neigh = centred(splits[2], (F, H), F ** -0.5, 0.21875)
    src_tiles = touch_ends(jax.random.randint(splits[3], (NTILES, SLOTS), 0, NTILES), jax.random.fold_in(splits[3], 1), 0, NTILES - 1).astype(jnp.int32)
    counts = draw_counts(jax.random.fold_in(splits[7], 71), 0)
    edge_rows = touch_ends(jax.random.randint(splits[5], (NTILES, SLOTS, TILE), 0, TILE), jax.random.fold_in(splits[5], 1), 0, TILE - 1).astype(jnp.int32)
    cotangent = noise_with(splits[6], (NODES, H), 1.0, 24.0, ((0, 256),), (0, 1, 256, 6.0))
    return dict(features=features, w_self=w_self, w_neigh=w_neigh, src_tiles=src_tiles, counts=counts, edge_rows=edge_rows, cotangent=cotangent)


def reference(features, w_self, w_neigh, src_tiles, counts, edge_rows, cotangent):
    tile_view = features.reshape(NTILES, TILE, F)

    def one_tile(tile_index):
        source_ids = src_tiles[tile_index]
        blocks = tile_view[source_ids]
        picked = jnp.take_along_axis(blocks, edge_rows[tile_index][:, :, None], axis=1)
        live_slots = jnp.arange(SLOTS) < counts[tile_index]
        summed = lax.optimization_barrier(jnp.sum(jnp.where(live_slots[:, None, None], picked.astype(jnp.float32), 0.0), axis=0))
        return (summed / counts[tile_index].astype(jnp.float32)).astype(jnp.bfloat16)
    agg = lax.map(one_tile, jnp.arange(NTILES)).reshape(NODES, F)
    preact = jnp.dot(features, w_self, preferred_element_type=jnp.float32) + jnp.dot(agg, w_neigh, preferred_element_type=jnp.float32)
    outputs, pullback = jax.vjp(partial(jax.nn.gelu, approximate=True), preact)
    grad_z = pullback(cotangent.astype(preact.dtype))[0].astype(jnp.bfloat16)
    grad_self = jnp.dot(features.T, grad_z, preferred_element_type=jnp.float32)
    grad_neigh = jnp.dot(agg.T, grad_z, preferred_element_type=jnp.float32)
    return (outputs.astype(jnp.bfloat16), jnp.concatenate([grad_self, grad_neigh], axis=1))
```

```python
import functools
from functools import partial

import jax
import jax.numpy as jnp
from jax import lax
from jax.experimental import pallas as pl
from jax.experimental.pallas import tpu as pltpu
from jax.sharding import PartitionSpec as P

UNROLL = 8


def agg_kernel(src_ref, cnt_ref, rows_ref, g_ref, out_ref, picks_ref):
    tiles, slots, span = rows_ref.shape
    cols = g_ref.shape[1]
    per_block = g_ref.shape[2] // span
    iota = lax.broadcasted_iota(jnp.int32, (span, span), 0).astype(jnp.float32).astype(jnp.bfloat16)
    one = jnp.ones((span, span), jnp.bfloat16)
    zero = jnp.zeros((span, span), jnp.bfloat16)
    slot_ids = lax.broadcasted_iota(jnp.int32, (slots, span), 0)

    def tile(t, carry):
        used = cnt_ref[t]
        picks_ref[...] = jnp.where(slot_ids < used, rows_ref[t], -1).astype(jnp.float32)

        def step(i, acc):
            onehots, blocks = [], []
            for u in range(UNROLL):
                k = i * UNROLL + u
                pick = jnp.broadcast_to(picks_ref[pl.ds(k, 1), :], (16, span)).astype(jnp.bfloat16)
                pick = jnp.concatenate([pick] * (span // 16), axis=0)
                onehots.append(jnp.where(pick == iota, one, zero))
                s = src_ref[t, k]
                start = pl.multiple_of((s % per_block) * span, span)
                blocks.append(g_ref[s // per_block, :, pl.ds(start, span)])
            return acc + jnp.dot(
                jnp.concatenate(blocks, axis=1),
                jnp.concatenate(onehots, axis=0),
                preferred_element_type=jnp.float32,
            )

        total = lax.fori_loop(0, (used + UNROLL - 1) // UNROLL, step, jnp.zeros((cols, span), jnp.float32))
        mean = total / used.astype(jnp.float32)
        out_ref[:, pl.ds(pl.multiple_of(t * span, span), span)] = mean.astype(jnp.bfloat16)
        return carry

    lax.fori_loop(0, tiles, tile, 0)


def neighbour_mean(src_tiles, counts, edge_rows, gathered):
    tiles, slots, span = edge_rows.shape
    cols = gathered.shape[1]
    return pl.pallas_call(
        agg_kernel,
        out_shape=jax.ShapeDtypeStruct((cols, tiles * span), jnp.bfloat16),
        in_specs=[pl.BlockSpec(memory_space=pltpu.SMEM)] * 2 + [pl.BlockSpec(memory_space=pltpu.VMEM)] * 2,
        out_specs=pl.BlockSpec(memory_space=pltpu.VMEM),
        scratch_shapes=[pltpu.VMEM((slots, span), jnp.float32)],
        compiler_params=pltpu.CompilerParams(vmem_limit_bytes=40 * 2**20),
    )(src_tiles, counts, edge_rows, gathered)


def per_device(features, w_self, w_neigh, src_tiles, counts, edge_rows, cotangent):
    cols = features.shape[1]
    feat_t = features.T
    gathered = lax.all_gather(feat_t, "nodes", axis=0)
    agg_t = neighbour_mean(src_tiles, counts, edge_rows, gathered)
    first = (((0,), (0,)), ((), ()))
    self_rows = lax.all_to_all(feat_t, "feat", split_axis=1, concat_axis=0, tiled=True)
    agg_rows = lax.all_to_all(agg_t, "feat", split_axis=1, concat_axis=0, tiled=True)
    preact = lax.dot_general(self_rows, w_self, first, preferred_element_type=jnp.float32) + lax.dot_general(
        agg_rows, w_neigh, first, preferred_element_type=jnp.float32
    )
    outputs, pullback = jax.vjp(partial(jax.nn.gelu, approximate=True), preact)
    grad_z = pullback(cotangent.astype(jnp.float32))[0].astype(jnp.bfloat16)
    grad_all = lax.all_gather(grad_z, "feat", axis=0, tiled=True)
    term = jnp.dot(jnp.concatenate([feat_t, agg_t], axis=0), grad_all, preferred_element_type=jnp.float32)
    term = jnp.concatenate([term[:cols], term[cols:]], axis=1)
    blocks = lax.axis_size("nodes")
    pieces = term.reshape(cols, blocks, -1).transpose(1, 2, 0)
    pieces = lax.all_to_all(pieces, "nodes", split_axis=0, concat_axis=0, tiled=True)
    return outputs.astype(jnp.bfloat16), jnp.sum(pieces, axis=0).T


def solution(mesh):
    in_specs = (
        P("nodes", "feat"),
        P(),
        P(),
        P("nodes", None),
        P("nodes"),
        P("nodes", None, None),
        P(("nodes", "feat"), None),
    )
    out_specs = (P(("nodes", "feat"), None), P("feat", "nodes"))
    return jax.shard_map(
        per_device, mesh=mesh, in_specs=in_specs, out_specs=out_specs, check_vma=False
    )
```

```python
import functools
from functools import partial

import jax
import jax.numpy as jnp
from jax import lax
from jax.experimental import pallas as pl
from jax.experimental.pallas import tpu as pltpu
from jax.sharding import PartitionSpec as P

UNROLL = 8
MESH = pl.DeviceIdType.MESH

def plan(xs, zs, cut):
    ways = {"x+": (1, 0), "x-": (-1, 0), "z+": (0, 1), "z-": (0, -1)}
    sends = []
    have = {}
    def norm(dx, dz):
        return dx % xs, dz % zs
    def add(way, dx, dz, region, half):
        deps = set()
        for h in ((0, 1) if half is None else (half,)):
            deps |= set(have[(norm(dx, dz), region, h)])
        sid = len(sends)
        sends.append(dict(way=way, off=norm(dx, dz), region=region, half=half, deps=sorted(deps)))
        wx, wz = ways[way]
        got = norm(dx - wx, dz - wz)
        for h in ((0, 1) if half is None else (half,)):
            have.setdefault((got, region, h), []).append(sid)
    for region in (0, 1):
        for h in (0, 1):
            have[((0, 0), region, h)] = []
    def ring(axis, size, region, other):
        for d in range(1, size // 2 + 1):
            for sign, s in (("+", 1), ("-", -1)):
                half = None if d < size // 2 or size % 2 else (0 if s == 1 else 1)
                o = -s * (d - 1)
                off = (o, other) if axis == "x" else (other, o)
                add(axis + sign, off[0], off[1], region, half)
    ring("x", xs, 0, 0)
    ring("z", zs, 1, 0)
    for dx in [0, 1, -1, 2][:xs]:
        ring("z", zs, 0, dx)
    order = [0]
    for d in range(1, zs // 2): order += [d, -d]
    order += [zs // 2]
    for dz in order:
        ring("x", xs, 1, dz)
    return sends

def schedule(sends, cost):
    n = len(sends)
    arrive = {}
    free = {w: 0.0 for w in ("x+", "x-", "z+", "z-")}
    todo = set(range(n))
    LAT = 1.5
    chain = [0] * n
    for i in reversed(range(n)):
        chain[i] = max([chain[j] + 1 for j in range(n) if i in sends[j]["deps"]], default=0)
    starts = {}
    while todo:
        best = None
        for i in todo:
            if any(d not in arrive for d in sends[i]["deps"]): continue
            ready = max([arrive[d] for d in sends[i]["deps"]], default=0.0)
            st = max(ready, free[sends[i]["way"]])
            key = (st, -chain[i], ready, i)
            if best is None or key < best[0]: best = (key, i, ready, st)
        key, i, ready, st = best
        todo.remove(i)
        s = sends[i]
        free[s["way"]] = st + cost(s)
        arrive[i] = st + cost(s) + LAT
        starts[i] = (ready, st)
    seq = []
    waited = set(); started = set()
    for i in sorted(range(n), key=lambda i: starts[i][1]):
        for d in sorted(sends[i]["deps"], key=lambda d: arrive[d]):
            if d not in waited:
                waited.add(d); seq.append(("wait", d))
        seq.append(("start", i))
    for d in sorted(range(n), key=lambda d: arrive[d]):
        if d not in waited: seq.append(("wait", d))
    return seq, max(arrive.values())

def gather_kernel(feat_ref, out_ref, send_sem, recv_sem, own_sem, *, xs, zs, cut, seq, sends):
    me = lax.axis_index("nodes")
    x, z = me // zs, me % zs
    cols, rows = feat_ref.shape
    peers = {"x+": ((x + 1) % xs) * zs + z, "x-": ((x + xs - 1) % xs) * zs + z,
             "z+": x * zs + (z + 1) % zs, "z-": x * zs + (z + zs - 1) % zs}
    barrier = pltpu.get_barrier_semaphore()
    for w in peers:
        pl.semaphore_signal(barrier, inc=1, device_id={"nodes": peers[w]}, device_id_type=MESH)
    pl.semaphore_wait(barrier, len(peers))
    own = pltpu.make_async_copy(feat_ref, out_ref.at[me], own_sem)
    own.start()
    def copy(i):
        s = sends[i]
        dx, dz = s["off"]
        src = ((x + dx) % xs) * zs + (z + dz) % zs
        c = pl.ds(0, cut) if s["region"] == 0 else pl.ds(cut, rows - cut)
        h = cols // 2
        r = pl.ds(0, cols) if s["half"] is None else pl.ds(s["half"] * h, h)
        from_ref = feat_ref.at[r, c] if (dx, dz) == (0, 0) else out_ref.at[src, r, c]
        return pltpu.make_async_remote_copy(
            src_ref=from_ref, dst_ref=out_ref.at[src, r, c], send_sem=send_sem.at[i], recv_sem=recv_sem.at[i],
            device_id={"nodes": peers[s["way"]]}, device_id_type=MESH)
    def arrival(i):
        s = sends[i]
        wx, wz = {"x+": (1, 0), "x-": (-1, 0), "z+": (0, 1), "z-": (0, -1)}[s["way"]]
        dx, dz = s["off"]
        src = ((x + dx - wx) % xs) * zs + (z + dz - wz) % zs
        c = pl.ds(0, cut) if s["region"] == 0 else pl.ds(cut, rows - cut)
        h = cols // 2
        r = pl.ds(0, cols) if s["half"] is None else pl.ds(s["half"] * h, h)
        return pltpu.make_async_remote_copy(
            src_ref=out_ref.at[src, r, c], dst_ref=out_ref.at[src, r, c], send_sem=send_sem.at[i], recv_sem=recv_sem.at[i],
            device_id={"nodes": peers[s["way"]]}, device_id_type=MESH)
    for what, i in seq:
        if what == "start": copy(i).start()
        else: arrival(i).wait_recv()
    for i in range(len(sends)): copy(i).wait_send()
    own.wait()

def gather(feat_t, xs=4, zs=8, cut=768, cid=1):
    cols, rows = feat_t.shape
    sends = plan(xs, zs, cut)
    def cost(s):
        n = cols * (cut if s["region"] == 0 else rows - cut) * 2 * 2 / (1 if s["half"] is None else 2)
        return n / 100e3
    seq, end = schedule(sends, cost)
    return pl.pallas_call(
        functools.partial(gather_kernel, xs=xs, zs=zs, cut=cut, seq=seq, sends=sends),
        out_shape=jax.ShapeDtypeStruct((xs * zs, cols, rows), feat_t.dtype),
        in_specs=[pl.BlockSpec(memory_space=pl.ANY)],
        out_specs=pl.BlockSpec(memory_space=pl.ANY),
        scratch_shapes=[pltpu.SemaphoreType.DMA((len(sends),)), pltpu.SemaphoreType.DMA((len(sends),)), pltpu.SemaphoreType.DMA],
        compiler_params=pltpu.CompilerParams(collective_id=cid, has_side_effects=True),
    )(feat_t)


def agg_kernel(src_ref, cnt_ref, rows_ref, g_ref, out_ref, picks_ref):
    tiles, slots, span = rows_ref.shape
    cols = g_ref.shape[1]
    per_block = g_ref.shape[2] // span
    iota = lax.broadcasted_iota(jnp.int32, (span, span), 0).astype(jnp.float32).astype(jnp.bfloat16)
    one = jnp.ones((span, span), jnp.bfloat16)
    zero = jnp.zeros((span, span), jnp.bfloat16)
    slot_ids = lax.broadcasted_iota(jnp.int32, (slots, span), 0)

    def tile(t, carry):
        used = cnt_ref[t]
        picks_ref[...] = jnp.where(slot_ids < used, rows_ref[t], -1).astype(jnp.float32)

        def step(i, acc):
            onehots, blocks = [], []
            for u in range(UNROLL):
                k = i * UNROLL + u
                pick = jnp.broadcast_to(picks_ref[pl.ds(k, 1), :], (16, span)).astype(jnp.bfloat16)
                pick = jnp.concatenate([pick] * (span // 16), axis=0)
                onehots.append(jnp.where(pick == iota, one, zero))
                s = src_ref[t, k]
                start = pl.multiple_of((s % per_block) * span, span)
                blocks.append(g_ref[s // per_block, :, pl.ds(start, span)])
            return acc + jnp.dot(
                jnp.concatenate(blocks, axis=1),
                jnp.concatenate(onehots, axis=0),
                preferred_element_type=jnp.float32,
            )

        total = lax.fori_loop(0, (used + UNROLL - 1) // UNROLL, step, jnp.zeros((cols, span), jnp.float32))
        mean = total / used.astype(jnp.float32)
        out_ref[:, pl.ds(pl.multiple_of(t * span, span), span)] = mean.astype(jnp.bfloat16)
        return carry

    lax.fori_loop(0, tiles, tile, 0)


def neighbour_mean(src_tiles, counts, edge_rows, gathered):
    tiles, slots, span = edge_rows.shape
    cols = gathered.shape[1]
    return pl.pallas_call(
        agg_kernel,
        out_shape=jax.ShapeDtypeStruct((cols, tiles * span), jnp.bfloat16),
        in_specs=[pl.BlockSpec(memory_space=pltpu.SMEM)] * 2 + [pl.BlockSpec(memory_space=pltpu.VMEM)] * 2,
        out_specs=pl.BlockSpec(memory_space=pltpu.VMEM),
        scratch_shapes=[pltpu.VMEM((slots, span), jnp.float32)],
        compiler_params=pltpu.CompilerParams(vmem_limit_bytes=40 * 2**20),
    )(src_tiles, counts, edge_rows, gathered)


def per_device(features, w_self, w_neigh, src_tiles, counts, edge_rows, cotangent):
    cols = features.shape[1]
    feat_t = features.T
    gathered = gather(feat_t)
    agg_t = neighbour_mean(src_tiles, counts, edge_rows, gathered)
    first = (((0,), (0,)), ((), ()))
    self_rows = lax.all_to_all(feat_t, "feat", split_axis=1, concat_axis=0, tiled=True)
    agg_rows = lax.all_to_all(agg_t, "feat", split_axis=1, concat_axis=0, tiled=True)
    preact = lax.dot_general(self_rows, w_self, first, preferred_element_type=jnp.float32) + lax.dot_general(
        agg_rows, w_neigh, first, preferred_element_type=jnp.float32
    )
    outputs, pullback = jax.vjp(partial(jax.nn.gelu, approximate=True), preact)
    grad_z = pullback(cotangent.astype(jnp.float32))[0].astype(jnp.bfloat16)
    grad_all = lax.all_gather(grad_z, "feat", axis=0, tiled=True)
    term = jnp.dot(jnp.concatenate([feat_t, agg_t], axis=0), grad_all, preferred_element_type=jnp.float32)
    term = jnp.concatenate([term[:cols], term[cols:]], axis=1)
    blocks = lax.axis_size("nodes")
    pieces = term.reshape(cols, blocks, -1).transpose(1, 2, 0)
    pieces = lax.all_to_all(pieces, "nodes", split_axis=0, concat_axis=0, tiled=True)
    return outputs.astype(jnp.bfloat16), jnp.sum(pieces, axis=0).T


def solution(mesh):
    in_specs = (
        P("nodes", "feat"),
        P(),
        P(),
        P("nodes", None),
        P("nodes"),
        P("nodes", None, None),
        P(("nodes", "feat"), None),
    )
    out_specs = (P(("nodes", "feat"), None), P("feat", "nodes"))
    return jax.shard_map(
        per_device, mesh=mesh, in_specs=in_specs, out_specs=out_specs, check_vma=False
    )
```

```python
import functools
import math

import jax
import jax.numpy as jnp
from jax import lax
from jax.experimental import pallas as pl
from jax.experimental.pallas import tpu as pltpu
from jax.sharding import PartitionSpec as P

UNROLL = 8
MESH = pl.DeviceIdType.MESH

def plan(xs, zs, cut):
    ways = {"x+": (1, 0), "x-": (-1, 0), "z+": (0, 1), "z-": (0, -1)}
    sends = []
    have = {}
    def norm(dx, dz):
        return dx % xs, dz % zs
    def add(way, dx, dz, region, half):
        deps = set()
        for h in ((0, 1) if half is None else (half,)):
            deps |= set(have[(norm(dx, dz), region, h)])
        sid = len(sends)
        sends.append(dict(way=way, off=norm(dx, dz), region=region, half=half, deps=sorted(deps)))
        wx, wz = ways[way]
        got = norm(dx - wx, dz - wz)
        for h in ((0, 1) if half is None else (half,)):
            have.setdefault((got, region, h), []).append(sid)
    for region in (0, 1):
        for h in (0, 1):
            have[((0, 0), region, h)] = []
    def ring(axis, size, region, other):
        for d in range(1, size // 2 + 1):
            for sign, s in (("+", 1), ("-", -1)):
                half = None if d < size // 2 or size % 2 else (0 if s == 1 else 1)
                o = -s * (d - 1)
                off = (o, other) if axis == "x" else (other, o)
                add(axis + sign, off[0], off[1], region, half)
    ring("x", xs, 0, 0)
    ring("z", zs, 1, 0)
    for dx in [0, 1, -1, 2][:xs]:
        ring("z", zs, 0, dx)
    order = [0]
    for d in range(1, zs // 2): order += [d, -d]
    order += [zs // 2]
    for dz in order:
        ring("x", xs, 1, dz)
    return sends

def schedule(sends, cost):
    n = len(sends)
    arrive = {}
    free = {w: 0.0 for w in ("x+", "x-", "z+", "z-")}
    todo = set(range(n))
    LAT = 1.5
    chain = [0] * n
    for i in reversed(range(n)):
        chain[i] = max([chain[j] + 1 for j in range(n) if i in sends[j]["deps"]], default=0)
    starts = {}
    while todo:
        best = None
        for i in todo:
            if any(d not in arrive for d in sends[i]["deps"]): continue
            ready = max([arrive[d] for d in sends[i]["deps"]], default=0.0)
            st = max(ready, free[sends[i]["way"]])
            key = (st, -chain[i], ready, i)
            if best is None or key < best[0]: best = (key, i, ready, st)
        key, i, ready, st = best
        todo.remove(i)
        s = sends[i]
        free[s["way"]] = st + cost(s)
        arrive[i] = st + cost(s) + LAT
        starts[i] = (ready, st)
    seq = []
    waited = set(); started = set()
    for i in sorted(range(n), key=lambda i: starts[i][1]):
        for d in sorted(sends[i]["deps"], key=lambda d: arrive[d]):
            if d not in waited:
                waited.add(d); seq.append(("wait", d))
        seq.append(("start", i))
    for d in sorted(range(n), key=lambda d: arrive[d]):
        if d not in waited: seq.append(("wait", d))
    return seq, max(arrive.values())

def gather_kernel(feat_ref, out_ref, send_sem, recv_sem, own_sem, *, xs, zs, cut, seq, sends):
    me = lax.axis_index("nodes")
    x, z = me // zs, me % zs
    cols, rows = feat_ref.shape
    peers = {"x+": ((x + 1) % xs) * zs + z, "x-": ((x + xs - 1) % xs) * zs + z,
             "z+": x * zs + (z + 1) % zs, "z-": x * zs + (z + zs - 1) % zs}
    barrier = pltpu.get_barrier_semaphore()
    for w in peers:
        pl.semaphore_signal(barrier, inc=1, device_id={"nodes": peers[w]}, device_id_type=MESH)
    pl.semaphore_wait(barrier, len(peers))
    own = pltpu.make_async_copy(feat_ref, out_ref.at[me], own_sem)
    own.start()
    def copy(i):
        s = sends[i]
        dx, dz = s["off"]
        src = ((x + dx) % xs) * zs + (z + dz) % zs
        c = pl.ds(0, cut) if s["region"] == 0 else pl.ds(cut, rows - cut)
        h = cols // 2
        r = pl.ds(0, cols) if s["half"] is None else pl.ds(s["half"] * h, h)
        from_ref = feat_ref.at[r, c] if (dx, dz) == (0, 0) else out_ref.at[src, r, c]
        return pltpu.make_async_remote_copy(
            src_ref=from_ref, dst_ref=out_ref.at[src, r, c], send_sem=send_sem.at[i], recv_sem=recv_sem.at[i],
            device_id={"nodes": peers[s["way"]]}, device_id_type=MESH)
    def arrival(i):
        s = sends[i]
        wx, wz = {"x+": (1, 0), "x-": (-1, 0), "z+": (0, 1), "z-": (0, -1)}[s["way"]]
        dx, dz = s["off"]
        src = ((x + dx - wx) % xs) * zs + (z + dz - wz) % zs
        c = pl.ds(0, cut) if s["region"] == 0 else pl.ds(cut, rows - cut)
        h = cols // 2
        r = pl.ds(0, cols) if s["half"] is None else pl.ds(s["half"] * h, h)
        return pltpu.make_async_remote_copy(
            src_ref=out_ref.at[src, r, c], dst_ref=out_ref.at[src, r, c], send_sem=send_sem.at[i], recv_sem=recv_sem.at[i],
            device_id={"nodes": peers[s["way"]]}, device_id_type=MESH)
    for what, i in seq:
        if what == "start": copy(i).start()
        else: arrival(i).wait_recv()
    for i in range(len(sends)): copy(i).wait_send()
    own.wait()

def gather(feat_t, xs=4, zs=8, cut=768, cid=1):
    cols, rows = feat_t.shape
    sends = plan(xs, zs, cut)
    def cost(s):
        n = cols * (cut if s["region"] == 0 else rows - cut) * 2 * 2 / (1 if s["half"] is None else 2)
        return n / 100e3
    seq, end = schedule(sends, cost)
    return pl.pallas_call(
        functools.partial(gather_kernel, xs=xs, zs=zs, cut=cut, seq=seq, sends=sends),
        out_shape=jax.ShapeDtypeStruct((xs * zs, cols, rows), feat_t.dtype),
        in_specs=[pl.BlockSpec(memory_space=pl.ANY)],
        out_specs=pl.BlockSpec(memory_space=pl.ANY),
        scratch_shapes=[pltpu.SemaphoreType.DMA((len(sends),)), pltpu.SemaphoreType.DMA((len(sends),)), pltpu.SemaphoreType.DMA],
        compiler_params=pltpu.CompilerParams(collective_id=cid, has_side_effects=True),
    )(feat_t)

def layer_kernel(feat_ref, agg_ref, self_ref, ws_ref, wn_ref, cot_ref, act_ref, wg_ref,
                 rows_buf, lhs, base, left, gz, xout, xbuf, zout, zbuf,
                 a_send, a_recv, y_send, y_recv, x_send, x_recv, z_send, z_recv, *, xs, zs, ys):
    me = lax.axis_index("nodes")
    f = lax.axis_index("feat")
    x, z = me // zs, me % zs
    y, core = f // 2, f % 2
    feats = 2 * ys
    cols = feat_ref.shape[0]
    own = cot_ref.shape[0]
    hidden = ws_ref.shape[1]
    chunks = hidden // 256
    half = hidden // 2

    def remote(src, dst, send, recv, **where):
        return pltpu.make_async_remote_copy(src_ref=src, dst_ref=dst, send_sem=send, recv_sem=recv,
                                            device_id=where, device_id_type=MESH)

    barrier = pltpu.get_barrier_semaphore()
    for d in range(1, feats):
        pl.semaphore_signal(barrier, inc=1, device_id={"feat": (f + d) % feats}, device_id_type=MESH)
    for d in range(1, xs):
        pl.semaphore_signal(barrier, inc=1, device_id={"nodes": ((x + d) % xs) * zs + z}, device_id_type=MESH)
    for d in range(1, zs):
        pl.semaphore_signal(barrier, inc=1, device_id={"nodes": x * zs + (z + d) % zs}, device_id_type=MESH)
    pl.semaphore_wait(barrier, feats + xs + zs - 3)

    def to_owner(d):
        j = (f + d) % feats
        return remote(agg_ref.at[:, pl.ds(pl.multiple_of(j * own, own), own)], rows_buf.at[f],
                      a_send.at[d], a_recv.at[d], feat=j)
    for d in range(1, feats):
        to_owner(d).start()
    rows_buf[f] = agg_ref[:, pl.ds(pl.multiple_of(f * own, own), own)]
    left[0:cols, :] = feat_ref[...]
    left[cols:, :] = agg_ref[...]
    lhs[...] = self_ref[...].reshape(feats * cols, own).T
    base[...] = jnp.dot(lhs[...], ws_ref[...], preferred_element_type=jnp.float32)
    for d in range(1, feats):
        to_owner(d).wait()
    lhs[...] = rows_buf[...].reshape(feats * cols, own).T

    up, down = (y + 1) % ys, (y + ys - 1) % ys
    far = (y + 2) % ys
    sibling = 2 * y + 1 - core
    hrows = own // 2
    def spread(c, k):
        by = (y, y, y, down, up, down, up, far, far)[k]
        to = (sibling, 2 * up + core, 2 * down + core, 2 * up + core, 2 * down + core) + (sibling,) * 4
        r = {3: pl.ds(0, hrows), 4: pl.ds(hrows, hrows), 7: pl.ds(0, hrows), 8: pl.ds(hrows, hrows)}.get(k, pl.ds(0, own))
        ref = gz.at[c, 2 * by + core, r]
        return remote(ref, ref, y_send.at[c, k], y_recv.at[c, k], feat=to[k])

    def columns(ref, c):
        return jnp.concatenate([ref[:, pl.ds(pl.multiple_of(c * 128, 128), 128)],
                                ref[:, pl.ds(pl.multiple_of(half + c * 128, 128), 128)]], axis=1)

    def layer(c, carry):
        v = columns(base, c) + jnp.dot(lhs[...], columns(wn_ref, c), preferred_element_type=jnp.float32)
        s = math.sqrt(2 / math.pi)
        v2 = v * v
        t = jnp.tanh(s * (v + 0.044715 * (v2 * v)))
        cdf = 0.5 * (1.0 + t)
        out = (v * cdf).astype(jnp.bfloat16)
        act_ref[:, pl.ds(pl.multiple_of(c * 128, 128), 128)] = out[:, :128]
        act_ref[:, pl.ds(pl.multiple_of(half + c * 128, 128), 128)] = out[:, 128:]
        slope = cdf + (0.5 * s) * v * (1.0 - t * t) * (1.0 + (3 * 0.044715) * v2)
        gz[c, f] = (columns(cot_ref, c).astype(jnp.float32) * slope).astype(jnp.bfloat16)
        for k in (1, 2, 0):
            spread(c, k).start()
        return carry
    lax.fori_loop(0, chunks, layer, 0)

    def xcopy(c, d):
        to = (x + d) % xs
        return remote(xout.at[c, to], xbuf.at[c, d], x_send.at[c, d], x_recv.at[c, d], nodes=to * zs + z)
    def zcopy(c, p, zto):
        return remote(zout.at[c, p], zbuf.at[z], z_send.at[c, p], z_recv.at[z], nodes=x * zs + zto)

    def relay(c, carry):
        spread(c, 1).wait_recv()
        spread(c, 3).start()
        spread(c, 5).start()
        spread(c, 2).wait_recv()
        spread(c, 4).start()
        spread(c, 6).start()
        return carry
    def terms(c, carry):
        for k in (3, 4):
            spread(c, k).wait_recv()
            spread(c, k + 4).start()
        for k in (0, 5, 6, 7, 8):
            spread(c, k).wait_recv()
        g = gz[c].reshape(feats * own, 256)
        term = jnp.dot(left[...], g, preferred_element_type=jnp.float32)
        for q in range(4):
            piece = term[(q // 2) * cols:(q // 2 + 1) * cols, (q % 2) * 128:(q % 2) * 128 + 128]
            xout[c, q] = piece
        for d in range(1, xs):
            xcopy(c, d).start()
        return carry
    def sums(c, carry):
        for d in range(1, xs):
            xcopy(c, d).wait_recv()
        total = xout[c, x] + xbuf[c, 1] + xbuf[c, 2] + xbuf[c, 3]
        total = jnp.concatenate([total, jnp.zeros((128 - cols, 128), jnp.float32)], axis=0).T
        for p in range(2):
            zto = 2 * c + p
            zout[c, p] = total[64 * p:64 * p + 64]
            @pl.when(zto != z)
            def _():
                zcopy(c, p, zto).start()
            @pl.when(zto == z)
            def _():
                zbuf[z] = total[64 * p:64 * p + 64]
        return carry
    def both(c, carry):
        relay(c, carry)
        @pl.when(c > 0)
        def _():
            terms(c - 1, carry)
        @pl.when(c > 1)
        def _():
            sums(c - 2, carry)
        return carry
    lax.fori_loop(0, chunks, both, 0)
    terms(chunks - 1, 0)
    sums(chunks - 2, 0)
    sums(chunks - 1, 0)
    def arrived(i, carry):
        @pl.when(i != z)
        def _():
            remote(zout.at[0, 0], zbuf.at[i], z_send.at[0, 0], z_recv.at[i], nodes=x * zs + i).wait_recv()
        return carry
    lax.fori_loop(0, zs, arrived, 0)
    wg_ref[...] = jnp.sum(zbuf[...], axis=0)[:, :cols]

    def finish(c, carry):
        for k in range(9):
            spread(c, k).wait_send()
        for d in range(1, xs):
            xcopy(c, d).wait_send()
        for p in range(2):
            @pl.when(2 * c + p != z)
            def _():
                zcopy(c, p, 2 * c + p).wait_send()
        return carry
    lax.fori_loop(0, chunks, finish, 0)

def layer(feat_t, agg_t, self_rows, w_self, w_neigh, cot, xs=4, zs=8, ys=4, cid=2):
    cols, rows = feat_t.shape
    own, hidden = cot.shape
    feats, chunks = 2 * ys, hidden // 256
    v = pl.BlockSpec(memory_space=pltpu.VMEM)
    dma = pltpu.SemaphoreType.DMA
    f32, bf16 = jnp.float32, jnp.bfloat16
    return pl.pallas_call(
        functools.partial(layer_kernel, xs=xs, zs=zs, ys=ys),
        out_shape=(jax.ShapeDtypeStruct((own, hidden), bf16), jax.ShapeDtypeStruct((hidden // (xs * zs) * 2, cols), f32)),
        in_specs=[v] * 6,
        out_specs=(v, v),
        scratch_shapes=[
            pltpu.VMEM((feats, cols, own), bf16), pltpu.VMEM((own, feats * cols), bf16), pltpu.VMEM((own, hidden), f32),
            pltpu.VMEM((2 * cols, rows), bf16), pltpu.VMEM((chunks, feats, own, 256), bf16),
            pltpu.VMEM((chunks, 4, cols, 128), f32), pltpu.VMEM((chunks, xs, cols, 128), f32),
            pltpu.VMEM((chunks, 2, 64, 128), f32), pltpu.VMEM((zs, 64, 128), f32),
            dma((feats,)), dma((feats,)), dma((chunks, 9)), dma((chunks, 9)),
            dma((chunks, xs)), dma((chunks, xs)), dma((chunks, 2)), dma((zs,)),
        ],
        compiler_params=pltpu.CompilerParams(collective_id=cid, has_side_effects=True, vmem_limit_bytes=48 * 2**20),
    )(feat_t, agg_t, self_rows, w_self, w_neigh, cot)


def agg_kernel(src_ref, cnt_ref, rows_ref, g_ref, out_ref, picks_ref):
    tiles, slots, span = rows_ref.shape
    cols = g_ref.shape[1]
    per_block = g_ref.shape[2] // span
    iota = lax.broadcasted_iota(jnp.int32, (span, span), 0).astype(jnp.float32).astype(jnp.bfloat16)
    one = jnp.ones((span, span), jnp.bfloat16)
    zero = jnp.zeros((span, span), jnp.bfloat16)
    slot_ids = lax.broadcasted_iota(jnp.int32, (slots, span), 0)

    def tile(t, carry):
        used = cnt_ref[t]
        picks_ref[...] = jnp.where(slot_ids < used, rows_ref[t], -1).astype(jnp.float32)

        def step(i, acc):
            onehots, blocks = [], []
            for u in range(UNROLL):
                k = i * UNROLL + u
                pick = jnp.broadcast_to(picks_ref[pl.ds(k, 1), :], (16, span)).astype(jnp.bfloat16)
                pick = jnp.concatenate([pick] * (span // 16), axis=0)
                onehots.append(jnp.where(pick == iota, one, zero))
                s = src_ref[t, k]
                start = pl.multiple_of((s % per_block) * span, span)
                blocks.append(g_ref[s // per_block, :, pl.ds(start, span)])
            return acc + jnp.dot(
                jnp.concatenate(blocks, axis=1),
                jnp.concatenate(onehots, axis=0),
                preferred_element_type=jnp.float32,
            )

        total = lax.fori_loop(0, (used + UNROLL - 1) // UNROLL, step, jnp.zeros((cols, span), jnp.float32))
        mean = total / used.astype(jnp.float32)
        out_ref[:, pl.ds(pl.multiple_of(t * span, span), span)] = mean.astype(jnp.bfloat16)
        return carry

    lax.fori_loop(0, tiles, tile, 0)


def neighbour_mean(src_tiles, counts, edge_rows, gathered):
    tiles, slots, span = edge_rows.shape
    cols = gathered.shape[1]
    return pl.pallas_call(
        agg_kernel,
        out_shape=jax.ShapeDtypeStruct((cols, tiles * span), jnp.bfloat16),
        in_specs=[pl.BlockSpec(memory_space=pltpu.SMEM)] * 2 + [pl.BlockSpec(memory_space=pltpu.VMEM)] * 2,
        out_specs=pl.BlockSpec(memory_space=pltpu.VMEM),
        scratch_shapes=[pltpu.VMEM((slots, span), jnp.float32)],
        compiler_params=pltpu.CompilerParams(vmem_limit_bytes=40 * 2**20),
    )(src_tiles, counts, edge_rows, gathered)


def per_device(features, w_self, w_neigh, src_tiles, counts, edge_rows, cotangent):
    feat_t = features.T
    cols, rows = feat_t.shape
    own = cotangent.shape[0]
    self_rows = lax.all_to_all(feat_t.reshape(cols, -1, own), "feat", split_axis=1, concat_axis=0, tiled=True)
    self_rows = self_rows.reshape(-1, cols, own)
    gathered = gather(feat_t)
    agg_t = neighbour_mean(src_tiles, counts, edge_rows, gathered)
    activations, grads_t = layer(feat_t, agg_t, self_rows, w_self, w_neigh, cotangent)
    return activations, grads_t.T


def solution(mesh):
    in_specs = (
        P("nodes", "feat"),
        P(),
        P(),
        P("nodes", None),
        P("nodes"),
        P("nodes", None, None),
        P(("nodes", "feat"), None),
    )
    out_specs = (P(("nodes", "feat"), None), P("feat", "nodes"))
    return jax.shard_map(
        per_device, mesh=mesh, in_specs=in_specs, out_specs=out_specs, check_vma=False
    )
```

```python
import functools
import math

import jax
import jax.numpy as jnp
from jax import lax
from jax.experimental import pallas as pl
from jax.experimental.pallas import tpu as pltpu
from jax.sharding import PartitionSpec as P

UNROLL = 8
MESH = pl.DeviceIdType.MESH
WAYS = {"x+": (1, 0), "x-": (-1, 0), "z+": (0, 1), "z-": (0, -1)}

def plan_gather(zs, seconds):
    sends, have = [], {}

    def add(way, block, region, half, passing, get):
        deps = [] if passing is None else [passing]
        if passing is None:
            for h in (0, 1) if half is None else (half,):
                deps += have.get((block, region, h), [])
        sends.append(dict(way=way, block=block, region=region, half=half, relayed=passing is not None,
                          lands=get, deps=sorted(set(deps))))
        if get is not None and get != "sibling":
            for h in (0, 1) if half is None else (half,):
                have[(get, region, h)] = [len(sends) - 1]
        return len(sends) - 1

    def along_z(other, region):
        for d in range(1, zs // 2 + 1):
            for way, s in (("z+", 1), ("z-", -1)):
                half = None if d < zs // 2 else (0 if s == 1 else 1)
                add(way, (other, -s * (d - 1) % zs), region, half, None, (other, -s * d % zs))

    def along_x(dz, region):
        for way, half in (("x+", 0), ("x-", 1)):
            first = add(way, (0, dz), region, half, None, None)
            add(way, (0, dz), region, half, first, (1, dz))

    order = [0]
    for d in range(1, zs // 2):
        order += [d, zs - d]
    order += [zs // 2]
    along_x(0, 0)
    along_z(0, 1)
    along_z(0, 0)
    along_z(1, 0)
    for dz in order:
        along_x(dz, 1)
    for other in (0, 1):
        for dz in order:
            for region in (0, 1):
                add("core", (other, dz), region, None, None, "sibling")

    n = len(sends)
    chain = [0] * n
    for i in reversed(range(n)):
        for d in sends[i]["deps"]:
            chain[d] = max(chain[d], chain[i] + 1)
    free, arrive, starts, todo = {}, {}, {}, set(range(n))
    while todo:
        best = None
        for i in todo:
            if all(d in arrive for d in sends[i]["deps"]):
                ready = max([arrive[d] for d in sends[i]["deps"]], default=0.0)
                at = max(ready, free.get(sends[i]["way"], 0.0))
                key = (at, -chain[i], ready, i)
                best = key if best is None else min(best, key)
        at, _, _, i = best
        todo.remove(i)
        starts[i] = at
        free[sends[i]["way"]] = at + seconds(sends[i])
        arrive[i] = at + seconds(sends[i]) + 1.5
    steps, waited = [], set()
    for i in sorted(range(n), key=lambda i: (starts[i], i)):
        for d in sorted(sends[i]["deps"], key=lambda d: arrive[d]):
            if d not in waited:
                waited.add(d)
                steps.append(("wait", d))
        steps.append(("start", i))
    steps += [("wait", d) for d in sorted(range(n), key=lambda d: arrive[d]) if d not in waited]
    return sends, steps, max(arrive.values())

def gather_kernel(feat_ref, edge_ref, table_ref, out_ref, relay_ref, self_ref, edge_out, table_out,
                  send_sem, recv_sem, row_send, row_recv, swap_send, swap_recv, own_sem, *, xs, zs, cut, sends, steps):
    me = lax.axis_index("nodes")
    f = lax.axis_index("feat")
    feats = lax.axis_size("feat")
    x, z = me // zs, me % zs
    core, parity = f % 2, x % 2
    cols, rows = feat_ref.shape
    own = rows // feats
    sibling = f + 1 - 2 * core
    across = (x + 1 - 2 * parity) * zs + z
    base = (x - parity + core)
    home = base * zs + z
    peers = {w: ((x + dx) % xs) * zs + (z + dz) % zs for w, (dx, dz) in WAYS.items()}

    barrier = pltpu.get_barrier_semaphore()
    for w in peers:
        pl.semaphore_signal(barrier, inc=1, device_id={"nodes": peers[w]}, device_id_type=MESH)
    for d in range(1, feats):
        pl.semaphore_signal(barrier, inc=1, device_id={"feat": (f + d) % feats}, device_id_type=MESH)
    pl.semaphore_signal(barrier, inc=1, device_id={"nodes": across, "feat": sibling}, device_id_type=MESH)
    pl.semaphore_wait(barrier, len(peers) + feats)

    left, right = pl.ds(0, cut), pl.ds(cut, rows - cut)
    moves = ((feat_ref.at[:, left], out_ref.at[home, :, left]), (feat_ref.at[:, right], out_ref.at[home, :, right]),
             (table_ref, table_out), (edge_ref, edge_out))
    theirs = (x + 1 - 2 * parity) - (1 - parity) + (1 - core)
    theirs = theirs * zs + z
    there = (out_ref.at[theirs, :, left], out_ref.at[theirs, :, right], table_out, edge_out)

    def swap(i):
        return pltpu.make_async_remote_copy(
            src_ref=moves[i][0], dst_ref=there[i], send_sem=swap_send.at[i], recv_sem=swap_recv.at[i],
            device_id={"nodes": across, "feat": sibling}, device_id_type=MESH)
    def keep(i):
        return pltpu.make_async_copy(moves[i][0], moves[i][1], own_sem.at[i])

    def to_owner(d):
        j = (f + d) % feats
        return pltpu.make_async_remote_copy(
            src_ref=feat_ref.at[:, pl.ds(pl.multiple_of(j * own, own), own)], dst_ref=self_ref.at[f],
            send_sem=row_send.at[d], recv_sem=row_recv.at[d], device_id={"feat": j}, device_id_type=MESH)

    @pl.when(parity != core)
    def _():
        for i in range(4):
            swap(i).start()
    @pl.when(parity == core)
    def _():
        for i in range(4):
            keep(i).start()
    mine = pltpu.make_async_copy(feat_ref.at[:, pl.ds(pl.multiple_of(f * own, own), own)], self_ref.at[f], own_sem.at[4])
    mine.start()
    for d in range(1, feats):
        to_owner(d).start()
    @pl.when(parity != core)
    def _():
        for i in range(2):
            swap(i).wait_recv()
    @pl.when(parity == core)
    def _():
        for i in range(2):
            keep(i).wait()

    def refs(s, block, relay, b):
        other, dz = block
        c = left if s["region"] == 0 else right
        r = pl.ds(0, cols) if s["half"] is None else pl.ds(s["half"] * (cols // 2), cols // 2)
        if relay:
            return relay_ref.at[dz, r, c]
        return out_ref.at[((b + 2 * other) % xs) * zs + (z + dz) % zs, r, c]

    def copy(i):
        s = sends[i]
        src = refs(s, s["block"], s["relayed"], base)
        wx, wz = WAYS.get(s["way"], (0, 0))
        if s["lands"] == "sibling":
            dst = src
            where = {"feat": sibling}
        else:
            where = {"nodes": peers[s["way"]]}
            if s["lands"] is None:
                dst = refs(s, s["block"], True, base)
            elif s["relayed"]:
                b = (x + wx) % xs
                b = b - b % 2 + core
                dst = relay_dst(s, b)
            else:
                dst = src
        return pltpu.make_async_remote_copy(src_ref=src, dst_ref=dst, send_sem=send_sem.at[i], recv_sem=recv_sem.at[i],
                                            device_id=where, device_id_type=MESH)

    def relay_dst(s, b):
        return refs(s, (1, s["block"][1]), False, b)

    def arrival(i):
        s = sends[i]
        if s["lands"] == "sibling":
            b = x - parity + 1 - core
            dst = refs(s, s["block"], False, b)
            where = {"feat": sibling}
        else:
            where = {"nodes": peers[s["way"]]}
            dst = refs(s, s["block"], True, base) if s["lands"] is None else refs(s, s["lands"], False, base)
        return pltpu.make_async_remote_copy(src_ref=dst, dst_ref=dst, send_sem=send_sem.at[i], recv_sem=recv_sem.at[i],
                                            device_id=where, device_id_type=MESH)

    for what, i in steps:
        if what == "start":
            copy(i).start()
        else:
            arrival(i).wait_recv()
    for i in range(len(sends)):
        copy(i).wait_send()
    for d in range(1, feats):
        to_owner(d).wait()
    mine.wait()
    @pl.when(parity != core)
    def _():
        for i in range(2):
            swap(i).wait_send()
        for i in (2, 3):
            swap(i).wait()
    @pl.when(parity == core)
    def _():
        for i in (2, 3):
            keep(i).wait()

def gather(feat_t, edge_rows, tables, xs=4, zs=8, feats=8, cut=896, cid=1):
    cols, rows = feat_t.shape
    def seconds(s):
        n = cols * (cut if s["region"] == 0 else rows - cut) * 2 / (1 if s["half"] is None else 2)
        return n / 300e3 if s["way"] == "core" else 2 * n / 90e3
    sends, steps, end = plan_gather(zs, seconds)
    anywhere = pl.BlockSpec(memory_space=pl.ANY)
    dma = pltpu.SemaphoreType.DMA
    return pl.pallas_call(
        functools.partial(gather_kernel, xs=xs, zs=zs, cut=cut, sends=sends, steps=steps),
        out_shape=(jax.ShapeDtypeStruct((xs * zs, cols, rows), feat_t.dtype),
                   jax.ShapeDtypeStruct((zs, cols, rows), feat_t.dtype),
                   jax.ShapeDtypeStruct((feats, cols, rows // feats), feat_t.dtype),
                   jax.ShapeDtypeStruct(edge_rows.shape, edge_rows.dtype),
                   jax.ShapeDtypeStruct(tables.shape, tables.dtype)),
        in_specs=[anywhere] * 3,
        out_specs=(anywhere,) * 5,
        scratch_shapes=[dma((len(sends),)), dma((len(sends),)), dma((feats,)), dma((feats,)), dma((4,)), dma((4,)), dma((5,))],
        compiler_params=pltpu.CompilerParams(collective_id=cid, has_side_effects=True),
    )(feat_t, edge_rows, tables)

def layer_kernel(feat_ref, agg_ref, self_ref, ws_ref, wn_ref, cot_ref, act_ref, wg_ref,
                 rows_buf, lhs, base, left, gz, xout, xbuf, zout, zbuf,
                 a_send, a_recv, y_send, y_recv, x_send, x_recv, z_send, z_recv, s_send, s_recv, *, xs, zs, ys):
    me = lax.axis_index("nodes")
    f = lax.axis_index("feat")
    x, z = me // zs, me % zs
    y, core = f // 2, f % 2
    feats = 2 * ys
    cols = feat_ref.shape[0]
    own = cot_ref.shape[0]
    hidden = ws_ref.shape[1]
    chunks = hidden // 256
    half = hidden // 2

    def remote(src, dst, send, recv, **where):
        return pltpu.make_async_remote_copy(src_ref=src, dst_ref=dst, send_sem=send, recv_sem=recv,
                                            device_id=where, device_id_type=MESH)

    parity = x % 2
    pair = x - parity
    across = (pair + 1 - parity) * zs + z
    shard = 2 * y + parity

    barrier = pltpu.get_barrier_semaphore()
    for d in range(feats):
        j = (f + d) % feats
        if d:
            pl.semaphore_signal(barrier, inc=1, device_id={"feat": j}, device_id_type=MESH)
        pl.semaphore_signal(barrier, inc=1, device_id={"nodes": across, "feat": j}, device_id_type=MESH)
    for other in (x + 2, x + xs - 1 + 2 * parity):
        pl.semaphore_signal(barrier, inc=1, device_id={"nodes": (other % xs) * zs + z}, device_id_type=MESH)
    for d in range(1, zs):
        pl.semaphore_signal(barrier, inc=1, device_id={"nodes": x * zs + (z + d) % zs}, device_id_type=MESH)
    pl.semaphore_wait(barrier, 2 * feats - 1 + 2 + zs - 1)

    def to_owner(d):
        j = (f + d) % feats
        return remote(agg_ref.at[:, pl.ds(pl.multiple_of(j * own, own), own)], rows_buf.at[shard],
                      a_send.at[d], a_recv.at[shard], nodes=(pair + core) * zs + z, feat=j)
    def from_shard(i):
        return remote(rows_buf.at[i], rows_buf.at[i], a_send.at[0], a_recv.at[i],
                      nodes=(pair + i % 2) * zs + z, feat=i - i % 2 + parity)
    def swap():
        return remote(agg_ref, left.at[pl.ds(cols, cols)], s_send, s_recv, nodes=across, feat=f + 1 - 2 * core)
    for d in range(1, feats):
        to_owner(d).start()
    @pl.when(parity != core)
    def _():
        to_owner(0).start()
        swap().start()
    @pl.when(parity == core)
    def _():
        rows_buf[f] = agg_ref[:, pl.ds(pl.multiple_of(f * own, own), own)]
        left[cols:, :] = agg_ref[...]
    left[0:cols, :] = feat_ref[...]
    lhs[...] = self_ref[...].reshape(feats * cols, own).T
    base[...] = jnp.dot(lhs[...], ws_ref[...], preferred_element_type=jnp.float32)
    for d in range(feats):
        i = (f + d) % feats
        if d:
            from_shard(i).wait_recv()
        else:
            @pl.when(parity != core)
            def _():
                from_shard(i).wait_recv()
    lhs[...] = rows_buf[...].reshape(feats * cols, own).T

    up, down = (y + 1) % ys, (y + ys - 1) % ys
    far = (y + 2) % ys
    sibling = 2 * y + 1 - core
    hrows = own // 2
    def spread(c, k):
        by = (y, y, y, down, up, down, up, far, far)[k]
        to = (sibling, 2 * up + core, 2 * down + core, 2 * up + core, 2 * down + core) + (sibling,) * 4
        r = {3: pl.ds(0, hrows), 4: pl.ds(hrows, hrows), 7: pl.ds(0, hrows), 8: pl.ds(hrows, hrows)}.get(k, pl.ds(0, own))
        ref = gz.at[c, 2 * by + core, r]
        return remote(ref, ref, y_send.at[c, k], y_recv.at[c, k], feat=to[k])

    def columns(ref, c):
        return jnp.concatenate([ref[:, pl.ds(pl.multiple_of(c * 128, 128), 128)],
                                ref[:, pl.ds(pl.multiple_of(half + c * 128, 128), 128)]], axis=1)

    def layer(c, carry):
        v = columns(base, c) + jnp.dot(lhs[...], columns(wn_ref, c), preferred_element_type=jnp.float32)
        s = math.sqrt(2 / math.pi)
        v2 = v * v
        t = jnp.tanh(s * (v + 0.044715 * (v2 * v)))
        cdf = 0.5 * (1.0 + t)
        out = (v * cdf).astype(jnp.bfloat16)
        act_ref[:, pl.ds(pl.multiple_of(c * 128, 128), 128)] = out[:, :128]
        act_ref[:, pl.ds(pl.multiple_of(half + c * 128, 128), 128)] = out[:, 128:]
        slope = cdf + (0.5 * s) * v * (1.0 - t * t) * (1.0 + (3 * 0.044715) * v2)
        gz[c, f] = (columns(cot_ref, c).astype(jnp.float32) * slope).astype(jnp.bfloat16)
        for k in (1, 2, 0):
            spread(c, k).start()
        return carry
    lax.fori_loop(0, chunks, layer, 0)

    def xcopy(c, d):
        to = (x + d) % xs
        return remote(xout.at[c, to], xbuf.at[c, d], x_send.at[c, d], x_recv.at[c, d], nodes=to * zs + z)
    def zcopy(c, p, zto):
        return remote(zout.at[c, p], zbuf.at[z], z_send.at[c, p], z_recv.at[z], nodes=x * zs + zto)

    def relay(c, carry):
        spread(c, 1).wait_recv()
        spread(c, 3).start()
        spread(c, 5).start()
        spread(c, 2).wait_recv()
        spread(c, 4).start()
        spread(c, 6).start()
        return carry
    def terms(c, carry):
        for k in (3, 4):
            spread(c, k).wait_recv()
            spread(c, k + 4).start()
        for k in (0, 5, 6, 7, 8):
            spread(c, k).wait_recv()
        g = gz[c].reshape(feats * own, 256)
        term = jnp.dot(left[...], g, preferred_element_type=jnp.float32)
        for q in range(4):
            piece = term[(q // 2) * cols:(q // 2 + 1) * cols, (q % 2) * 128:(q % 2) * 128 + 128]
            xout[c, q] = piece
        for d in range(1, xs):
            xcopy(c, d).start()
        return carry
    def sums(c, carry):
        for d in range(1, xs):
            xcopy(c, d).wait_recv()
        total = xout[c, x] + xbuf[c, 1] + xbuf[c, 2] + xbuf[c, 3]
        total = jnp.concatenate([total, jnp.zeros((128 - cols, 128), jnp.float32)], axis=0).T
        for p in range(2):
            zto = 2 * c + p
            zout[c, p] = total[64 * p:64 * p + 64]
            @pl.when(zto != z)
            def _():
                zcopy(c, p, zto).start()
            @pl.when(zto == z)
            def _():
                zbuf[z] = total[64 * p:64 * p + 64]
        return carry
    def both(c, carry):
        relay(c, carry)
        @pl.when(c > 0)
        def _():
            terms(c - 1, carry)
        @pl.when(c > 1)
        def _():
            sums(c - 2, carry)
        return carry
    @pl.when(parity != core)
    def _():
        swap().wait_recv()
    lax.fori_loop(0, chunks, both, 0)
    terms(chunks - 1, 0)
    sums(chunks - 2, 0)
    sums(chunks - 1, 0)
    def arrived(i, carry):
        @pl.when(i != z)
        def _():
            remote(zout.at[0, 0], zbuf.at[i], z_send.at[0, 0], z_recv.at[i], nodes=x * zs + i).wait_recv()
        return carry
    lax.fori_loop(0, zs, arrived, 0)
    wg_ref[...] = jnp.sum(zbuf[...], axis=0)[:, :cols]

    def finish(c, carry):
        for k in range(9):
            spread(c, k).wait_send()
        for d in range(1, xs):
            xcopy(c, d).wait_send()
        for p in range(2):
            @pl.when(2 * c + p != z)
            def _():
                zcopy(c, p, 2 * c + p).wait_send()
        return carry
    lax.fori_loop(0, chunks, finish, 0)
    for d in range(1, feats):
        to_owner(d).wait_send()
    @pl.when(parity != core)
    def _():
        to_owner(0).wait_send()
        swap().wait_send()

def layer(feat_t, agg_t, self_rows, w_self, w_neigh, cot, xs=4, zs=8, ys=4, cid=2):
    cols, rows = feat_t.shape
    own, hidden = cot.shape
    feats, chunks = 2 * ys, hidden // 256
    v = pl.BlockSpec(memory_space=pltpu.VMEM)
    dma = pltpu.SemaphoreType.DMA
    f32, bf16 = jnp.float32, jnp.bfloat16
    return pl.pallas_call(
        functools.partial(layer_kernel, xs=xs, zs=zs, ys=ys),
        out_shape=(jax.ShapeDtypeStruct((own, hidden), bf16), jax.ShapeDtypeStruct((hidden // (xs * zs) * 2, cols), f32)),
        in_specs=[v] * 6,
        out_specs=(v, v),
        scratch_shapes=[
            pltpu.VMEM((feats, cols, own), bf16), pltpu.VMEM((own, feats * cols), bf16), pltpu.VMEM((own, hidden), f32),
            pltpu.VMEM((2 * cols, rows), bf16), pltpu.VMEM((chunks, feats, own, 256), bf16),
            pltpu.VMEM((chunks, 4, cols, 128), f32), pltpu.VMEM((chunks, xs, cols, 128), f32),
            pltpu.VMEM((chunks, 2, 64, 128), f32), pltpu.VMEM((zs, 64, 128), f32),
            dma((feats,)), dma((feats,)), dma((chunks, 9)), dma((chunks, 9)),
            dma((chunks, xs)), dma((chunks, xs)), dma((chunks, 2)), dma((zs,)), dma, dma,
        ],
        compiler_params=pltpu.CompilerParams(collective_id=cid, has_side_effects=True, vmem_limit_bytes=48 * 2**20),
    )(feat_t, agg_t, self_rows, w_self, w_neigh, cot)


def agg_kernel(table_ref, rows_ref, g_ref, out_ref, picks_ref):
    tiles, slots, span = rows_ref.shape
    cols = g_ref.shape[1]
    per_block = g_ref.shape[2] // span
    iota = lax.broadcasted_iota(jnp.int32, (span, span), 0).astype(jnp.float32).astype(jnp.bfloat16)
    one = jnp.ones((span, span), jnp.bfloat16)
    zero = jnp.zeros((span, span), jnp.bfloat16)
    slot_ids = lax.broadcasted_iota(jnp.int32, (slots, span), 0)

    def tile(t, carry):
        used = table_ref[t, slots]
        picks_ref[...] = jnp.where(slot_ids < used, rows_ref[t], -1).astype(jnp.float32)

        def step(i, acc):
            onehots, blocks = [], []
            for u in range(UNROLL):
                k = i * UNROLL + u
                pick = jnp.broadcast_to(picks_ref[pl.ds(k, 1), :], (16, span)).astype(jnp.bfloat16)
                pick = jnp.concatenate([pick] * (span // 16), axis=0)
                onehots.append(jnp.where(pick == iota, one, zero))
                s = table_ref[t, k]
                start = pl.multiple_of((s % per_block) * span, span)
                blocks.append(g_ref[s // per_block, :, pl.ds(start, span)])
            return acc + jnp.dot(
                jnp.concatenate(blocks, axis=1),
                jnp.concatenate(onehots, axis=0),
                preferred_element_type=jnp.float32,
            )

        total = lax.fori_loop(0, (used + UNROLL - 1) // UNROLL, step, jnp.zeros((cols, span), jnp.float32))
        mean = total / used.astype(jnp.float32)
        out_ref[:, pl.ds(pl.multiple_of(t * span, span), span)] = mean.astype(jnp.bfloat16)
        return carry

    lax.fori_loop(0, tiles, tile, 0)


def neighbour_mean(tables, edge_rows, gathered):
    tiles, slots, span = edge_rows.shape
    cols = gathered.shape[1]
    return pl.pallas_call(
        agg_kernel,
        out_shape=jax.ShapeDtypeStruct((cols, tiles * span), jnp.bfloat16),
        in_specs=[pl.BlockSpec(memory_space=pltpu.SMEM)] + [pl.BlockSpec(memory_space=pltpu.VMEM)] * 2,
        out_specs=pl.BlockSpec(memory_space=pltpu.VMEM),
        scratch_shapes=[pltpu.VMEM((slots, span), jnp.float32)],
        compiler_params=pltpu.CompilerParams(vmem_limit_bytes=40 * 2**20),
    )(tables, edge_rows, gathered)


def per_device(features, w_self, w_neigh, src_tiles, counts, edge_rows, cotangent):
    feat_t = features.T
    tables = jnp.concatenate([src_tiles, jnp.broadcast_to(counts[:, None], src_tiles.shape)], axis=1)
    gathered, _, self_rows, edge_rows, tables = gather(feat_t, edge_rows, tables)
    agg_t = neighbour_mean(tables, edge_rows, gathered)
    activations, grads_t = layer(feat_t, agg_t, self_rows, w_self, w_neigh, cotangent)
    return activations, grads_t.T


def solution(mesh):
    in_specs = (
        P("nodes", "feat"),
        P(),
        P(),
        P("nodes", None),
        P("nodes"),
        P("nodes", None, None),
        P(("nodes", "feat"), None),
    )
    out_specs = (P(("nodes", "feat"), None), P("feat", "nodes"))
    return jax.shard_map(
        per_device, mesh=mesh, in_specs=in_specs, out_specs=out_specs, check_vma=False
    )
```

```python
import functools
import math

import jax
import jax.numpy as jnp
from jax import lax
from jax.experimental import pallas as pl
from jax.experimental.pallas import tpu as pltpu
from jax.sharding import PartitionSpec as P

UNROLL = 8
MESH = pl.DeviceIdType.MESH
WAYS = {"x+": (1, 0), "x-": (-1, 0), "z+": (0, 1), "z-": (0, -1)}

def plan_gather(zs, seconds, ahead=4.0):
    sends, have = [], {}

    def add(way, block, region, half, passing, get):
        deps = [] if passing is None else [passing]
        if passing is None:
            for h in (0, 1) if half is None else (half,):
                deps += have.get((block, region, h), [])
        sends.append(dict(way=way, block=block, region=region, half=half, relayed=passing is not None,
                          lands=get, deps=sorted(set(deps))))
        if get is not None and get != "sibling":
            for h in (0, 1) if half is None else (half,):
                have[(get, region, h)] = [len(sends) - 1]
        return len(sends) - 1

    def along_z(other, region):
        for d in range(1, zs // 2 + 1):
            for way, s in (("z+", 1), ("z-", -1)):
                half = None if d < zs // 2 else (0 if s == 1 else 1)
                add(way, (other, -s * (d - 1) % zs), region, half, None, (other, -s * d % zs))

    def along_x(dz, region):
        for way, half in (("x+", 0), ("x-", 1)):
            first = add(way, (0, dz), region, half, None, None)
            add(way, (0, dz), region, half, first, (1, dz))

    order = [0]
    for d in range(1, zs // 2):
        order += [d, zs - d]
    order += [zs // 2]
    along_x(0, 0)
    along_z(0, 1)
    along_z(0, 0)
    along_z(1, 0)
    for dz in order:
        along_x(dz, 1)
    for other in (0, 1):
        for dz in order:
            for region in (0, 1):
                add("core", (other, dz), region, None, None, "sibling")

    n = len(sends)
    chain = [0] * n
    for i in reversed(range(n)):
        for d in sends[i]["deps"]:
            chain[d] = max(chain[d], chain[i] + 1)
    free, arrive, starts, todo = {}, {}, {}, set(range(n))
    while todo:
        best = None
        for i in todo:
            if all(d in arrive for d in sends[i]["deps"]):
                ready = max([arrive[d] for d in sends[i]["deps"]], default=0.0)
                at = max(ready, free.get(sends[i]["way"], 0.0))
                key = (at, -chain[i], ready, i)
                best = key if best is None else min(best, key)
        at, _, _, i = best
        todo.remove(i)
        starts[i] = at
        free[sends[i]["way"]] = at + seconds(sends[i])
        arrive[i] = at + seconds(sends[i]) + 1.5
    steps, waited = [], set()
    when = {i: max([arrive[d] for d in sends[i]["deps"]] + [starts[i] - ahead]) for i in range(n)}
    for i in sorted(range(n), key=lambda i: (when[i], starts[i], i)):
        for d in sorted(sends[i]["deps"], key=lambda d: arrive[d]):
            if d not in waited:
                waited.add(d)
                steps.append(("wait", d))
        steps.append(("start", i))
    steps += [("wait", d) for d in sorted(range(n), key=lambda d: arrive[d]) if d not in waited]
    return sends, steps, max(arrive.values())

def gather_kernel(feat_ref, edge_ref, src_ref, count_ref, out_ref, relay_ref, self_ref, edge_out, src_out, count_out,
                  edge_in, edge_half,
                  send_sem, recv_sem, row_send, row_recv, swap_send, swap_recv, own_sem, *, xs, zs, cut, sends, steps, after):
    me = lax.axis_index("nodes")
    f = lax.axis_index("feat")
    feats = lax.axis_size("feat")
    x, z = me // zs, me % zs
    core, parity = f % 2, x % 2
    cols, rows = feat_ref.shape
    own = rows // feats
    sibling = f + 1 - 2 * core
    across = (x + 1 - 2 * parity) * zs + z
    base = (x - parity + core)
    home = base * zs + z
    peers = {w: ((x + dx) % xs) * zs + (z + dz) % zs for w, (dx, dz) in WAYS.items()}

    barrier = pltpu.get_barrier_semaphore()
    for w in peers:
        pl.semaphore_signal(barrier, inc=1, device_id={"nodes": peers[w]}, device_id_type=MESH)
    for d in range(1, feats):
        pl.semaphore_signal(barrier, inc=1, device_id={"feat": (f + d) % feats}, device_id_type=MESH)
    pl.semaphore_signal(barrier, inc=1, device_id={"nodes": across, "feat": sibling}, device_id_type=MESH)
    pl.semaphore_wait(barrier, len(peers) + feats)

    left, right = pl.ds(0, cut), pl.ds(cut, rows - cut)
    moves = ((feat_ref.at[:, left], out_ref.at[home, :, left]), (feat_ref.at[:, right], out_ref.at[home, :, right]),
             (edge_half, edge_out), (src_ref, src_out), (count_ref, count_out))
    theirs = (x + 1 - 2 * parity) - (1 - parity) + (1 - core)
    theirs = theirs * zs + z
    there = (out_ref.at[theirs, :, left], out_ref.at[theirs, :, right], edge_out, src_out, count_out)

    def swap(i):
        return pltpu.make_async_remote_copy(
            src_ref=moves[i][0], dst_ref=there[i], send_sem=swap_send.at[i], recv_sem=swap_recv.at[i],
            device_id={"nodes": across, "feat": sibling}, device_id_type=MESH)
    def keep(i):
        return pltpu.make_async_copy(moves[i][0], moves[i][1], own_sem.at[i])

    def to_owner(d):
        j = (f + d) % feats
        return pltpu.make_async_remote_copy(
            src_ref=feat_ref.at[:, pl.ds(pl.multiple_of(j * own, own), own)], dst_ref=self_ref.at[f],
            send_sem=row_send.at[d], recv_sem=row_recv.at[d], device_id={"feat": j}, device_id_type=MESH)

    edges = pltpu.make_async_copy(edge_ref, edge_in, own_sem.at[6])
    edges.start()
    @pl.when(parity != core)
    def _():
        for i in (0, 1):
            swap(i).start()
    @pl.when(parity == core)
    def _():
        for i in (0, 1):
            keep(i).start()
    mine = pltpu.make_async_copy(feat_ref.at[:, pl.ds(pl.multiple_of(f * own, own), own)], self_ref.at[f], own_sem.at[5])
    mine.start()
    @pl.when(parity != core)
    def _():
        for i in (0, 1):
            swap(i).wait_recv()
    @pl.when(parity == core)
    def _():
        for i in (0, 1):
            keep(i).wait()

    def later():
        edges.wait()
        def narrow(t, carry):
            edge_half[t] = edge_in[t].astype(jnp.float32).astype(jnp.bfloat16)
            return carry
        lax.fori_loop(0, edge_in.shape[0], narrow, 0)
        for d in range(1, feats):
            to_owner(d).start()
        @pl.when(parity != core)
        def _():
            for i in (2, 3, 4):
                swap(i).start()
        @pl.when(parity == core)
        def _():
            for i in (2, 3, 4):
                keep(i).start()

    def refs(s, block, relay, b):
        other, dz = block
        c = left if s["region"] == 0 else right
        r = pl.ds(0, cols) if s["half"] is None else pl.ds(s["half"] * (cols // 2), cols // 2)
        if relay:
            return relay_ref.at[dz, r, c]
        return out_ref.at[((b + 2 * other) % xs) * zs + (z + dz) % zs, r, c]

    def copy(i):
        s = sends[i]
        src = refs(s, s["block"], s["relayed"], base)
        wx, wz = WAYS.get(s["way"], (0, 0))
        if s["lands"] == "sibling":
            dst = src
            where = {"feat": sibling}
        else:
            where = {"nodes": peers[s["way"]]}
            if s["lands"] is None:
                dst = refs(s, s["block"], True, base)
            elif s["relayed"]:
                b = (x + wx) % xs
                b = b - b % 2 + core
                dst = relay_dst(s, b)
            else:
                dst = src
        return pltpu.make_async_remote_copy(src_ref=src, dst_ref=dst, send_sem=send_sem.at[i], recv_sem=recv_sem.at[i],
                                            device_id=where, device_id_type=MESH)

    def relay_dst(s, b):
        return refs(s, (1, s["block"][1]), False, b)

    def arrival(i):
        s = sends[i]
        if s["lands"] == "sibling":
            b = x - parity + 1 - core
            dst = refs(s, s["block"], False, b)
            where = {"feat": sibling}
        else:
            where = {"nodes": peers[s["way"]]}
            dst = refs(s, s["block"], True, base) if s["lands"] is None else refs(s, s["lands"], False, base)
        return pltpu.make_async_remote_copy(src_ref=dst, dst_ref=dst, send_sem=send_sem.at[i], recv_sem=recv_sem.at[i],
                                            device_id=where, device_id_type=MESH)

    for n, (what, i) in enumerate(steps):
        if n == steps.index(("wait", next(j for w, j in steps if w == "wait"))) + after:
            later()
        if what == "start":
            copy(i).start()
        else:
            arrival(i).wait_recv()
    for i in range(len(sends)):
        copy(i).wait_send()
    for d in range(1, feats):
        to_owner(d).wait()
    mine.wait()
    @pl.when(parity != core)
    def _():
        for i in range(2):
            swap(i).wait_send()
        for i in (2, 3, 4):
            swap(i).wait()
    @pl.when(parity == core)
    def _():
        for i in (2, 3, 4):
            keep(i).wait()

def gather(feat_t, edge_rows, src_tiles, counts, xs=4, zs=8, feats=8, cut=896, after=0, ahead=4.0, cid=1):
    cols, rows = feat_t.shape
    def seconds(s):
        n = cols * (cut if s["region"] == 0 else rows - cut) * 2 / (1 if s["half"] is None else 2)
        return n / 300e3 if s["way"] == "core" else 2 * n / 94e3
    sends, steps, end = plan_gather(zs, seconds, ahead)
    anywhere = pl.BlockSpec(memory_space=pl.ANY)
    dma = pltpu.SemaphoreType.DMA
    shape = jax.ShapeDtypeStruct
    return pl.pallas_call(
        functools.partial(gather_kernel, xs=xs, zs=zs, cut=cut, sends=sends, steps=steps, after=after),
        out_shape=(shape((xs * zs, cols, rows), feat_t.dtype), shape((zs, cols, rows), feat_t.dtype),
                   shape((feats, cols, rows // feats), feat_t.dtype), shape(edge_rows.shape, jnp.bfloat16),
                   shape(src_tiles.shape, src_tiles.dtype), shape(counts.shape, counts.dtype)),
        in_specs=[pl.BlockSpec(memory_space=pltpu.VMEM)] + [anywhere] * 3,
        out_specs=(anywhere,) * 6,
        scratch_shapes=[pltpu.VMEM(edge_rows.shape, edge_rows.dtype), pltpu.VMEM(edge_rows.shape, jnp.bfloat16),
                        dma((len(sends),)), dma((len(sends),)), dma((feats,)), dma((feats,)), dma((5,)), dma((5,)), dma((7,))],
        compiler_params=pltpu.CompilerParams(collective_id=cid, has_side_effects=True),
    )(feat_t, edge_rows, src_tiles, counts)

def layer_kernel(feat_ref, agg_ref, self_ref, ws_ref, wn_ref, cot_ref, act_ref, wg_ref,
                 rows_buf, lhs, base, left, gz, xout, xbuf, zout, zbuf,
                 a_send, a_recv, y_send, y_recv, x_send, x_recv, z_send, z_recv, s_send, s_recv, *, xs, zs, ys):
    me = lax.axis_index("nodes")
    f = lax.axis_index("feat")
    x, z = me // zs, me % zs
    y, core = f // 2, f % 2
    feats = 2 * ys
    cols = feat_ref.shape[0]
    own = cot_ref.shape[0]
    hidden = ws_ref.shape[1]
    chunks = hidden // 256
    half = hidden // 2

    def remote(src, dst, send, recv, **where):
        return pltpu.make_async_remote_copy(src_ref=src, dst_ref=dst, send_sem=send, recv_sem=recv,
                                            device_id=where, device_id_type=MESH)

    parity = x % 2
    pair = x - parity
    across = (pair + 1 - parity) * zs + z
    shard = 2 * y + parity

    barrier = pltpu.get_barrier_semaphore()
    for d in range(feats):
        j = (f + d) % feats
        if d:
            pl.semaphore_signal(barrier, inc=1, device_id={"feat": j}, device_id_type=MESH)
        pl.semaphore_signal(barrier, inc=1, device_id={"nodes": across, "feat": j}, device_id_type=MESH)
    for other in (x + 2, x + xs - 1 + 2 * parity):
        pl.semaphore_signal(barrier, inc=1, device_id={"nodes": (other % xs) * zs + z}, device_id_type=MESH)
    for d in range(1, zs):
        pl.semaphore_signal(barrier, inc=1, device_id={"nodes": x * zs + (z + d) % zs}, device_id_type=MESH)
    pl.semaphore_wait(barrier, 2 * feats - 1 + 2 + zs - 1)

    def to_owner(d):
        j = (f + d) % feats
        return remote(agg_ref.at[:, pl.ds(pl.multiple_of(j * own, own), own)], rows_buf.at[shard],
                      a_send.at[d], a_recv.at[shard], nodes=(pair + core) * zs + z, feat=j)
    def from_shard(i):
        return remote(rows_buf.at[i], rows_buf.at[i], a_send.at[0], a_recv.at[i],
                      nodes=(pair + i % 2) * zs + z, feat=i - i % 2 + parity)
    def swap():
        return remote(agg_ref, left.at[pl.ds(cols, cols)], s_send, s_recv, nodes=across, feat=f + 1 - 2 * core)
    for d in range(1, feats):
        to_owner(d).start()
    @pl.when(parity != core)
    def _():
        to_owner(0).start()
    @pl.when(parity == core)
    def _():
        rows_buf[f] = agg_ref[:, pl.ds(pl.multiple_of(f * own, own), own)]
        left[cols:, :] = agg_ref[...]
    left[0:cols, :] = feat_ref[...]
    lhs[...] = self_ref[...].reshape(feats * cols, own).T
    base[...] = jnp.dot(lhs[...], ws_ref[...], preferred_element_type=jnp.float32)
    for d in range(feats):
        i = (f + d) % feats
        if d:
            from_shard(i).wait_recv()
        else:
            @pl.when(parity != core)
            def _():
                from_shard(i).wait_recv()
    @pl.when(parity != core)
    def _():
        swap().start()
    lhs[...] = rows_buf[...].reshape(feats * cols, own).T

    up, down = (y + 1) % ys, (y + ys - 1) % ys
    far = (y + 2) % ys
    sibling = 2 * y + 1 - core
    hrows = own // 2
    def spread(c, k):
        by = (y, y, y, down, up, down, up, far, far)[k]
        to = (sibling, 2 * up + core, 2 * down + core, 2 * up + core, 2 * down + core) + (sibling,) * 4
        r = {3: pl.ds(0, hrows), 4: pl.ds(hrows, hrows), 7: pl.ds(0, hrows), 8: pl.ds(hrows, hrows)}.get(k, pl.ds(0, own))
        ref = gz.at[c, 2 * by + core, r]
        return remote(ref, ref, y_send.at[c, k], y_recv.at[c, k], feat=to[k])

    def columns(ref, c):
        return jnp.concatenate([ref[:, pl.ds(pl.multiple_of(c * 128, 128), 128)],
                                ref[:, pl.ds(pl.multiple_of(half + c * 128, 128), 128)]], axis=1)

    def layer(c, carry):
        v = columns(base, c) + jnp.dot(lhs[...], columns(wn_ref, c), preferred_element_type=jnp.float32)
        s = math.sqrt(2 / math.pi)
        v2 = v * v
        t = jnp.tanh(s * (v + 0.044715 * (v2 * v)))
        cdf = 0.5 * (1.0 + t)
        out = (v * cdf).astype(jnp.bfloat16)
        act_ref[:, pl.ds(pl.multiple_of(c * 128, 128), 128)] = out[:, :128]
        act_ref[:, pl.ds(pl.multiple_of(half + c * 128, 128), 128)] = out[:, 128:]
        slope = cdf + (0.5 * s) * v * (1.0 - t * t) * (1.0 + (3 * 0.044715) * v2)
        gz[c, f] = (columns(cot_ref, c).astype(jnp.float32) * slope).astype(jnp.bfloat16)
        for k in (1, 2, 0):
            spread(c, k).start()
        return carry
    lax.fori_loop(0, chunks, layer, 0)

    def xcopy(c, d):
        to = (x + d) % xs
        return remote(xout.at[c, to], xbuf.at[c, d], x_send.at[c, d], x_recv.at[c, d], nodes=to * zs + z)
    def zcopy(c, p, zto):
        return remote(zout.at[c, p], zbuf.at[z], z_send.at[c, p], z_recv.at[z], nodes=x * zs + zto)

    def relay(c, carry):
        spread(c, 1).wait_recv()
        spread(c, 3).start()
        spread(c, 5).start()
        spread(c, 2).wait_recv()
        spread(c, 4).start()
        spread(c, 6).start()
        return carry
    def terms(c, carry):
        for k in (3, 4):
            spread(c, k).wait_recv()
            spread(c, k + 4).start()
        for k in (0, 5, 6, 7, 8):
            spread(c, k).wait_recv()
        g = gz[c].reshape(feats * own, 256)
        term = jnp.dot(left[...], g, preferred_element_type=jnp.float32)
        for q in range(4):
            piece = term[(q // 2) * cols:(q // 2 + 1) * cols, (q % 2) * 128:(q % 2) * 128 + 128]
            xout[c, q] = piece
        for d in range(1, xs):
            xcopy(c, d).start()
        return carry
    def sums(c, carry):
        for d in range(1, xs):
            xcopy(c, d).wait_recv()
        total = xout[c, x] + xbuf[c, 1] + xbuf[c, 2] + xbuf[c, 3]
        total = jnp.concatenate([total, jnp.zeros((128 - cols, 128), jnp.float32)], axis=0).T
        for p in range(2):
            zto = 2 * c + p
            zout[c, p] = total[64 * p:64 * p + 64]
            @pl.when(zto != z)
            def _():
                zcopy(c, p, zto).start()
            @pl.when(zto == z)
            def _():
                zbuf[z] = total[64 * p:64 * p + 64]
        return carry
    def both(c, carry):
        relay(c, carry)
        @pl.when(c > 0)
        def _():
            terms(c - 1, carry)
        @pl.when(c > 1)
        def _():
            sums(c - 2, carry)
        return carry
    @pl.when(parity != core)
    def _():
        swap().wait_recv()
    lax.fori_loop(0, chunks, both, 0)
    terms(chunks - 1, 0)
    sums(chunks - 2, 0)
    sums(chunks - 1, 0)
    def arrived(i, carry):
        @pl.when(i != z)
        def _():
            remote(zout.at[0, 0], zbuf.at[i], z_send.at[0, 0], z_recv.at[i], nodes=x * zs + i).wait_recv()
        return carry
    lax.fori_loop(0, zs, arrived, 0)
    wg_ref[...] = jnp.sum(zbuf[...], axis=0)[:, :cols]

    def finish(c, carry):
        for k in range(9):
            spread(c, k).wait_send()
        for d in range(1, xs):
            xcopy(c, d).wait_send()
        for p in range(2):
            @pl.when(2 * c + p != z)
            def _():
                zcopy(c, p, 2 * c + p).wait_send()
        return carry
    lax.fori_loop(0, chunks, finish, 0)
    for d in range(1, feats):
        to_owner(d).wait_send()
    @pl.when(parity != core)
    def _():
        to_owner(0).wait_send()
        swap().wait_send()

def layer(feat_t, agg_t, self_rows, w_self, w_neigh, cot, xs=4, zs=8, ys=4, cid=2):
    cols, rows = feat_t.shape
    own, hidden = cot.shape
    feats, chunks = 2 * ys, hidden // 256
    v = pl.BlockSpec(memory_space=pltpu.VMEM)
    dma = pltpu.SemaphoreType.DMA
    f32, bf16 = jnp.float32, jnp.bfloat16
    return pl.pallas_call(
        functools.partial(layer_kernel, xs=xs, zs=zs, ys=ys),
        out_shape=(jax.ShapeDtypeStruct((own, hidden), bf16), jax.ShapeDtypeStruct((hidden // (xs * zs) * 2, cols), f32)),
        in_specs=[v] * 6,
        out_specs=(v, v),
        scratch_shapes=[
            pltpu.VMEM((feats, cols, own), bf16), pltpu.VMEM((own, feats * cols), bf16), pltpu.VMEM((own, hidden), f32),
            pltpu.VMEM((2 * cols, rows), bf16), pltpu.VMEM((chunks, feats, own, 256), bf16),
            pltpu.VMEM((chunks, 4, cols, 128), f32), pltpu.VMEM((chunks, xs, cols, 128), f32),
            pltpu.VMEM((chunks, 2, 64, 128), f32), pltpu.VMEM((zs, 64, 128), f32),
            dma((feats,)), dma((feats,)), dma((chunks, 9)), dma((chunks, 9)),
            dma((chunks, xs)), dma((chunks, xs)), dma((chunks, 2)), dma((zs,)), dma, dma,
        ],
        compiler_params=pltpu.CompilerParams(collective_id=cid, has_side_effects=True, vmem_limit_bytes=48 * 2**20),
    )(feat_t, agg_t, self_rows, w_self, w_neigh, cot)


def agg_kernel(src_ref, count_ref, rows_hbm, g_hbm, out_ref, picks_ref, rows_ref, g_ref, sems):
    tiles, slots, span = rows_ref.shape
    cols = g_ref.shape[1]
    blocks_total = g_ref.shape[0]
    per_block = g_ref.shape[2] // span
    iota = lax.broadcasted_iota(jnp.int32, (span, span), 0).astype(jnp.float32).astype(jnp.bfloat16)
    one = jnp.ones((span, span), jnp.bfloat16)
    zero = jnp.zeros((span, span), jnp.bfloat16)
    slot_ids = lax.broadcasted_iota(jnp.int32, (slots, span), 0)
    loads = [pltpu.make_async_copy(rows_hbm, rows_ref, sems.at[blocks_total])]
    loads += [pltpu.make_async_copy(g_hbm.at[n], g_ref.at[n], sems.at[n]) for n in range(blocks_total)]
    for load in loads:
        load.start()
    for load in loads:
        load.wait()

    def tile(t, carry):
        used = count_ref[t]
        picks_ref[...] = jnp.where(slot_ids < used, rows_ref[t].astype(jnp.float32), -1.0)

        def step(i, acc):
            onehots, blocks = [], []
            for u in range(UNROLL):
                k = i * UNROLL + u
                pick = jnp.broadcast_to(picks_ref[pl.ds(k, 1), :], (16, span)).astype(jnp.bfloat16)
                pick = jnp.concatenate([pick] * (span // 16), axis=0)
                onehots.append(jnp.where(pick == iota, one, zero))
                s = src_ref[t, k]
                start = pl.multiple_of((s % per_block) * span, span)
                blocks.append(g_ref[s // per_block, :, pl.ds(start, span)])
            return acc + jnp.dot(
                jnp.concatenate(blocks, axis=1),
                jnp.concatenate(onehots, axis=0),
                preferred_element_type=jnp.float32,
            )

        total = lax.fori_loop(0, (used + UNROLL - 1) // UNROLL, step, jnp.zeros((cols, span), jnp.float32))
        mean = total / used.astype(jnp.float32)
        out_ref[:, pl.ds(pl.multiple_of(t * span, span), span)] = mean.astype(jnp.bfloat16)
        return carry

    lax.fori_loop(0, tiles, tile, 0)


def neighbour_mean(src_tiles, counts, edge_rows, gathered):
    tiles, slots, span = edge_rows.shape
    blocks, cols, rows = gathered.shape
    smem = pl.BlockSpec(memory_space=pltpu.SMEM)
    anywhere = pl.BlockSpec(memory_space=pl.ANY)
    return pl.pallas_call(
        agg_kernel,
        out_shape=jax.ShapeDtypeStruct((cols, tiles * span), jnp.bfloat16),
        in_specs=[smem, smem, anywhere, anywhere],
        out_specs=pl.BlockSpec(memory_space=pltpu.VMEM),
        scratch_shapes=[pltpu.VMEM((slots, span), jnp.float32), pltpu.VMEM(edge_rows.shape, edge_rows.dtype),
                        pltpu.VMEM(gathered.shape, gathered.dtype), pltpu.SemaphoreType.DMA((blocks + 1,))],
        compiler_params=pltpu.CompilerParams(vmem_limit_bytes=62 * 2**20),
    )(src_tiles, counts, edge_rows, gathered)


def per_device(features, w_self, w_neigh, src_tiles, counts, edge_rows, cotangent):
    feat_t = features.T
    gathered, _, self_rows, edge_rows, src_tiles, counts = gather(feat_t, edge_rows, src_tiles, counts)
    agg_t = neighbour_mean(src_tiles, counts, edge_rows, gathered)
    activations, grads_t = layer(feat_t, agg_t, self_rows, w_self, w_neigh, cotangent)
    return activations, grads_t.T


def solution(mesh):
    in_specs = (
        P("nodes", "feat"),
        P(),
        P(),
        P("nodes", None),
        P("nodes"),
        P("nodes", None, None),
        P(("nodes", "feat"), None),
    )
    out_specs = (P(("nodes", "feat"), None), P("feat", "nodes"))
    return jax.shard_map(
        per_device, mesh=mesh, in_specs=in_specs, out_specs=out_specs, check_vma=False
    )
```

```python
import functools
import math

import jax
import jax.numpy as jnp
from jax import lax
from jax.experimental import pallas as pl
from jax.experimental.pallas import tpu as pltpu
from jax.sharding import PartitionSpec as P

UNROLL = 8
MESH = pl.DeviceIdType.MESH
WAYS = {"x+": (1, 0), "x-": (-1, 0), "z+": (0, 1), "z-": (0, -1)}

def plan_gather(zs, seconds, ahead=4.0):
    sends, have = [], {}

    def add(way, block, region, half, passing, get):
        deps = [] if passing is None else [passing]
        if passing is None:
            for h in (0, 1) if half is None else (half,):
                deps += have.get((block, region, h), [])
        sends.append(dict(way=way, block=block, region=region, half=half, relayed=passing is not None,
                          lands=get, deps=sorted(set(deps))))
        if get is not None and get != "sibling":
            for h in (0, 1) if half is None else (half,):
                have[(get, region, h)] = [len(sends) - 1]
        return len(sends) - 1

    def along_z(other, region):
        for d in range(1, zs // 2 + 1):
            for way, s in (("z+", 1), ("z-", -1)):
                half = None if d < zs // 2 else (0 if s == 1 else 1)
                add(way, (other, -s * (d - 1) % zs), region, half, None, (other, -s * d % zs))

    def along_x(dz, region):
        for way, half in (("x+", 0), ("x-", 1)):
            first = add(way, (0, dz), region, half, None, None)
            add(way, (0, dz), region, half, first, (1, dz))

    order = [0]
    for d in range(1, zs // 2):
        order += [d, zs - d]
    order += [zs // 2]
    along_x(0, 0)
    along_z(0, 1)
    along_z(0, 0)
    along_z(1, 0)
    for dz in order:
        along_x(dz, 1)
    for other in (0, 1):
        for dz in order:
            for region in (0, 1):
                add("core", (other, dz), region, None, None, "sibling")

    n = len(sends)
    chain = [0] * n
    for i in reversed(range(n)):
        for d in sends[i]["deps"]:
            chain[d] = max(chain[d], chain[i] + 1)
    free, arrive, starts, todo = {}, {}, {}, set(range(n))
    while todo:
        best = None
        for i in todo:
            if all(d in arrive for d in sends[i]["deps"]):
                ready = max([arrive[d] for d in sends[i]["deps"]], default=0.0)
                at = max(ready, free.get(sends[i]["way"], 0.0))
                key = (at, -chain[i], ready, i)
                best = key if best is None else min(best, key)
        at, _, _, i = best
        todo.remove(i)
        starts[i] = at
        free[sends[i]["way"]] = at + seconds(sends[i])
        arrive[i] = at + seconds(sends[i]) + 1.5
    steps, waited = [], set()
    when = {i: max([arrive[d] for d in sends[i]["deps"]] + [starts[i] - ahead]) for i in range(n)}
    for i in sorted(range(n), key=lambda i: (when[i], starts[i], i)):
        for d in sorted(sends[i]["deps"], key=lambda d: arrive[d]):
            if d not in waited:
                waited.add(d)
                steps.append(("wait", d))
        steps.append(("start", i))
    steps += [("wait", d) for d in sorted(range(n), key=lambda d: arrive[d]) if d not in waited]
    return sends, steps, max(arrive.values())

def gather_kernel(feat_ref, edge_ref, src_ref, count_ref, out_ref, self_ref, edge_out, src_out, count_out,
                  relay_ref, edge_half,
                  send_sem, recv_sem, row_send, row_recv, swap_send, swap_recv, own_sem, *, xs, zs, cut, sends, steps, after):
    me = lax.axis_index("nodes")
    f = lax.axis_index("feat")
    feats = lax.axis_size("feat")
    x, z = me // zs, me % zs
    core, parity = f % 2, x % 2
    cols, rows = feat_ref.shape
    own = rows // feats
    sibling = f + 1 - 2 * core
    across = (x + 1 - 2 * parity) * zs + z
    base = (x - parity + core)
    home = base * zs + z
    peers = {w: ((x + dx) % xs) * zs + (z + dz) % zs for w, (dx, dz) in WAYS.items()}

    barrier = pltpu.get_barrier_semaphore()
    for w in peers:
        pl.semaphore_signal(barrier, inc=1, device_id={"nodes": peers[w]}, device_id_type=MESH)
    for d in range(1, feats):
        pl.semaphore_signal(barrier, inc=1, device_id={"feat": (f + d) % feats}, device_id_type=MESH)
    pl.semaphore_signal(barrier, inc=1, device_id={"nodes": across, "feat": sibling}, device_id_type=MESH)
    pl.semaphore_wait(barrier, len(peers) + feats)

    left, right = pl.ds(0, cut), pl.ds(cut, rows - cut)
    moves = ((feat_ref.at[:, left], out_ref.at[home, :, left]), (feat_ref.at[:, right], out_ref.at[home, :, right]),
             (edge_half, edge_out), (src_ref, src_out), (count_ref, count_out))
    theirs = (x + 1 - 2 * parity) - (1 - parity) + (1 - core)
    theirs = theirs * zs + z
    there = (out_ref.at[theirs, :, left], out_ref.at[theirs, :, right], edge_out, src_out, count_out)

    def swap(i):
        return pltpu.make_async_remote_copy(
            src_ref=moves[i][0], dst_ref=there[i], send_sem=swap_send.at[i], recv_sem=swap_recv.at[i],
            device_id={"nodes": across, "feat": sibling}, device_id_type=MESH)
    def keep(i):
        return pltpu.make_async_copy(moves[i][0], moves[i][1], own_sem.at[i])

    def to_owner(d):
        j = (f + d) % feats
        return pltpu.make_async_remote_copy(
            src_ref=feat_ref.at[:, pl.ds(pl.multiple_of(j * own, own), own)], dst_ref=self_ref.at[f],
            send_sem=row_send.at[d], recv_sem=row_recv.at[d], device_id={"feat": j}, device_id_type=MESH)

    @pl.when(parity != core)
    def _():
        for i in (0, 1):
            swap(i).start()
    @pl.when(parity == core)
    def _():
        for i in (0, 1):
            keep(i).start()
    mine = pltpu.make_async_copy(feat_ref.at[:, pl.ds(pl.multiple_of(f * own, own), own)], self_ref.at[f], own_sem.at[5])
    mine.start()
    @pl.when(parity != core)
    def _():
        for i in (0, 1):
            swap(i).wait_recv()
    @pl.when(parity == core)
    def _():
        for i in (0, 1):
            keep(i).wait()

    def later():
        def narrow(t, carry):
            edge_half[t] = edge_ref[t].astype(jnp.float32).astype(jnp.bfloat16)
            return carry
        lax.fori_loop(0, edge_ref.shape[0], narrow, 0)
        for d in range(1, feats):
            to_owner(d).start()
        @pl.when(parity != core)
        def _():
            for i in (2, 3, 4):
                swap(i).start()
        @pl.when(parity == core)
        def _():
            for i in (2, 3, 4):
                keep(i).start()

    def refs(s, block, relay, b):
        other, dz = block
        c = left if s["region"] == 0 else right
        r = pl.ds(0, cols) if s["half"] is None else pl.ds(s["half"] * (cols // 2), cols // 2)
        if relay:
            return relay_ref.at[dz, r, c]
        return out_ref.at[((b + 2 * other) % xs) * zs + (z + dz) % zs, r, c]

    def copy(i):
        s = sends[i]
        src = refs(s, s["block"], s["relayed"], base)
        wx, wz = WAYS.get(s["way"], (0, 0))
        if s["lands"] == "sibling":
            dst = src
            where = {"feat": sibling}
        else:
            where = {"nodes": peers[s["way"]]}
            if s["lands"] is None:
                dst = refs(s, s["block"], True, base)
            elif s["relayed"]:
                b = (x + wx) % xs
                b = b - b % 2 + core
                dst = relay_dst(s, b)
            else:
                dst = src
        return pltpu.make_async_remote_copy(src_ref=src, dst_ref=dst, send_sem=send_sem.at[i], recv_sem=recv_sem.at[i],
                                            device_id=where, device_id_type=MESH)

    def relay_dst(s, b):
        return refs(s, (1, s["block"][1]), False, b)

    def arrival(i):
        s = sends[i]
        if s["lands"] == "sibling":
            b = x - parity + 1 - core
            dst = refs(s, s["block"], False, b)
            where = {"feat": sibling}
        else:
            where = {"nodes": peers[s["way"]]}
            dst = refs(s, s["block"], True, base) if s["lands"] is None else refs(s, s["lands"], False, base)
        return pltpu.make_async_remote_copy(src_ref=dst, dst_ref=dst, send_sem=send_sem.at[i], recv_sem=recv_sem.at[i],
                                            device_id=where, device_id_type=MESH)

    for n, (what, i) in enumerate(steps):
        if n == steps.index(("wait", next(j for w, j in steps if w == "wait"))) + after:
            later()
        if what == "start":
            copy(i).start()
        else:
            arrival(i).wait_recv()
    for i in range(len(sends)):
        copy(i).wait_send()
    for d in range(1, feats):
        to_owner(d).wait()
    mine.wait()
    @pl.when(parity != core)
    def _():
        for i in range(2):
            swap(i).wait_send()
        for i in (2, 3, 4):
            swap(i).wait()
    @pl.when(parity == core)
    def _():
        for i in (2, 3, 4):
            keep(i).wait()

def gather(feat_t, edge_rows, src_tiles, counts, xs=4, zs=8, feats=8, cut=896, after=0, ahead=2.0, cid=1):
    cols, rows = feat_t.shape
    def seconds(s):
        n = cols * (cut if s["region"] == 0 else rows - cut) * 2 / (1 if s["half"] is None else 2)
        return n / 300e3 if s["way"] == "core" else 2 * n / 94e3
    sends, steps, end = plan_gather(zs, seconds, ahead)
    anywhere = pl.BlockSpec(memory_space=pl.ANY)
    vmem = pl.BlockSpec(memory_space=pltpu.VMEM)
    dma = pltpu.SemaphoreType.DMA
    shape = jax.ShapeDtypeStruct
    return pl.pallas_call(
        functools.partial(gather_kernel, xs=xs, zs=zs, cut=cut, sends=sends, steps=steps, after=after),
        out_shape=(shape((xs * zs, cols, rows), feat_t.dtype),
                   shape((feats, cols, rows // feats), feat_t.dtype), shape(edge_rows.shape, jnp.bfloat16),
                   shape(src_tiles.shape, src_tiles.dtype), shape(counts.shape, counts.dtype)),
        in_specs=[vmem, vmem, anywhere, anywhere],
        out_specs=(vmem,) * 3 + (anywhere,) * 2,
        scratch_shapes=[pltpu.VMEM((zs, cols, rows), feat_t.dtype), pltpu.VMEM(edge_rows.shape, jnp.bfloat16),
                        dma((len(sends),)), dma((len(sends),)), dma((feats,)), dma((feats,)), dma((5,)), dma((5,)), dma((7,))],
        compiler_params=pltpu.CompilerParams(collective_id=cid, has_side_effects=True, vmem_limit_bytes=24 * 2**20),
    )(feat_t, edge_rows, src_tiles, counts)

def layer_kernel(feat_ref, agg_ref, self_ref, ws_ref, wn_ref, cot_ref, act_ref, wg_ref,
                 rows_buf, lhs, base, left, gz, xout, xbuf, zout, zbuf,
                 a_send, a_recv, y_send, y_recv, x_send, x_recv, z_send, z_recv, s_send, s_recv, *, xs, zs, ys):
    me = lax.axis_index("nodes")
    f = lax.axis_index("feat")
    x, z = me // zs, me % zs
    y, core = f // 2, f % 2
    feats = 2 * ys
    cols = feat_ref.shape[0]
    own = cot_ref.shape[0]
    hidden = ws_ref.shape[1]
    chunks = hidden // 256
    half = hidden // 2

    def remote(src, dst, send, recv, **where):
        return pltpu.make_async_remote_copy(src_ref=src, dst_ref=dst, send_sem=send, recv_sem=recv,
                                            device_id=where, device_id_type=MESH)

    parity = x % 2
    pair = x - parity
    across = (pair + 1 - parity) * zs + z
    shard = 2 * y + parity

    barrier = pltpu.get_barrier_semaphore()
    for d in range(feats):
        j = (f + d) % feats
        if d:
            pl.semaphore_signal(barrier, inc=1, device_id={"feat": j}, device_id_type=MESH)
        pl.semaphore_signal(barrier, inc=1, device_id={"nodes": across, "feat": j}, device_id_type=MESH)
    for other in (x + 2, x + xs - 1 + 2 * parity):
        pl.semaphore_signal(barrier, inc=1, device_id={"nodes": (other % xs) * zs + z}, device_id_type=MESH)
    for d in range(1, zs):
        pl.semaphore_signal(barrier, inc=1, device_id={"nodes": x * zs + (z + d) % zs}, device_id_type=MESH)
    pl.semaphore_wait(barrier, 2 * feats - 1 + 2 + zs - 1)

    def to_owner(d):
        j = (f + d) % feats
        return remote(agg_ref.at[:, pl.ds(pl.multiple_of(j * own, own), own)], rows_buf.at[shard],
                      a_send.at[d], a_recv.at[shard], nodes=(pair + core) * zs + z, feat=j)
    def from_shard(i):
        return remote(rows_buf.at[i], rows_buf.at[i], a_send.at[0], a_recv.at[i],
                      nodes=(pair + i % 2) * zs + z, feat=i - i % 2 + parity)
    def swap():
        return remote(agg_ref, left.at[pl.ds(cols, cols)], s_send, s_recv, nodes=across, feat=f + 1 - 2 * core)
    for d in range(1, feats):
        to_owner(d).start()
    @pl.when(parity != core)
    def _():
        to_owner(0).start()
    @pl.when(parity == core)
    def _():
        rows_buf[f] = agg_ref[:, pl.ds(pl.multiple_of(f * own, own), own)]
        left[cols:, :] = agg_ref[...]
    left[0:cols, :] = feat_ref[...]
    lhs[...] = self_ref[...].reshape(feats * cols, own).T
    base[...] = jnp.dot(lhs[...], ws_ref[...], preferred_element_type=jnp.float32)
    for d in range(feats):
        i = (f + d) % feats
        if d:
            from_shard(i).wait_recv()
        else:
            @pl.when(parity != core)
            def _():
                from_shard(i).wait_recv()
    @pl.when(parity != core)
    def _():
        swap().start()
    lhs[...] = rows_buf[...].reshape(feats * cols, own).T

    up, down = (y + 1) % ys, (y + ys - 1) % ys
    far = (y + 2) % ys
    sibling = 2 * y + 1 - core
    hrows = own // 2
    def spread(c, k):
        by = (y, y, y, down, up, down, up, far, far)[k]
        to = (sibling, 2 * up + core, 2 * down + core, 2 * up + core, 2 * down + core) + (sibling,) * 4
        r = {3: pl.ds(0, hrows), 4: pl.ds(hrows, hrows), 7: pl.ds(0, hrows), 8: pl.ds(hrows, hrows)}.get(k, pl.ds(0, own))
        ref = gz.at[c, 2 * by + core, r]
        return remote(ref, ref, y_send.at[c, k], y_recv.at[c, k], feat=to[k])

    def columns(ref, c):
        return jnp.concatenate([ref[:, pl.ds(pl.multiple_of(c * 128, 128), 128)],
                                ref[:, pl.ds(pl.multiple_of(half + c * 128, 128), 128)]], axis=1)

    def layer(c, carry):
        v = columns(base, c) + jnp.dot(lhs[...], columns(wn_ref, c), preferred_element_type=jnp.float32)
        s = math.sqrt(2 / math.pi)
        v2 = v * v
        t = jnp.tanh(s * (v + 0.044715 * (v2 * v)))
        cdf = 0.5 * (1.0 + t)
        out = (v * cdf).astype(jnp.bfloat16)
        act_ref[:, pl.ds(pl.multiple_of(c * 128, 128), 128)] = out[:, :128]
        act_ref[:, pl.ds(pl.multiple_of(half + c * 128, 128), 128)] = out[:, 128:]
        slope = cdf + (0.5 * s) * v * (1.0 - t * t) * (1.0 + (3 * 0.044715) * v2)
        gz[c, f] = (columns(cot_ref, c).astype(jnp.float32) * slope).astype(jnp.bfloat16)
        for k in (1, 2, 0):
            spread(c, k).start()
        return carry
    lax.fori_loop(0, chunks, layer, 0)

    def xcopy(c, d):
        to = (x + d) % xs
        return remote(xout.at[c, to], xbuf.at[c, d], x_send.at[c, d], x_recv.at[c, d], nodes=to * zs + z)
    def zcopy(c, p, zto):
        return remote(zout.at[c, p], zbuf.at[z], z_send.at[c, p], z_recv.at[z], nodes=x * zs + zto)

    def relay(c, carry):
        spread(c, 1).wait_recv()
        spread(c, 3).start()
        spread(c, 5).start()
        spread(c, 2).wait_recv()
        spread(c, 4).start()
        spread(c, 6).start()
        return carry
    def terms(c, carry):
        for k in (3, 4):
            spread(c, k).wait_recv()
            spread(c, k + 4).start()
        for k in (0, 5, 6, 7, 8):
            spread(c, k).wait_recv()
        g = gz[c].reshape(feats * own, 256)
        term = jnp.dot(left[...], g, preferred_element_type=jnp.float32)
        for q in range(4):
            piece = term[(q // 2) * cols:(q // 2 + 1) * cols, (q % 2) * 128:(q % 2) * 128 + 128]
            xout[c, q] = piece
        for d in range(1, xs):
            xcopy(c, d).start()
        return carry
    def sums(c, carry):
        for d in range(1, xs):
            xcopy(c, d).wait_recv()
        total = xout[c, x] + xbuf[c, 1] + xbuf[c, 2] + xbuf[c, 3]
        total = jnp.concatenate([total, jnp.zeros((128 - cols, 128), jnp.float32)], axis=0).T
        for p in range(2):
            zto = 2 * c + p
            zout[c, p] = total[64 * p:64 * p + 64]
            @pl.when(zto != z)
            def _():
                zcopy(c, p, zto).start()
            @pl.when(zto == z)
            def _():
                zbuf[z] = total[64 * p:64 * p + 64]
        return carry
    def both(c, carry):
        relay(c, carry)
        @pl.when(c > 0)
        def _():
            terms(c - 1, carry)
        @pl.when(c > 1)
        def _():
            sums(c - 2, carry)
        return carry
    @pl.when(parity != core)
    def _():
        swap().wait_recv()
    lax.fori_loop(0, chunks, both, 0)
    terms(chunks - 1, 0)
    sums(chunks - 2, 0)
    sums(chunks - 1, 0)
    def arrived(i, carry):
        @pl.when(i != z)
        def _():
            remote(zout.at[0, 0], zbuf.at[i], z_send.at[0, 0], z_recv.at[i], nodes=x * zs + i).wait_recv()
        return carry
    lax.fori_loop(0, zs, arrived, 0)
    wg_ref[...] = jnp.sum(zbuf[...], axis=0)[:, :cols]

    def finish(c, carry):
        for k in range(9):
            spread(c, k).wait_send()
        for d in range(1, xs):
            xcopy(c, d).wait_send()
        for p in range(2):
            @pl.when(2 * c + p != z)
            def _():
                zcopy(c, p, 2 * c + p).wait_send()
        return carry
    lax.fori_loop(0, chunks, finish, 0)
    for d in range(1, feats):
        to_owner(d).wait_send()
    @pl.when(parity != core)
    def _():
        to_owner(0).wait_send()
        swap().wait_send()

def layer(feat_t, agg_t, self_rows, w_self, w_neigh, cot, xs=4, zs=8, ys=4, cid=2):
    cols, rows = feat_t.shape
    own, hidden = cot.shape
    feats, chunks = 2 * ys, hidden // 256
    v = pl.BlockSpec(memory_space=pltpu.VMEM)
    dma = pltpu.SemaphoreType.DMA
    f32, bf16 = jnp.float32, jnp.bfloat16
    return pl.pallas_call(
        functools.partial(layer_kernel, xs=xs, zs=zs, ys=ys),
        out_shape=(jax.ShapeDtypeStruct((own, hidden), bf16), jax.ShapeDtypeStruct((hidden // (xs * zs) * 2, cols), f32)),
        in_specs=[v] * 6,
        out_specs=(v, v),
        scratch_shapes=[
            pltpu.VMEM((feats, cols, own), bf16), pltpu.VMEM((own, feats * cols), bf16), pltpu.VMEM((own, hidden), f32),
            pltpu.VMEM((2 * cols, rows), bf16), pltpu.VMEM((chunks, feats, own, 256), bf16),
            pltpu.VMEM((chunks, 4, cols, 128), f32), pltpu.VMEM((chunks, xs, cols, 128), f32),
            pltpu.VMEM((chunks, 2, 64, 128), f32), pltpu.VMEM((zs, 64, 128), f32),
            dma((feats,)), dma((feats,)), dma((chunks, 9)), dma((chunks, 9)),
            dma((chunks, xs)), dma((chunks, xs)), dma((chunks, 2)), dma((zs,)), dma, dma,
        ],
        compiler_params=pltpu.CompilerParams(collective_id=cid, has_side_effects=True, vmem_limit_bytes=48 * 2**20),
    )(feat_t, agg_t, self_rows, w_self, w_neigh, cot)


def agg_kernel(src_ref, count_ref, rows_ref, g_ref, out_ref, picks_ref):
    tiles, slots, span = rows_ref.shape
    cols = g_ref.shape[1]
    per_block = g_ref.shape[2] // span
    iota = lax.broadcasted_iota(jnp.int32, (span, span), 0).astype(jnp.float32).astype(jnp.bfloat16)
    one = jnp.ones((span, span), jnp.bfloat16)
    zero = jnp.zeros((span, span), jnp.bfloat16)
    slot_ids = lax.broadcasted_iota(jnp.int32, (slots, span), 0)
    def tile(t, carry):
        used = count_ref[t]
        picks_ref[...] = jnp.where(slot_ids < used, rows_ref[t].astype(jnp.float32), -1.0)

        def step(i, acc):
            onehots, blocks = [], []
            for u in range(UNROLL):
                k = i * UNROLL + u
                pick = jnp.broadcast_to(picks_ref[pl.ds(k, 1), :], (16, span)).astype(jnp.bfloat16)
                pick = jnp.concatenate([pick] * (span // 16), axis=0)
                onehots.append(jnp.where(pick == iota, one, zero))
                s = src_ref[t, k]
                start = pl.multiple_of((s % per_block) * span, span)
                blocks.append(g_ref[s // per_block, :, pl.ds(start, span)])
            return acc + jnp.dot(
                jnp.concatenate(blocks, axis=1),
                jnp.concatenate(onehots, axis=0),
                preferred_element_type=jnp.float32,
            )

        total = lax.fori_loop(0, (used + UNROLL - 1) // UNROLL, step, jnp.zeros((cols, span), jnp.float32))
        mean = total / used.astype(jnp.float32)
        out_ref[:, pl.ds(pl.multiple_of(t * span, span), span)] = mean.astype(jnp.bfloat16)
        return carry

    lax.fori_loop(0, tiles, tile, 0)


def neighbour_mean(src_tiles, counts, edge_rows, gathered):
    tiles, slots, span = edge_rows.shape
    cols = gathered.shape[1]
    smem = pl.BlockSpec(memory_space=pltpu.SMEM)
    vmem = pl.BlockSpec(memory_space=pltpu.VMEM)
    return pl.pallas_call(
        agg_kernel,
        out_shape=jax.ShapeDtypeStruct((cols, tiles * span), jnp.bfloat16),
        in_specs=[smem, smem, vmem, vmem],
        out_specs=pl.BlockSpec(memory_space=pltpu.VMEM),
        scratch_shapes=[pltpu.VMEM((slots, span), jnp.float32)],
        compiler_params=pltpu.CompilerParams(vmem_limit_bytes=24 * 2**20),
    )(src_tiles, counts, edge_rows, gathered)


def per_device(features, w_self, w_neigh, src_tiles, counts, edge_rows, cotangent):
    feat_t = features.T
    gathered, self_rows, edge_rows, src_tiles, counts = gather(feat_t, edge_rows, src_tiles, counts)
    agg_t = neighbour_mean(src_tiles, counts, edge_rows, gathered)
    activations, grads_t = layer(feat_t, agg_t, self_rows, w_self, w_neigh, cotangent)
    return activations, grads_t.T


def solution(mesh):
    in_specs = (
        P("nodes", "feat"),
        P(),
        P(),
        P("nodes", None),
        P("nodes"),
        P("nodes", None, None),
        P(("nodes", "feat"), None),
    )
    out_specs = (P(("nodes", "feat"), None), P("feat", "nodes"))
    return jax.shard_map(
        per_device, mesh=mesh, in_specs=in_specs, out_specs=out_specs, check_vma=False
    )
```

```python
import functools
import math

import jax
import jax.numpy as jnp
from jax import lax
from jax.experimental import pallas as pl
from jax.experimental.pallas import tpu as pltpu
from jax.sharding import PartitionSpec as P

UNROLL = 8
MESH = pl.DeviceIdType.MESH
WAYS = {"x+": (1, 0), "x-": (-1, 0), "z+": (0, 1), "z-": (0, -1)}

def plan_gather(zs, seconds, ahead=4.0):
    sends, have = [], {}

    def add(way, block, region, half, passing, get):
        deps = [] if passing is None else [passing]
        if passing is None:
            for h in (0, 1) if half is None else (half,):
                deps += have.get((block, region, h), [])
        sends.append(dict(way=way, block=block, region=region, half=half, relayed=passing is not None,
                          lands=get, deps=sorted(set(deps))))
        if get is not None and get != "sibling":
            for h in (0, 1) if half is None else (half,):
                have[(get, region, h)] = [len(sends) - 1]
        return len(sends) - 1

    def along_z(other, region):
        for d in range(1, zs // 2 + 1):
            for way, s in (("z+", 1), ("z-", -1)):
                half = None if d < zs // 2 else (0 if s == 1 else 1)
                add(way, (other, -s * (d - 1) % zs), region, half, None, (other, -s * d % zs))

    def along_x(dz, region):
        for way, half in (("x+", 0), ("x-", 1)):
            first = add(way, (0, dz), region, half, None, None)
            add(way, (0, dz), region, half, first, (1, dz))

    order = [0]
    for d in range(1, zs // 2):
        order += [d, zs - d]
    order += [zs // 2]
    along_x(0, 0)
    along_z(0, 1)
    along_z(0, 0)
    along_z(1, 0)
    for dz in order:
        along_x(dz, 1)
    for other in (0, 1):
        for dz in order:
            for region in (0, 1):
                add("core", (other, dz), region, None, None, "sibling")

    n = len(sends)
    chain = [0] * n
    for i in reversed(range(n)):
        for d in sends[i]["deps"]:
            chain[d] = max(chain[d], chain[i] + 1)
    free, arrive, starts, todo = {}, {}, {}, set(range(n))
    while todo:
        best = None
        for i in todo:
            if all(d in arrive for d in sends[i]["deps"]):
                ready = max([arrive[d] for d in sends[i]["deps"]], default=0.0)
                at = max(ready, free.get(sends[i]["way"], 0.0))
                key = (at, -chain[i], ready, i)
                best = key if best is None else min(best, key)
        at, _, _, i = best
        todo.remove(i)
        starts[i] = at
        free[sends[i]["way"]] = at + seconds(sends[i])
        arrive[i] = at + seconds(sends[i]) + 1.5
    steps, waited = [], set()
    when = {i: max([arrive[d] for d in sends[i]["deps"]] + [starts[i] - ahead]) for i in range(n)}
    for i in sorted(range(n), key=lambda i: (when[i], starts[i], i)):
        for d in sorted(sends[i]["deps"], key=lambda d: arrive[d]):
            if d not in waited:
                waited.add(d)
                steps.append(("wait", d))
        steps.append(("start", i))
    steps += [("wait", d) for d in sorted(range(n), key=lambda d: arrive[d]) if d not in waited]
    return sends, steps, max(arrive.values())

def gather_kernel(feat_ref, edge_ref, src_ref, count_ref, out_ref, self_ref, edge_out, src_out, count_out,
                  relay_ref, edge_half,
                  send_sem, recv_sem, row_send, row_recv, swap_send, swap_recv, own_sem, *, xs, zs, cut, sends, steps, after):
    me = lax.axis_index("nodes")
    f = lax.axis_index("feat")
    feats = lax.axis_size("feat")
    x, z = me // zs, me % zs
    core, parity = f % 2, x % 2
    cols, rows = feat_ref.shape
    own = rows // feats
    sibling = f + 1 - 2 * core
    across = (x + 1 - 2 * parity) * zs + z
    base = (x - parity + core)
    home = base * zs + z
    peers = {w: ((x + dx) % xs) * zs + (z + dz) % zs for w, (dx, dz) in WAYS.items()}

    barrier = pltpu.get_barrier_semaphore()
    for w in peers:
        pl.semaphore_signal(barrier, inc=1, device_id={"nodes": peers[w]}, device_id_type=MESH)
    for d in range(1, feats):
        pl.semaphore_signal(barrier, inc=1, device_id={"feat": (f + d) % feats}, device_id_type=MESH)
    pl.semaphore_signal(barrier, inc=1, device_id={"nodes": across, "feat": sibling}, device_id_type=MESH)
    pl.semaphore_wait(barrier, len(peers) + feats)

    left, right = pl.ds(0, cut), pl.ds(cut, rows - cut)
    moves = ((feat_ref.at[:, left], out_ref.at[home, :, left]), (feat_ref.at[:, right], out_ref.at[home, :, right]),
             (edge_half, edge_out), (src_ref, src_out), (count_ref, count_out))
    theirs = (x + 1 - 2 * parity) - (1 - parity) + (1 - core)
    theirs = theirs * zs + z
    there = (out_ref.at[theirs, :, left], out_ref.at[theirs, :, right], edge_out, src_out, count_out)

    def swap(i):
        return pltpu.make_async_remote_copy(
            src_ref=moves[i][0], dst_ref=there[i], send_sem=swap_send.at[i], recv_sem=swap_recv.at[i],
            device_id={"nodes": across, "feat": sibling}, device_id_type=MESH)
    def keep(i):
        return pltpu.make_async_copy(moves[i][0], moves[i][1], own_sem.at[i])

    def to_owner(d):
        j = (f + d) % feats
        return pltpu.make_async_remote_copy(
            src_ref=feat_ref.at[:, pl.ds(pl.multiple_of(j * own, own), own)], dst_ref=self_ref.at[f],
            send_sem=row_send.at[d], recv_sem=row_recv.at[d], device_id={"feat": j}, device_id_type=MESH)

    @pl.when(parity != core)
    def _():
        for i in (0, 1):
            swap(i).start()
    @pl.when(parity == core)
    def _():
        for i in (0, 1):
            keep(i).start()
    mine = pltpu.make_async_copy(feat_ref.at[:, pl.ds(pl.multiple_of(f * own, own), own)], self_ref.at[f], own_sem.at[5])
    mine.start()
    @pl.when(parity != core)
    def _():
        for i in (0, 1):
            swap(i).wait_recv()
    @pl.when(parity == core)
    def _():
        for i in (0, 1):
            keep(i).wait()

    def later():
        def narrow(t, carry):
            edge_half[t] = edge_ref[t].astype(jnp.float32).astype(jnp.bfloat16)
            return carry
        lax.fori_loop(0, edge_ref.shape[0], narrow, 0)
        for d in range(1, feats):
            to_owner(d).start()
        @pl.when(parity != core)
        def _():
            for i in (2, 3, 4):
                swap(i).start()
        @pl.when(parity == core)
        def _():
            for i in (2, 3, 4):
                keep(i).start()

    def refs(s, block, relay, b):
        other, dz = block
        c = left if s["region"] == 0 else right
        r = pl.ds(0, cols) if s["half"] is None else pl.ds(s["half"] * (cols // 2), cols // 2)
        if relay:
            return relay_ref.at[dz, r, c]
        return out_ref.at[((b + 2 * other) % xs) * zs + (z + dz) % zs, r, c]

    def copy(i):
        s = sends[i]
        src = refs(s, s["block"], s["relayed"], base)
        wx, wz = WAYS.get(s["way"], (0, 0))
        if s["lands"] == "sibling":
            dst = src
            where = {"feat": sibling}
        else:
            where = {"nodes": peers[s["way"]]}
            if s["lands"] is None:
                dst = refs(s, s["block"], True, base)
            elif s["relayed"]:
                b = (x + wx) % xs
                b = b - b % 2 + core
                dst = relay_dst(s, b)
            else:
                dst = src
        return pltpu.make_async_remote_copy(src_ref=src, dst_ref=dst, send_sem=send_sem.at[i], recv_sem=recv_sem.at[i],
                                            device_id=where, device_id_type=MESH)

    def relay_dst(s, b):
        return refs(s, (1, s["block"][1]), False, b)

    def arrival(i):
        s = sends[i]
        if s["lands"] == "sibling":
            b = x - parity + 1 - core
            dst = refs(s, s["block"], False, b)
            where = {"feat": sibling}
        else:
            where = {"nodes": peers[s["way"]]}
            dst = refs(s, s["block"], True, base) if s["lands"] is None else refs(s, s["lands"], False, base)
        return pltpu.make_async_remote_copy(src_ref=dst, dst_ref=dst, send_sem=send_sem.at[i], recv_sem=recv_sem.at[i],
                                            device_id=where, device_id_type=MESH)

    for n, (what, i) in enumerate(steps):
        if n == steps.index(("wait", next(j for w, j in steps if w == "wait"))) + after:
            later()
        if what == "start":
            copy(i).start()
        else:
            arrival(i).wait_recv()
    for i in range(len(sends)):
        copy(i).wait_send()
    for d in range(1, feats):
        to_owner(d).wait()
    mine.wait()
    @pl.when(parity != core)
    def _():
        for i in range(2):
            swap(i).wait_send()
        for i in (2, 3, 4):
            swap(i).wait()
    @pl.when(parity == core)
    def _():
        for i in (2, 3, 4):
            keep(i).wait()

def gather(feat_t, edge_rows, src_tiles, counts, xs=4, zs=8, feats=8, cut=896, after=0, ahead=2.0, cid=1):
    cols, rows = feat_t.shape
    def seconds(s):
        n = cols * (cut if s["region"] == 0 else rows - cut) * 2 / (1 if s["half"] is None else 2)
        return n / 300e3 if s["way"] == "core" else 2 * n / 94e3
    sends, steps, end = plan_gather(zs, seconds, ahead)
    anywhere = pl.BlockSpec(memory_space=pl.ANY)
    vmem = pl.BlockSpec(memory_space=pltpu.VMEM)
    dma = pltpu.SemaphoreType.DMA
    shape = jax.ShapeDtypeStruct
    return pl.pallas_call(
        functools.partial(gather_kernel, xs=xs, zs=zs, cut=cut, sends=sends, steps=steps, after=after),
        out_shape=(shape((xs * zs, cols, rows), feat_t.dtype),
                   shape((feats, cols, rows // feats), feat_t.dtype), shape(edge_rows.shape, jnp.bfloat16),
                   shape(src_tiles.shape, src_tiles.dtype), shape(counts.shape, counts.dtype)),
        in_specs=[vmem, vmem, anywhere, anywhere],
        out_specs=(vmem,) * 3 + (anywhere,) * 2,
        scratch_shapes=[pltpu.VMEM((zs, cols, rows), feat_t.dtype), pltpu.VMEM(edge_rows.shape, jnp.bfloat16),
                        dma((len(sends),)), dma((len(sends),)), dma((feats,)), dma((feats,)), dma((5,)), dma((5,)), dma((7,))],
        compiler_params=pltpu.CompilerParams(collective_id=cid, has_side_effects=True, vmem_limit_bytes=24 * 2**20),
    )(feat_t, edge_rows, src_tiles, counts)

def layer_kernel(feat_ref, agg_ref, self_ref, ws_ref, wn_ref, cot_ref, act_ref, wg_ref,
                 rows_buf, lhs, base, left, gz, xout, xbuf, zout, zbuf,
                 a_send, a_recv, y_send, y_recv, x_send, x_recv, z_send, z_recv, s_send, s_recv, *, xs, zs, ys):
    me = lax.axis_index("nodes")
    f = lax.axis_index("feat")
    x, z = me // zs, me % zs
    y, core = f // 2, f % 2
    feats = 2 * ys
    cols = feat_ref.shape[0]
    own = cot_ref.shape[0]
    hidden = ws_ref.shape[1]
    chunks = hidden // 256
    half = hidden // 2

    def remote(src, dst, send, recv, **where):
        return pltpu.make_async_remote_copy(src_ref=src, dst_ref=dst, send_sem=send, recv_sem=recv,
                                            device_id=where, device_id_type=MESH)

    parity = x % 2
    pair = x - parity
    across = (pair + 1 - parity) * zs + z
    shard = 2 * y + parity

    barrier = pltpu.get_barrier_semaphore()
    for d in range(feats):
        j = (f + d) % feats
        if d:
            pl.semaphore_signal(barrier, inc=1, device_id={"feat": j}, device_id_type=MESH)
        pl.semaphore_signal(barrier, inc=1, device_id={"nodes": across, "feat": j}, device_id_type=MESH)
    for other in (x + 2, x + xs - 1 + 2 * parity):
        pl.semaphore_signal(barrier, inc=1, device_id={"nodes": (other % xs) * zs + z}, device_id_type=MESH)
    for d in range(1, zs):
        pl.semaphore_signal(barrier, inc=1, device_id={"nodes": x * zs + (z + d) % zs}, device_id_type=MESH)
    pl.semaphore_wait(barrier, 2 * feats - 1 + 2 + zs - 1)

    def to_owner(d):
        j = (f + d) % feats
        return remote(agg_ref.at[:, pl.ds(pl.multiple_of(j * own, own), own)], rows_buf.at[shard],
                      a_send.at[d], a_recv.at[shard], nodes=(pair + core) * zs + z, feat=j)
    def from_shard(i):
        return remote(rows_buf.at[i], rows_buf.at[i], a_send.at[0], a_recv.at[i],
                      nodes=(pair + i % 2) * zs + z, feat=i - i % 2 + parity)
    def swap():
        return remote(agg_ref, left.at[pl.ds(cols, cols)], s_send, s_recv, nodes=across, feat=f + 1 - 2 * core)
    for d in range(1, feats):
        to_owner(d).start()
    @pl.when(parity != core)
    def _():
        to_owner(0).start()
    @pl.when(parity == core)
    def _():
        rows_buf[f] = agg_ref[:, pl.ds(pl.multiple_of(f * own, own), own)]
        left[cols:, :] = agg_ref[...]
    left[0:cols, :] = feat_ref[...]
    lhs[...] = self_ref[...].reshape(feats * cols, own).T
    base[...] = jnp.dot(lhs[...], ws_ref[...], preferred_element_type=jnp.float32)
    for d in range(feats):
        i = (f + d) % feats
        if d:
            from_shard(i).wait_recv()
        else:
            @pl.when(parity != core)
            def _():
                from_shard(i).wait_recv()
    @pl.when(parity != core)
    def _():
        swap().start()
    lhs[...] = rows_buf[...].reshape(feats * cols, own).T

    up, down = (y + 1) % ys, (y + ys - 1) % ys
    far = (y + 2) % ys
    sibling = 2 * y + 1 - core
    hrows = own // 2
    def spread(c, k):
        by = (y, y, y, down, up, down, up, far, far)[k]
        to = (sibling, 2 * up + core, 2 * down + core, 2 * up + core, 2 * down + core) + (sibling,) * 4
        r = {3: pl.ds(0, hrows), 4: pl.ds(hrows, hrows), 7: pl.ds(0, hrows), 8: pl.ds(hrows, hrows)}.get(k, pl.ds(0, own))
        ref = gz.at[c, 2 * by + core, r]
        return remote(ref, ref, y_send.at[c, k], y_recv.at[c, k], feat=to[k])

    def columns(ref, c):
        return jnp.concatenate([ref[:, pl.ds(pl.multiple_of(c * 128, 128), 128)],
                                ref[:, pl.ds(pl.multiple_of(half + c * 128, 128), 128)]], axis=1)

    def layer(c, carry):
        v = columns(base, c) + jnp.dot(lhs[...], columns(wn_ref, c), preferred_element_type=jnp.float32)
        s = math.sqrt(2 / math.pi)
        v2 = v * v
        t = jnp.tanh(s * (v + 0.044715 * (v2 * v)))
        cdf = 0.5 * (1.0 + t)
        out = (v * cdf).astype(jnp.bfloat16)
        act_ref[:, pl.ds(pl.multiple_of(c * 128, 128), 128)] = out[:, :128]
        act_ref[:, pl.ds(pl.multiple_of(half + c * 128, 128), 128)] = out[:, 128:]
        slope = cdf + (0.5 * s) * v * (1.0 - t * t) * (1.0 + (3 * 0.044715) * v2)
        gz[c, f] = (columns(cot_ref, c).astype(jnp.float32) * slope).astype(jnp.bfloat16)
        for k in (1, 2, 0):
            spread(c, k).start()
        return carry
    lax.fori_loop(0, 2, layer, 0)

    def xcopy(c, d):
        to = (x + d) % xs
        return remote(xout.at[c, to], xbuf.at[c, d], x_send.at[c, d], x_recv.at[c, d], nodes=to * zs + z)
    def zcopy(c, p, zto):
        return remote(zout.at[c, p], zbuf.at[z], z_send.at[c, p], z_recv.at[z], nodes=x * zs + zto)

    def relay(c, carry):
        spread(c, 1).wait_recv()
        spread(c, 3).start()
        spread(c, 5).start()
        spread(c, 2).wait_recv()
        spread(c, 4).start()
        spread(c, 6).start()
        return carry
    def terms(c, carry):
        for k in (3, 4):
            spread(c, k).wait_recv()
            spread(c, k + 4).start()
        for k in (0, 5, 6, 7, 8):
            spread(c, k).wait_recv()
        g = gz[c].reshape(feats * own, 256)
        term = jnp.dot(left[...], g, preferred_element_type=jnp.float32)
        for q in range(4):
            piece = term[(q // 2) * cols:(q // 2 + 1) * cols, (q % 2) * 128:(q % 2) * 128 + 128]
            xout[c, q] = piece
        for d in range(1, xs):
            xcopy(c, d).start()
        return carry
    def sums(c, carry):
        for d in range(1, xs):
            xcopy(c, d).wait_recv()
        total = xout[c, x] + xbuf[c, 1] + xbuf[c, 2] + xbuf[c, 3]
        total = jnp.concatenate([total, jnp.zeros((128 - cols, 128), jnp.float32)], axis=0).T
        for p in range(2):
            zto = 2 * c + p
            zout[c, p] = total[64 * p:64 * p + 64]
            @pl.when(zto != z)
            def _():
                zcopy(c, p, zto).start()
            @pl.when(zto == z)
            def _():
                zbuf[z] = total[64 * p:64 * p + 64]
        return carry
    def stage(s, carry):
        @pl.when(s < chunks)
        def _():
            relay(s, 0)
        @pl.when(s < chunks - 2)
        def _():
            layer(s + 2, 0)
        @pl.when((s >= 1) & (s <= chunks))
        def _():
            terms(s - 1, 0)
        @pl.when(s >= 2)
        def _():
            sums(s - 2, 0)
        return carry
    @pl.when(parity != core)
    def _():
        swap().wait_recv()
    lax.fori_loop(0, chunks + 2, stage, 0)
    def arrived(i, carry):
        @pl.when(i != z)
        def _():
            remote(zout.at[0, 0], zbuf.at[i], z_send.at[0, 0], z_recv.at[i], nodes=x * zs + i).wait_recv()
        return carry
    lax.fori_loop(0, zs, arrived, 0)
    wg_ref[...] = jnp.sum(zbuf[...], axis=0)[:, :cols]

    def finish(c, carry):
        for k in range(9):
            spread(c, k).wait_send()
        for d in range(1, xs):
            xcopy(c, d).wait_send()
        for p in range(2):
            @pl.when(2 * c + p != z)
            def _():
                zcopy(c, p, 2 * c + p).wait_send()
        return carry
    lax.fori_loop(0, chunks, finish, 0)
    for d in range(1, feats):
        to_owner(d).wait_send()
    @pl.when(parity != core)
    def _():
        to_owner(0).wait_send()
        swap().wait_send()

def layer(feat_t, agg_t, self_rows, w_self, w_neigh, cot, xs=4, zs=8, ys=4, cid=2):
    cols, rows = feat_t.shape
    own, hidden = cot.shape
    feats, chunks = 2 * ys, hidden // 256
    v = pl.BlockSpec(memory_space=pltpu.VMEM)
    dma = pltpu.SemaphoreType.DMA
    f32, bf16 = jnp.float32, jnp.bfloat16
    return pl.pallas_call(
        functools.partial(layer_kernel, xs=xs, zs=zs, ys=ys),
        out_shape=(jax.ShapeDtypeStruct((own, hidden), bf16), jax.ShapeDtypeStruct((hidden // (xs * zs) * 2, cols), f32)),
        in_specs=[v] * 6,
        out_specs=(v, v),
        scratch_shapes=[
            pltpu.VMEM((feats, cols, own), bf16), pltpu.VMEM((own, feats * cols), bf16), pltpu.VMEM((own, hidden), f32),
            pltpu.VMEM((2 * cols, rows), bf16), pltpu.VMEM((chunks, feats, own, 256), bf16),
            pltpu.VMEM((chunks, 4, cols, 128), f32), pltpu.VMEM((chunks, xs, cols, 128), f32),
            pltpu.VMEM((chunks, 2, 64, 128), f32), pltpu.VMEM((zs, 64, 128), f32),
            dma((feats,)), dma((feats,)), dma((chunks, 9)), dma((chunks, 9)),
            dma((chunks, xs)), dma((chunks, xs)), dma((chunks, 2)), dma((zs,)), dma, dma,
        ],
        compiler_params=pltpu.CompilerParams(collective_id=cid, has_side_effects=True, vmem_limit_bytes=48 * 2**20),
    )(feat_t, agg_t, self_rows, w_self, w_neigh, cot)


def agg_kernel(src_ref, count_ref, rows_ref, g_ref, out_ref, picks_ref):
    tiles, slots, span = rows_ref.shape
    cols = g_ref.shape[1]
    per_block = g_ref.shape[2] // span
    iota = lax.broadcasted_iota(jnp.int32, (span, span), 0).astype(jnp.float32).astype(jnp.bfloat16)
    one = jnp.ones((span, span), jnp.bfloat16)
    zero = jnp.zeros((span, span), jnp.bfloat16)
    slot_ids = lax.broadcasted_iota(jnp.int32, (slots, span), 0)
    def tile(t, carry):
        used = count_ref[t]
        picks_ref[...] = jnp.where(slot_ids < used, rows_ref[t].astype(jnp.float32), -1.0)

        def step(i, acc):
            onehots, blocks = [], []
            for u in range(UNROLL):
                k = i * UNROLL + u
                pick = jnp.broadcast_to(picks_ref[pl.ds(k, 1), :], (16, span)).astype(jnp.bfloat16)
                pick = jnp.concatenate([pick] * (span // 16), axis=0)
                onehots.append(jnp.where(pick == iota, one, zero))
                s = src_ref[t, k]
                start = pl.multiple_of((s % per_block) * span, span)
                blocks.append(g_ref[s // per_block, :, pl.ds(start, span)])
            return acc + jnp.dot(
                jnp.concatenate(blocks, axis=1),
                jnp.concatenate(onehots, axis=0),
                preferred_element_type=jnp.float32,
            )

        total = lax.fori_loop(0, (used + UNROLL - 1) // UNROLL, step, jnp.zeros((cols, span), jnp.float32))
        mean = total / used.astype(jnp.float32)
        out_ref[:, pl.ds(pl.multiple_of(t * span, span), span)] = mean.astype(jnp.bfloat16)
        return carry

    lax.fori_loop(0, tiles, tile, 0)


def neighbour_mean(src_tiles, counts, edge_rows, gathered):
    tiles, slots, span = edge_rows.shape
    cols = gathered.shape[1]
    smem = pl.BlockSpec(memory_space=pltpu.SMEM)
    vmem = pl.BlockSpec(memory_space=pltpu.VMEM)
    return pl.pallas_call(
        agg_kernel,
        out_shape=jax.ShapeDtypeStruct((cols, tiles * span), jnp.bfloat16),
        in_specs=[smem, smem, vmem, vmem],
        out_specs=pl.BlockSpec(memory_space=pltpu.VMEM),
        scratch_shapes=[pltpu.VMEM((slots, span), jnp.float32)],
        compiler_params=pltpu.CompilerParams(vmem_limit_bytes=24 * 2**20),
    )(src_tiles, counts, edge_rows, gathered)


def per_device(features, w_self, w_neigh, src_tiles, counts, edge_rows, cotangent):
    feat_t = features.T
    gathered, self_rows, edge_rows, src_tiles, counts = gather(feat_t, edge_rows, src_tiles, counts)
    agg_t = neighbour_mean(src_tiles, counts, edge_rows, gathered)
    activations, grads_t = layer(feat_t, agg_t, self_rows, w_self, w_neigh, cotangent)
    return activations, grads_t.T


def solution(mesh):
    in_specs = (
        P("nodes", "feat"),
        P(),
        P(),
        P("nodes", None),
        P("nodes"),
        P("nodes", None, None),
        P(("nodes", "feat"), None),
    )
    out_specs = (P(("nodes", "feat"), None), P("feat", "nodes"))
    return jax.shard_map(
        per_device, mesh=mesh, in_specs=in_specs, out_specs=out_specs, check_vma=False
    )
```

```python
import functools
import math

import jax
import jax.numpy as jnp
from jax import lax
from jax.experimental import pallas as pl
from jax.experimental.pallas import tpu as pltpu
from jax.sharding import PartitionSpec as P

GROUPS = (32, 16, 8)
MESH = pl.DeviceIdType.MESH
WAYS = {"x+": (1, 0), "x-": (-1, 0), "z+": (0, 1), "z-": (0, -1)}

def plan_gather(zs, seconds, ahead=4.0):
    sends, have = [], {}

    def add(way, block, region, half, passing, get):
        deps = [] if passing is None else [passing]
        if passing is None:
            for h in (0, 1) if half is None else (half,):
                deps += have.get((block, region, h), [])
        sends.append(dict(way=way, block=block, region=region, half=half, relayed=passing is not None,
                          lands=get, deps=sorted(set(deps))))
        if get is not None and get != "sibling":
            for h in (0, 1) if half is None else (half,):
                have[(get, region, h)] = [len(sends) - 1]
        return len(sends) - 1

    def along_z(other, region):
        for d in range(1, zs // 2 + 1):
            for way, s in (("z+", 1), ("z-", -1)):
                half = None if d < zs // 2 else (0 if s == 1 else 1)
                add(way, (other, -s * (d - 1) % zs), region, half, None, (other, -s * d % zs))

    def along_x(dz, region):
        for way, half in (("x+", 0), ("x-", 1)):
            first = add(way, (0, dz), region, half, None, None)
            add(way, (0, dz), region, half, first, (1, dz))

    order = [0]
    for d in range(1, zs // 2):
        order += [d, zs - d]
    order += [zs // 2]
    along_x(0, 0)
    along_z(0, 1)
    along_z(0, 0)
    along_z(1, 0)
    for dz in order:
        along_x(dz, 1)
    for other in (0, 1):
        for dz in order:
            for region in (0, 1):
                add("core", (other, dz), region, None, None, "sibling")

    n = len(sends)
    chain = [0] * n
    for i in reversed(range(n)):
        for d in sends[i]["deps"]:
            chain[d] = max(chain[d], chain[i] + 1)
    free, arrive, starts, todo = {}, {}, {}, set(range(n))
    while todo:
        best = None
        for i in todo:
            if all(d in arrive for d in sends[i]["deps"]):
                ready = max([arrive[d] for d in sends[i]["deps"]], default=0.0)
                at = max(ready, free.get(sends[i]["way"], 0.0))
                key = (at, -chain[i], ready, i)
                best = key if best is None else min(best, key)
        at, _, _, i = best
        todo.remove(i)
        starts[i] = at
        free[sends[i]["way"]] = at + seconds(sends[i])
        arrive[i] = at + seconds(sends[i]) + 1.5
    steps, waited = [], set()
    when = {i: max([arrive[d] for d in sends[i]["deps"]] + [starts[i] - ahead]) for i in range(n)}
    for i in sorted(range(n), key=lambda i: (when[i], starts[i], i)):
        for d in sorted(sends[i]["deps"], key=lambda d: arrive[d]):
            if d not in waited:
                waited.add(d)
                steps.append(("wait", d))
        steps.append(("start", i))
    steps += [("wait", d) for d in sorted(range(n), key=lambda d: arrive[d]) if d not in waited]
    return sends, steps, max(arrive.values())

def gather_kernel(feat_ref, edge_ref, src_ref, count_ref, out_ref, self_ref, edge_out, src_out, count_out,
                  relay_ref, edge_half,
                  send_sem, recv_sem, row_send, row_recv, swap_send, swap_recv, own_sem, *, xs, zs, cut, sends, steps, after):
    me = lax.axis_index("nodes")
    f = lax.axis_index("feat")
    feats = lax.axis_size("feat")
    x, z = me // zs, me % zs
    core, parity = f % 2, x % 2
    cols, rows = feat_ref.shape
    own = rows // feats
    sibling = f + 1 - 2 * core
    across = (x + 1 - 2 * parity) * zs + z
    base = (x - parity + core)
    home = base * zs + z
    peers = {w: ((x + dx) % xs) * zs + (z + dz) % zs for w, (dx, dz) in WAYS.items()}

    barrier = pltpu.get_barrier_semaphore()
    for w in peers:
        pl.semaphore_signal(barrier, inc=1, device_id={"nodes": peers[w]}, device_id_type=MESH)
    for d in range(1, feats):
        pl.semaphore_signal(barrier, inc=1, device_id={"feat": (f + d) % feats}, device_id_type=MESH)
    pl.semaphore_signal(barrier, inc=1, device_id={"nodes": across, "feat": sibling}, device_id_type=MESH)
    pl.semaphore_wait(barrier, len(peers) + feats)

    left, right = pl.ds(0, cut), pl.ds(cut, rows - cut)
    moves = ((feat_ref.at[:, left], out_ref.at[home, :, left]), (feat_ref.at[:, right], out_ref.at[home, :, right]),
             (edge_half, edge_out), (src_ref, src_out), (count_ref, count_out))
    theirs = (x + 1 - 2 * parity) - (1 - parity) + (1 - core)
    theirs = theirs * zs + z
    there = (out_ref.at[theirs, :, left], out_ref.at[theirs, :, right], edge_out, src_out, count_out)

    def swap(i):
        return pltpu.make_async_remote_copy(
            src_ref=moves[i][0], dst_ref=there[i], send_sem=swap_send.at[i], recv_sem=swap_recv.at[i],
            device_id={"nodes": across, "feat": sibling}, device_id_type=MESH)
    def keep(i):
        return pltpu.make_async_copy(moves[i][0], moves[i][1], own_sem.at[i])

    def to_owner(d):
        j = (f + d) % feats
        return pltpu.make_async_remote_copy(
            src_ref=feat_ref.at[:, pl.ds(pl.multiple_of(j * own, own), own)], dst_ref=self_ref.at[f],
            send_sem=row_send.at[d], recv_sem=row_recv.at[d], device_id={"feat": j}, device_id_type=MESH)

    @pl.when(parity != core)
    def _():
        for i in (0, 1):
            swap(i).start()
    @pl.when(parity == core)
    def _():
        for i in (0, 1):
            keep(i).start()
    mine = pltpu.make_async_copy(feat_ref.at[:, pl.ds(pl.multiple_of(f * own, own), own)], self_ref.at[f], own_sem.at[5])
    mine.start()
    @pl.when(parity != core)
    def _():
        for i in (0, 1):
            swap(i).wait_recv()
    @pl.when(parity == core)
    def _():
        for i in (0, 1):
            keep(i).wait()

    def later():
        def narrow(t, carry):
            edge_half[t] = edge_ref[t].astype(jnp.float32).astype(jnp.bfloat16)
            return carry
        lax.fori_loop(0, edge_ref.shape[0], narrow, 0)
        for d in range(1, feats):
            to_owner(d).start()
        @pl.when(parity != core)
        def _():
            for i in (2, 3, 4):
                swap(i).start()
        @pl.when(parity == core)
        def _():
            for i in (2, 3, 4):
                keep(i).start()

    def refs(s, block, relay, b):
        other, dz = block
        c = left if s["region"] == 0 else right
        r = pl.ds(0, cols) if s["half"] is None else pl.ds(s["half"] * (cols // 2), cols // 2)
        if relay:
            return relay_ref.at[dz, r, c]
        return out_ref.at[((b + 2 * other) % xs) * zs + (z + dz) % zs, r, c]

    def copy(i):
        s = sends[i]
        src = refs(s, s["block"], s["relayed"], base)
        wx, wz = WAYS.get(s["way"], (0, 0))
        if s["lands"] == "sibling":
            dst = src
            where = {"feat": sibling}
        else:
            where = {"nodes": peers[s["way"]]}
            if s["lands"] is None:
                dst = refs(s, s["block"], True, base)
            elif s["relayed"]:
                b = (x + wx) % xs
                b = b - b % 2 + core
                dst = relay_dst(s, b)
            else:
                dst = src
        return pltpu.make_async_remote_copy(src_ref=src, dst_ref=dst, send_sem=send_sem.at[i], recv_sem=recv_sem.at[i],
                                            device_id=where, device_id_type=MESH)

    def relay_dst(s, b):
        return refs(s, (1, s["block"][1]), False, b)

    def arrival(i):
        s = sends[i]
        if s["lands"] == "sibling":
            b = x - parity + 1 - core
            dst = refs(s, s["block"], False, b)
            where = {"feat": sibling}
        else:
            where = {"nodes": peers[s["way"]]}
            dst = refs(s, s["block"], True, base) if s["lands"] is None else refs(s, s["lands"], False, base)
        return pltpu.make_async_remote_copy(src_ref=dst, dst_ref=dst, send_sem=send_sem.at[i], recv_sem=recv_sem.at[i],
                                            device_id=where, device_id_type=MESH)

    for n, (what, i) in enumerate(steps):
        if n == steps.index(("wait", next(j for w, j in steps if w == "wait"))) + after:
            later()
        if what == "start":
            copy(i).start()
        else:
            arrival(i).wait_recv()
    for i in range(len(sends)):
        copy(i).wait_send()
    for d in range(1, feats):
        to_owner(d).wait()
    mine.wait()
    @pl.when(parity != core)
    def _():
        for i in range(2):
            swap(i).wait_send()
        for i in (2, 3, 4):
            swap(i).wait()
    @pl.when(parity == core)
    def _():
        for i in (2, 3, 4):
            keep(i).wait()

def gather(feat_t, edge_rows, src_tiles, counts, xs=4, zs=8, feats=8, cut=896, after=0, ahead=2.0, cid=1):
    cols, rows = feat_t.shape
    def seconds(s):
        n = cols * (cut if s["region"] == 0 else rows - cut) * 2 / (1 if s["half"] is None else 2)
        return n / 300e3 if s["way"] == "core" else 2 * n / 94e3
    sends, steps, end = plan_gather(zs, seconds, ahead)
    anywhere = pl.BlockSpec(memory_space=pl.ANY)
    vmem = pl.BlockSpec(memory_space=pltpu.VMEM)
    dma = pltpu.SemaphoreType.DMA
    shape = jax.ShapeDtypeStruct
    return pl.pallas_call(
        functools.partial(gather_kernel, xs=xs, zs=zs, cut=cut, sends=sends, steps=steps, after=after),
        out_shape=(shape((xs * zs, cols, rows), feat_t.dtype),
                   shape((feats, cols, rows // feats), feat_t.dtype), shape(edge_rows.shape, jnp.bfloat16),
                   shape(src_tiles.shape, src_tiles.dtype), shape(counts.shape, counts.dtype)),
        in_specs=[vmem, vmem, anywhere, anywhere],
        out_specs=(vmem,) * 3 + (anywhere,) * 2,
        scratch_shapes=[pltpu.VMEM((zs, cols, rows), feat_t.dtype), pltpu.VMEM(edge_rows.shape, jnp.bfloat16),
                        dma((len(sends),)), dma((len(sends),)), dma((feats,)), dma((feats,)), dma((5,)), dma((5,)), dma((7,))],
        compiler_params=pltpu.CompilerParams(collective_id=cid, has_side_effects=True, vmem_limit_bytes=24 * 2**20),
    )(feat_t, edge_rows, src_tiles, counts)

def layer_kernel(feat_ref, agg_ref, self_ref, ws_ref, wn_ref, cot_ref, act_ref, wg_ref,
                 rows_buf, lhs, base, left, gz, xout, xbuf, zout, zbuf,
                 a_send, a_recv, y_send, y_recv, x_send, x_recv, z_send, z_recv, s_send, s_recv, *, xs, zs, ys):
    me = lax.axis_index("nodes")
    f = lax.axis_index("feat")
    x, z = me // zs, me % zs
    y, core = f // 2, f % 2
    feats = 2 * ys
    cols = feat_ref.shape[0]
    own = cot_ref.shape[0]
    hidden = ws_ref.shape[1]
    chunks = hidden // 256
    half = hidden // 2

    def remote(src, dst, send, recv, **where):
        return pltpu.make_async_remote_copy(src_ref=src, dst_ref=dst, send_sem=send, recv_sem=recv,
                                            device_id=where, device_id_type=MESH)

    parity = x % 2
    pair = x - parity
    across = (pair + 1 - parity) * zs + z
    shard = 2 * y + parity

    barrier = pltpu.get_barrier_semaphore()
    for d in range(feats):
        j = (f + d) % feats
        if d:
            pl.semaphore_signal(barrier, inc=1, device_id={"feat": j}, device_id_type=MESH)
        pl.semaphore_signal(barrier, inc=1, device_id={"nodes": across, "feat": j}, device_id_type=MESH)
    for other in (x + 2, x + xs - 1 + 2 * parity):
        pl.semaphore_signal(barrier, inc=1, device_id={"nodes": (other % xs) * zs + z}, device_id_type=MESH)
    for d in range(1, zs):
        pl.semaphore_signal(barrier, inc=1, device_id={"nodes": x * zs + (z + d) % zs}, device_id_type=MESH)
    pl.semaphore_wait(barrier, 2 * feats - 1 + 2 + zs - 1)

    def to_owner(d):
        j = (f + d) % feats
        return remote(agg_ref.at[:, pl.ds(pl.multiple_of(j * own, own), own)], rows_buf.at[shard],
                      a_send.at[d], a_recv.at[shard], nodes=(pair + core) * zs + z, feat=j)
    def from_shard(i):
        return remote(rows_buf.at[i], rows_buf.at[i], a_send.at[0], a_recv.at[i],
                      nodes=(pair + i % 2) * zs + z, feat=i - i % 2 + parity)
    def swap():
        return remote(agg_ref, left.at[pl.ds(cols, cols)], s_send, s_recv, nodes=across, feat=f + 1 - 2 * core)
    for d in range(1, feats):
        to_owner(d).start()
    @pl.when(parity != core)
    def _():
        to_owner(0).start()
    @pl.when(parity == core)
    def _():
        rows_buf[f] = agg_ref[:, pl.ds(pl.multiple_of(f * own, own), own)]
        left[cols:, :] = agg_ref[...]
    left[0:cols, :] = feat_ref[...]
    lhs[...] = self_ref[...].reshape(feats * cols, own).T
    base[...] = jnp.dot(lhs[...], ws_ref[...], preferred_element_type=jnp.float32)
    for d in range(feats):
        i = (f + d) % feats
        if d:
            from_shard(i).wait_recv()
        else:
            @pl.when(parity != core)
            def _():
                from_shard(i).wait_recv()
    @pl.when(parity != core)
    def _():
        swap().start()
    lhs[...] = rows_buf[...].reshape(feats * cols, own).T

    up, down = (y + 1) % ys, (y + ys - 1) % ys
    far = (y + 2) % ys
    sibling = 2 * y + 1 - core
    hrows = own // 2
    def spread(c, k):
        by = (y, y, y, down, up, down, up, far, far)[k]
        to = (sibling, 2 * up + core, 2 * down + core, 2 * up + core, 2 * down + core) + (sibling,) * 4
        r = {3: pl.ds(0, hrows), 4: pl.ds(hrows, hrows), 7: pl.ds(0, hrows), 8: pl.ds(hrows, hrows)}.get(k, pl.ds(0, own))
        ref = gz.at[c, 2 * by + core, r]
        return remote(ref, ref, y_send.at[c, k], y_recv.at[c, k], feat=to[k])

    def columns(ref, c):
        return jnp.concatenate([ref[:, pl.ds(pl.multiple_of(c * 128, 128), 128)],
                                ref[:, pl.ds(pl.multiple_of(half + c * 128, 128), 128)]], axis=1)

    def layer(c, carry):
        v = columns(base, c) + jnp.dot(lhs[...], columns(wn_ref, c), preferred_element_type=jnp.float32)
        s = math.sqrt(2 / math.pi)
        v2 = v * v
        t = jnp.tanh(s * (v + 0.044715 * (v2 * v)))
        cdf = 0.5 * (1.0 + t)
        out = (v * cdf).astype(jnp.bfloat16)
        act_ref[:, pl.ds(pl.multiple_of(c * 128, 128), 128)] = out[:, :128]
        act_ref[:, pl.ds(pl.multiple_of(half + c * 128, 128), 128)] = out[:, 128:]
        slope = cdf + (0.5 * s) * v * (1.0 - t * t) * (1.0 + (3 * 0.044715) * v2)
        gz[c, f] = (columns(cot_ref, c).astype(jnp.float32) * slope).astype(jnp.bfloat16)
        for k in (1, 2, 0):
            spread(c, k).start()
        return carry
    lax.fori_loop(0, 2, layer, 0)

    def xcopy(c, d):
        to = (x + d) % xs
        return remote(xout.at[c, to], xbuf.at[c, d], x_send.at[c, d], x_recv.at[c, d], nodes=to * zs + z)
    def zcopy(c, p, zto):
        return remote(zout.at[c, p], zbuf.at[z], z_send.at[c, p], z_recv.at[z], nodes=x * zs + zto)

    def relay(c, carry):
        spread(c, 1).wait_recv()
        spread(c, 3).start()
        spread(c, 5).start()
        spread(c, 2).wait_recv()
        spread(c, 4).start()
        spread(c, 6).start()
        return carry
    def terms(c, carry):
        for k in (3, 4):
            spread(c, k).wait_recv()
            spread(c, k + 4).start()
        for k in (0, 5, 6, 7, 8):
            spread(c, k).wait_recv()
        g = gz[c].reshape(feats * own, 256)
        term = jnp.dot(left[...], g, preferred_element_type=jnp.float32)
        for q in range(4):
            piece = term[(q // 2) * cols:(q // 2 + 1) * cols, (q % 2) * 128:(q % 2) * 128 + 128]
            xout[c, q] = piece
        for d in range(1, xs):
            xcopy(c, d).start()
        return carry
    def sums(c, carry):
        for d in range(1, xs):
            xcopy(c, d).wait_recv()
        total = xout[c, x] + xbuf[c, 1] + xbuf[c, 2] + xbuf[c, 3]
        total = jnp.concatenate([total, jnp.zeros((128 - cols, 128), jnp.float32)], axis=0).T
        for p in range(2):
            zto = 2 * c + p
            zout[c, p] = total[64 * p:64 * p + 64]
            @pl.when(zto != z)
            def _():
                zcopy(c, p, zto).start()
            @pl.when(zto == z)
            def _():
                zbuf[z] = total[64 * p:64 * p + 64]
        return carry
    def stage(s, carry):
        @pl.when(s < chunks)
        def _():
            relay(s, 0)
        @pl.when(s < chunks - 2)
        def _():
            layer(s + 2, 0)
        @pl.when((s >= 1) & (s <= chunks))
        def _():
            terms(s - 1, 0)
        @pl.when(s >= 2)
        def _():
            sums(s - 2, 0)
        return carry
    @pl.when(parity != core)
    def _():
        swap().wait_recv()
    lax.fori_loop(0, chunks + 2, stage, 0)
    def arrived(i, carry):
        @pl.when(i != z)
        def _():
            remote(zout.at[0, 0], zbuf.at[i], z_send.at[0, 0], z_recv.at[i], nodes=x * zs + i).wait_recv()
        return carry
    lax.fori_loop(0, zs, arrived, 0)
    wg_ref[...] = jnp.sum(zbuf[...], axis=0)[:, :cols]

    def finish(c, carry):
        for k in range(9):
            spread(c, k).wait_send()
        for d in range(1, xs):
            xcopy(c, d).wait_send()
        for p in range(2):
            @pl.when(2 * c + p != z)
            def _():
                zcopy(c, p, 2 * c + p).wait_send()
        return carry
    lax.fori_loop(0, chunks, finish, 0)
    for d in range(1, feats):
        to_owner(d).wait_send()
    @pl.when(parity != core)
    def _():
        to_owner(0).wait_send()
        swap().wait_send()

def layer(feat_t, agg_t, self_rows, w_self, w_neigh, cot, xs=4, zs=8, ys=4, cid=2):
    cols, rows = feat_t.shape
    own, hidden = cot.shape
    feats, chunks = 2 * ys, hidden // 256
    v = pl.BlockSpec(memory_space=pltpu.VMEM)
    dma = pltpu.SemaphoreType.DMA
    f32, bf16 = jnp.float32, jnp.bfloat16
    return pl.pallas_call(
        functools.partial(layer_kernel, xs=xs, zs=zs, ys=ys),
        out_shape=(jax.ShapeDtypeStruct((own, hidden), bf16), jax.ShapeDtypeStruct((hidden // (xs * zs) * 2, cols), f32)),
        in_specs=[v] * 6,
        out_specs=(v, v),
        scratch_shapes=[
            pltpu.VMEM((feats, cols, own), bf16), pltpu.VMEM((own, feats * cols), bf16), pltpu.VMEM((own, hidden), f32),
            pltpu.VMEM((2 * cols, rows), bf16), pltpu.VMEM((chunks, feats, own, 256), bf16),
            pltpu.VMEM((chunks, 4, cols, 128), f32), pltpu.VMEM((chunks, xs, cols, 128), f32),
            pltpu.VMEM((chunks, 2, 64, 128), f32), pltpu.VMEM((zs, 64, 128), f32),
            dma((feats,)), dma((feats,)), dma((chunks, 9)), dma((chunks, 9)),
            dma((chunks, xs)), dma((chunks, xs)), dma((chunks, 2)), dma((zs,)), dma, dma,
        ],
        compiler_params=pltpu.CompilerParams(collective_id=cid, has_side_effects=True, vmem_limit_bytes=48 * 2**20),
    )(feat_t, agg_t, self_rows, w_self, w_neigh, cot)


def agg_kernel(src_ref, count_ref, rows_ref, g_ref, out_ref, picks_ref, *, groups):
    tiles, slots, span = rows_ref.shape
    cols = g_ref.shape[1]
    per_block = g_ref.shape[2] // span
    iota = lax.broadcasted_iota(jnp.int32, (span, span), 0).astype(jnp.float32).astype(jnp.bfloat16)
    one = jnp.ones((span, span), jnp.bfloat16)
    zero = jnp.zeros((span, span), jnp.bfloat16)
    slot_ids = lax.broadcasted_iota(jnp.int32, (slots, span), 0)

    def tile(t, carry):
        used = count_ref[t]
        picks_ref[...] = jnp.where(slot_ids < used, rows_ref[t].astype(jnp.float32), -1.0)

        def slot_group(first, size, acc):
            onehots, blocks = [], []
            for u in range(size):
                k = first + u
                pick = jnp.broadcast_to(picks_ref[pl.ds(k, 1), :], (16, span)).astype(jnp.bfloat16)
                pick = jnp.concatenate([pick] * (span // 16), axis=0)
                onehots.append(jnp.where(pick == iota, one, zero))
                s = src_ref[t, k]
                start = pl.multiple_of((s % per_block) * span, span)
                blocks.append(g_ref[s // per_block, :, pl.ds(start, span)])
            return acc + jnp.dot(
                jnp.concatenate(blocks, axis=1),
                jnp.concatenate(onehots, axis=0),
                preferred_element_type=jnp.float32,
            )

        total, first = jnp.zeros((cols, span), jnp.float32), 0
        for size in groups:
            left = used - first
            trips = (left + size - 1) // size if size == groups[-1] else left // size
            total = lax.fori_loop(0, trips, lambda i, acc, first=first, size=size: slot_group(first + i * size, size, acc), total)
            first = first + trips * size
        mean = total / used.astype(jnp.float32)
        out_ref[:, pl.ds(pl.multiple_of(t * span, span), span)] = mean.astype(jnp.bfloat16)
        return carry

    lax.fori_loop(0, tiles, tile, 0)


def neighbour_mean(src_tiles, counts, edge_rows, gathered):
    tiles, slots, span = edge_rows.shape
    cols = gathered.shape[1]
    smem = pl.BlockSpec(memory_space=pltpu.SMEM)
    vmem = pl.BlockSpec(memory_space=pltpu.VMEM)
    return pl.pallas_call(
        functools.partial(agg_kernel, groups=GROUPS),
        out_shape=jax.ShapeDtypeStruct((cols, tiles * span), jnp.bfloat16),
        in_specs=[smem, smem, vmem, vmem],
        out_specs=pl.BlockSpec(memory_space=pltpu.VMEM),
        scratch_shapes=[pltpu.VMEM((slots, span), jnp.float32)],
        compiler_params=pltpu.CompilerParams(vmem_limit_bytes=24 * 2**20),
    )(src_tiles, counts, edge_rows, gathered)


def per_device(features, w_self, w_neigh, src_tiles, counts, edge_rows, cotangent):
    feat_t = features.T
    gathered, self_rows, edge_rows, src_tiles, counts = gather(feat_t, edge_rows, src_tiles, counts)
    agg_t = neighbour_mean(src_tiles, counts, edge_rows, gathered)
    activations, grads_t = layer(feat_t, agg_t, self_rows, w_self, w_neigh, cotangent)
    return activations, grads_t.T


def solution(mesh):
    in_specs = (
        P("nodes", "feat"),
        P(),
        P(),
        P("nodes", None),
        P("nodes"),
        P("nodes", None, None),
        P(("nodes", "feat"), None),
    )
    out_specs = (P(("nodes", "feat"), None), P("feat", "nodes"))
    return jax.shard_map(
        per_device, mesh=mesh, in_specs=in_specs, out_specs=out_specs, check_vma=False
    )
```

```python
import functools
import math

import jax
import jax.numpy as jnp
from jax import lax
from jax.experimental import pallas as pl
from jax.experimental.pallas import tpu as pltpu
from jax.sharding import PartitionSpec as P

GROUPS = (32, 16, 8)
MESH = pl.DeviceIdType.MESH
WAYS = {"x+": (1, 0), "x-": (-1, 0), "z+": (0, 1), "z-": (0, -1)}

def plan_gather(zs, seconds, ahead=4.0):
    sends, have = [], {}

    def add(way, block, region, half, passing, get):
        deps = [] if passing is None else [passing]
        if passing is None:
            for h in (0, 1) if half is None else (half,):
                deps += have.get((block, region, h), [])
        sends.append(dict(way=way, block=block, region=region, half=half, relayed=passing is not None,
                          lands=get, deps=sorted(set(deps))))
        if get is not None and get != "sibling":
            for h in (0, 1) if half is None else (half,):
                have[(get, region, h)] = [len(sends) - 1]
        return len(sends) - 1

    def along_z(other, region):
        for d in range(1, zs // 2 + 1):
            for way, s in (("z+", 1), ("z-", -1)):
                half = None if d < zs // 2 else (0 if s == 1 else 1)
                add(way, (other, -s * (d - 1) % zs), region, half, None, (other, -s * d % zs))

    def along_x(dz, region):
        for way, half in (("x+", 0), ("x-", 1)):
            first = add(way, (0, dz), region, half, None, None)
            add(way, (0, dz), region, half, first, (1, dz))

    order = [0]
    for d in range(1, zs // 2):
        order += [d, zs - d]
    order += [zs // 2]
    along_x(0, 0)
    along_z(0, 1)
    along_z(0, 0)
    along_z(1, 0)
    for dz in order:
        along_x(dz, 1)
    for other in (0, 1):
        for dz in order:
            for region in (0, 1):
                add("core", (other, dz), region, None, None, "sibling")

    n = len(sends)
    chain = [0] * n
    for i in reversed(range(n)):
        for d in sends[i]["deps"]:
            chain[d] = max(chain[d], chain[i] + 1)
    free, arrive, starts, todo = {}, {}, {}, set(range(n))
    while todo:
        best = None
        for i in todo:
            if all(d in arrive for d in sends[i]["deps"]):
                ready = max([arrive[d] for d in sends[i]["deps"]], default=0.0)
                at = max(ready, free.get(sends[i]["way"], 0.0))
                key = (at, -chain[i], ready, i)
                best = key if best is None else min(best, key)
        at, _, _, i = best
        todo.remove(i)
        starts[i] = at
        free[sends[i]["way"]] = at + seconds(sends[i])
        arrive[i] = at + seconds(sends[i]) + 1.5
    steps, waited = [], set()
    when = {i: max([arrive[d] for d in sends[i]["deps"]] + [starts[i] - ahead]) for i in range(n)}
    for i in sorted(range(n), key=lambda i: (when[i], starts[i], i)):
        for d in sorted(sends[i]["deps"], key=lambda d: arrive[d]):
            if d not in waited:
                waited.add(d)
                steps.append(("wait", d))
        steps.append(("start", i))
    steps += [("wait", d) for d in sorted(range(n), key=lambda d: arrive[d]) if d not in waited]
    return sends, steps, max(arrive.values())

def gather_kernel(feat_ref, edge_ref, src_ref, count_ref, out_ref, self_ref, edge_out, src_out, count_out,
                  relay_ref, edge_half,
                  send_sem, recv_sem, row_send, row_recv, swap_send, swap_recv, edge_send, edge_recv, own_sem, *, xs, zs, cut, sends, steps, after):
    me = lax.axis_index("nodes")
    f = lax.axis_index("feat")
    feats = lax.axis_size("feat")
    x, z = me // zs, me % zs
    core, parity = f % 2, x % 2
    cols, rows = feat_ref.shape
    own = rows // feats
    sibling = f + 1 - 2 * core
    across = (x + 1 - 2 * parity) * zs + z
    base = (x - parity + core)
    home = base * zs + z
    peers = {w: ((x + dx) % xs) * zs + (z + dz) % zs for w, (dx, dz) in WAYS.items()}

    barrier = pltpu.get_barrier_semaphore()
    for w in peers:
        pl.semaphore_signal(barrier, inc=1, device_id={"nodes": peers[w]}, device_id_type=MESH)
    for d in range(1, feats):
        pl.semaphore_signal(barrier, inc=1, device_id={"feat": (f + d) % feats}, device_id_type=MESH)
    pl.semaphore_signal(barrier, inc=1, device_id={"nodes": across, "feat": sibling}, device_id_type=MESH)
    pl.semaphore_wait(barrier, len(peers) + feats)

    left, right = pl.ds(0, cut), pl.ds(cut, rows - cut)
    moves = ((feat_ref.at[:, left], out_ref.at[home, :, left]), (feat_ref.at[:, right], out_ref.at[home, :, right]),
             (edge_half, edge_out), (src_ref, src_out), (count_ref, count_out))
    theirs = (x + 1 - 2 * parity) - (1 - parity) + (1 - core)
    theirs = theirs * zs + z
    there = (out_ref.at[theirs, :, left], out_ref.at[theirs, :, right], edge_out, src_out, count_out)

    def swap(i):
        return pltpu.make_async_remote_copy(
            src_ref=moves[i][0], dst_ref=there[i], send_sem=swap_send.at[i], recv_sem=swap_recv.at[i],
            device_id={"nodes": across, "feat": sibling}, device_id_type=MESH)
    y, shares = f // 2, feats // 2
    part = edge_ref.shape[0] // shares
    def share(n):
        return pl.ds(n * part, part)
    def across_edges():
        return pltpu.make_async_remote_copy(
            src_ref=edge_half.at[share(y)], dst_ref=edge_out.at[share(y)], send_sem=edge_send.at[0], recv_sem=edge_recv.at[0],
            device_id={"nodes": across, "feat": sibling}, device_id_type=MESH)
    def along_y(d, owner):
        return pltpu.make_async_remote_copy(
            src_ref=edge_out.at[share(owner)], dst_ref=edge_out.at[share(owner)], send_sem=edge_send.at[d],
            recv_sem=edge_recv.at[d], device_id={"feat": (f + 2 * d) % feats}, device_id_type=MESH)
    def keep(i):
        return pltpu.make_async_copy(moves[i][0], moves[i][1], own_sem.at[i])

    def to_owner(d):
        j = (f + d) % feats
        return pltpu.make_async_remote_copy(
            src_ref=feat_ref.at[:, pl.ds(pl.multiple_of(j * own, own), own)], dst_ref=self_ref.at[f],
            send_sem=row_send.at[d], recv_sem=row_recv.at[d], device_id={"feat": j}, device_id_type=MESH)

    @pl.when(parity != core)
    def _():
        for i in (0, 1):
            swap(i).start()
    @pl.when(parity == core)
    def _():
        for i in (0, 1):
            keep(i).start()
    mine = pltpu.make_async_copy(feat_ref.at[:, pl.ds(pl.multiple_of(f * own, own), own)], self_ref.at[f], own_sem.at[5])
    mine.start()
    @pl.when(parity != core)
    def _():
        for i in (0, 1):
            swap(i).wait_recv()
    @pl.when(parity == core)
    def _():
        for i in (0, 1):
            keep(i).wait()

    def later():
        def narrow(t, carry):
            edge_half[t] = edge_ref[t].astype(jnp.float32).astype(jnp.bfloat16)
            return carry
        lax.fori_loop(0, edge_ref.shape[0], narrow, 0)
        for d in range(1, feats):
            to_owner(d).start()
        @pl.when(parity != core)
        def _():
            across_edges().start()
            for i in (3, 4):
                swap(i).start()
        @pl.when(parity == core)
        def _():
            for i in (2, 3, 4):
                keep(i).start()

    def latest():
        @pl.when(parity != core)
        def _():
            across_edges().wait_recv()
            for d in range(1, shares):
                along_y(d, y).start()

    def refs(s, block, relay, b):
        other, dz = block
        c = left if s["region"] == 0 else right
        r = pl.ds(0, cols) if s["half"] is None else pl.ds(s["half"] * (cols // 2), cols // 2)
        if relay:
            return relay_ref.at[dz, r, c]
        return out_ref.at[((b + 2 * other) % xs) * zs + (z + dz) % zs, r, c]

    def copy(i):
        s = sends[i]
        src = refs(s, s["block"], s["relayed"], base)
        wx, wz = WAYS.get(s["way"], (0, 0))
        if s["lands"] == "sibling":
            dst = src
            where = {"feat": sibling}
        else:
            where = {"nodes": peers[s["way"]]}
            if s["lands"] is None:
                dst = refs(s, s["block"], True, base)
            elif s["relayed"]:
                b = (x + wx) % xs
                b = b - b % 2 + core
                dst = relay_dst(s, b)
            else:
                dst = src
        return pltpu.make_async_remote_copy(src_ref=src, dst_ref=dst, send_sem=send_sem.at[i], recv_sem=recv_sem.at[i],
                                            device_id=where, device_id_type=MESH)

    def relay_dst(s, b):
        return refs(s, (1, s["block"][1]), False, b)

    def arrival(i):
        s = sends[i]
        if s["lands"] == "sibling":
            b = x - parity + 1 - core
            dst = refs(s, s["block"], False, b)
            where = {"feat": sibling}
        else:
            where = {"nodes": peers[s["way"]]}
            dst = refs(s, s["block"], True, base) if s["lands"] is None else refs(s, s["lands"], False, base)
        return pltpu.make_async_remote_copy(src_ref=dst, dst_ref=dst, send_sem=send_sem.at[i], recv_sem=recv_sem.at[i],
                                            device_id=where, device_id_type=MESH)

    for n, (what, i) in enumerate(steps):
        if n == steps.index(("wait", next(j for w, j in steps if w == "wait"))) + after:
            later()
        if n == len(steps) // 3:
            latest()
        if what == "start":
            copy(i).start()
        else:
            arrival(i).wait_recv()
    for i in range(len(sends)):
        copy(i).wait_send()
    for d in range(1, feats):
        to_owner(d).wait()
    mine.wait()
    @pl.when(parity != core)
    def _():
        for i in range(2):
            swap(i).wait_send()
        for i in (3, 4):
            swap(i).wait()
        across_edges().wait_send()
        for d in range(1, shares):
            along_y(d, y).wait_send()
            along_y(d, (y + shares - d) % shares).wait_recv()
    @pl.when(parity == core)
    def _():
        for i in (2, 3, 4):
            keep(i).wait()

def gather(feat_t, edge_rows, src_tiles, counts, xs=4, zs=8, feats=8, cut=896, after=0, ahead=2.0, cid=1):
    cols, rows = feat_t.shape
    def seconds(s):
        n = cols * (cut if s["region"] == 0 else rows - cut) * 2 / (1 if s["half"] is None else 2)
        return n / 300e3 if s["way"] == "core" else 2 * n / 94e3
    sends, steps, end = plan_gather(zs, seconds, ahead)
    anywhere = pl.BlockSpec(memory_space=pl.ANY)
    vmem = pl.BlockSpec(memory_space=pltpu.VMEM)
    dma = pltpu.SemaphoreType.DMA
    shape = jax.ShapeDtypeStruct
    return pl.pallas_call(
        functools.partial(gather_kernel, xs=xs, zs=zs, cut=cut, sends=sends, steps=steps, after=after),
        out_shape=(shape((xs * zs, cols, rows), feat_t.dtype),
                   shape((feats, cols, rows // feats), feat_t.dtype), shape(edge_rows.shape, jnp.bfloat16),
                   shape(src_tiles.shape, src_tiles.dtype), shape(counts.shape, counts.dtype)),
        in_specs=[vmem, vmem, anywhere, anywhere],
        out_specs=(vmem,) * 3 + (anywhere,) * 2,
        scratch_shapes=[pltpu.VMEM((zs, cols, rows), feat_t.dtype), pltpu.VMEM(edge_rows.shape, jnp.bfloat16),
                        dma((len(sends),)), dma((len(sends),)), dma((feats,)), dma((feats,)), dma((5,)), dma((5,)), dma((feats // 2,)), dma((feats // 2,)), dma((7,))],
        compiler_params=pltpu.CompilerParams(collective_id=cid, has_side_effects=True, vmem_limit_bytes=24 * 2**20),
    )(feat_t, edge_rows, src_tiles, counts)

def layer_kernel(feat_ref, agg_ref, self_ref, ws_ref, wn_ref, cot_ref, act_ref, wg_ref,
                 rows_buf, swapped, lhs, base, left, gz, xout, xbuf, zout, zbuf,
                 a_send, a_recv, y_send, y_recv, x_send, x_recv, z_send, z_recv, s_send, s_recv, *, xs, zs, ys):
    me = lax.axis_index("nodes")
    f = lax.axis_index("feat")
    x, z = me // zs, me % zs
    y, core = f // 2, f % 2
    feats = 2 * ys
    cols = feat_ref.shape[0]
    own = cot_ref.shape[0]
    hidden = ws_ref.shape[1]
    chunks = hidden // 256
    half = hidden // 2

    def remote(src, dst, send, recv, **where):
        return pltpu.make_async_remote_copy(src_ref=src, dst_ref=dst, send_sem=send, recv_sem=recv,
                                            device_id=where, device_id_type=MESH)

    parity = x % 2
    pair = x - parity
    across = (pair + 1 - parity) * zs + z
    shard = 2 * y + parity

    barrier = pltpu.get_barrier_semaphore()
    for d in range(feats):
        j = (f + d) % feats
        if d:
            pl.semaphore_signal(barrier, inc=1, device_id={"feat": j}, device_id_type=MESH)
        pl.semaphore_signal(barrier, inc=1, device_id={"nodes": across, "feat": j}, device_id_type=MESH)
    for other in (x + 2, x + xs - 1 + 2 * parity):
        pl.semaphore_signal(barrier, inc=1, device_id={"nodes": (other % xs) * zs + z}, device_id_type=MESH)
    for d in range(1, zs):
        pl.semaphore_signal(barrier, inc=1, device_id={"nodes": x * zs + (z + d) % zs}, device_id_type=MESH)
    pl.semaphore_wait(barrier, 2 * feats - 1 + 2 + zs - 1)

    def to_owner(d):
        j = (f + d) % feats
        return remote(agg_ref.at[j], rows_buf.at[shard],
                      a_send.at[d], a_recv.at[shard], nodes=(pair + core) * zs + z, feat=j)
    def from_shard(i):
        return remote(rows_buf.at[i], rows_buf.at[i], a_send.at[0], a_recv.at[i],
                      nodes=(pair + i % 2) * zs + z, feat=i - i % 2 + parity)
    def swap():
        return remote(agg_ref, swapped, s_send, s_recv, nodes=across, feat=f + 1 - 2 * core)
    for d in range(1, feats):
        to_owner(d).start()
    @pl.when(parity != core)
    def _():
        to_owner(0).start()
    @pl.when(parity == core)
    def _():
        rows_buf[f] = agg_ref[f]
        for j in range(feats):
            left[cols:, j * own:(j + 1) * own] = agg_ref[j]
    left[0:cols, :] = feat_ref[...]
    lhs[...] = self_ref[...].reshape(feats * cols, own).T
    base[...] = jnp.dot(lhs[...], ws_ref[...], preferred_element_type=jnp.float32)
    for d in range(feats):
        i = (f + d) % feats
        if d:
            from_shard(i).wait_recv()
        else:
            @pl.when(parity != core)
            def _():
                from_shard(i).wait_recv()
    @pl.when(parity != core)
    def _():
        swap().start()
    lhs[...] = rows_buf[...].reshape(feats * cols, own).T

    up, down = (y + 1) % ys, (y + ys - 1) % ys
    far = (y + 2) % ys
    sibling = 2 * y + 1 - core
    hrows = own // 2
    def spread(c, k):
        by = (y, y, y, down, up, down, up, far, far)[k]
        to = (sibling, 2 * up + core, 2 * down + core, 2 * up + core, 2 * down + core) + (sibling,) * 4
        r = {3: pl.ds(0, hrows), 4: pl.ds(hrows, hrows), 7: pl.ds(0, hrows), 8: pl.ds(hrows, hrows)}.get(k, pl.ds(0, own))
        ref = gz.at[c, 2 * by + core, r]
        return remote(ref, ref, y_send.at[c, k], y_recv.at[c, k], feat=to[k])

    def columns(ref, c):
        return jnp.concatenate([ref[:, pl.ds(pl.multiple_of(c * 128, 128), 128)],
                                ref[:, pl.ds(pl.multiple_of(half + c * 128, 128), 128)]], axis=1)

    def layer(c, carry):
        v = columns(base, c) + jnp.dot(lhs[...], columns(wn_ref, c), preferred_element_type=jnp.float32)
        s = math.sqrt(2 / math.pi)
        v2 = v * v
        t = jnp.tanh(s * (v + 0.044715 * (v2 * v)))
        cdf = 0.5 * (1.0 + t)
        out = (v * cdf).astype(jnp.bfloat16)
        act_ref[:, pl.ds(pl.multiple_of(c * 128, 128), 128)] = out[:, :128]
        act_ref[:, pl.ds(pl.multiple_of(half + c * 128, 128), 128)] = out[:, 128:]
        slope = cdf + (0.5 * s) * v * (1.0 - t * t) * (1.0 + (3 * 0.044715) * v2)
        gz[c, f] = (columns(cot_ref, c).astype(jnp.float32) * slope).astype(jnp.bfloat16)
        for k in (1, 2, 0):
            spread(c, k).start()
        return carry
    lax.fori_loop(0, 2, layer, 0)

    def xcopy(c, d):
        to = (x + d) % xs
        return remote(xout.at[c, to], xbuf.at[c, d], x_send.at[c, d], x_recv.at[c, d], nodes=to * zs + z)
    def zcopy(c, p, zto):
        return remote(zout.at[c, p], zbuf.at[z], z_send.at[c, p], z_recv.at[z], nodes=x * zs + zto)

    def relay(c, carry):
        spread(c, 1).wait_recv()
        spread(c, 3).start()
        spread(c, 5).start()
        spread(c, 2).wait_recv()
        spread(c, 4).start()
        spread(c, 6).start()
        return carry
    def terms(c, carry):
        for k in (3, 4):
            spread(c, k).wait_recv()
            spread(c, k + 4).start()
        for k in (0, 5, 6, 7, 8):
            spread(c, k).wait_recv()
        g = gz[c].reshape(feats * own, 256)
        term = jnp.dot(left[...], g, preferred_element_type=jnp.float32)
        for q in range(4):
            piece = term[(q // 2) * cols:(q // 2 + 1) * cols, (q % 2) * 128:(q % 2) * 128 + 128]
            xout[c, q] = piece
        for d in range(1, xs):
            xcopy(c, d).start()
        return carry
    def sums(c, carry):
        for d in range(1, xs):
            xcopy(c, d).wait_recv()
        total = xout[c, x] + xbuf[c, 1] + xbuf[c, 2] + xbuf[c, 3]
        total = jnp.concatenate([total, jnp.zeros((128 - cols, 128), jnp.float32)], axis=0).T
        for p in range(2):
            zto = 2 * c + p
            zout[c, p] = total[64 * p:64 * p + 64]
            @pl.when(zto != z)
            def _():
                zcopy(c, p, zto).start()
            @pl.when(zto == z)
            def _():
                zbuf[z] = total[64 * p:64 * p + 64]
        return carry
    def stage(s, carry):
        @pl.when(s < chunks)
        def _():
            relay(s, 0)
        @pl.when(s < chunks - 2)
        def _():
            layer(s + 2, 0)
        @pl.when((s >= 1) & (s <= chunks))
        def _():
            terms(s - 1, 0)
        @pl.when(s >= 2)
        def _():
            sums(s - 2, 0)
        return carry
    @pl.when(parity != core)
    def _():
        swap().wait_recv()
        for j in range(feats):
            left[cols:, j * own:(j + 1) * own] = swapped[j]
    lax.fori_loop(0, chunks + 2, stage, 0)
    def arrived(i, carry):
        @pl.when(i != z)
        def _():
            remote(zout.at[0, 0], zbuf.at[i], z_send.at[0, 0], z_recv.at[i], nodes=x * zs + i).wait_recv()
        return carry
    lax.fori_loop(0, zs, arrived, 0)
    wg_ref[...] = jnp.sum(zbuf[...], axis=0)[:, :cols]

    def finish(c, carry):
        for k in range(9):
            spread(c, k).wait_send()
        for d in range(1, xs):
            xcopy(c, d).wait_send()
        for p in range(2):
            @pl.when(2 * c + p != z)
            def _():
                zcopy(c, p, 2 * c + p).wait_send()
        return carry
    lax.fori_loop(0, chunks, finish, 0)
    for d in range(1, feats):
        to_owner(d).wait_send()
    @pl.when(parity != core)
    def _():
        to_owner(0).wait_send()
        swap().wait_send()

def layer(feat_t, agg_t, self_rows, w_self, w_neigh, cot, xs=4, zs=8, ys=4, cid=2):
    cols, rows = feat_t.shape
    own, hidden = cot.shape
    feats, chunks = 2 * ys, hidden // 256
    v = pl.BlockSpec(memory_space=pltpu.VMEM)
    dma = pltpu.SemaphoreType.DMA
    f32, bf16 = jnp.float32, jnp.bfloat16
    return pl.pallas_call(
        functools.partial(layer_kernel, xs=xs, zs=zs, ys=ys),
        out_shape=(jax.ShapeDtypeStruct((own, hidden), bf16), jax.ShapeDtypeStruct((hidden // (xs * zs) * 2, cols), f32)),
        in_specs=[v] * 6,
        out_specs=(v, v),
        scratch_shapes=[
            pltpu.VMEM((feats, cols, own), bf16), pltpu.VMEM((feats, cols, own), bf16), pltpu.VMEM((own, feats * cols), bf16), pltpu.VMEM((own, hidden), f32),
            pltpu.VMEM((2 * cols, rows), bf16), pltpu.VMEM((chunks, feats, own, 256), bf16),
            pltpu.VMEM((chunks, 4, cols, 128), f32), pltpu.VMEM((chunks, xs, cols, 128), f32),
            pltpu.VMEM((chunks, 2, 64, 128), f32), pltpu.VMEM((zs, 64, 128), f32),
            dma((feats,)), dma((feats,)), dma((chunks, 9)), dma((chunks, 9)),
            dma((chunks, xs)), dma((chunks, xs)), dma((chunks, 2)), dma((zs,)), dma, dma,
        ],
        compiler_params=pltpu.CompilerParams(collective_id=cid, has_side_effects=True, vmem_limit_bytes=48 * 2**20),
    )(feat_t, agg_t, self_rows, w_self, w_neigh, cot)


def agg_kernel(src_ref, count_ref, rows_ref, g_ref, out_ref, picks_ref, *, groups):
    tiles, slots, span = rows_ref.shape
    cols = g_ref.shape[1]
    per_block = g_ref.shape[2] // span
    iota = lax.broadcasted_iota(jnp.int32, (span, span), 0).astype(jnp.float32).astype(jnp.bfloat16)
    one = jnp.ones((span, span), jnp.bfloat16)
    zero = jnp.zeros((span, span), jnp.bfloat16)
    slot_ids = lax.broadcasted_iota(jnp.int32, (slots, span), 0)

    def tile(t, carry):
        used = count_ref[t]
        picks_ref[...] = jnp.where(slot_ids < used, rows_ref[t].astype(jnp.float32), -1.0)

        def slot_group(first, size, acc):
            onehots, blocks = [], []
            for u in range(size):
                k = first + u
                pick = jnp.broadcast_to(picks_ref[pl.ds(k, 1), :], (16, span)).astype(jnp.bfloat16)
                pick = jnp.concatenate([pick] * (span // 16), axis=0)
                onehots.append(jnp.where(pick == iota, one, zero))
                s = src_ref[t, k]
                start = pl.multiple_of((s % per_block) * span, span)
                blocks.append(g_ref[s // per_block, :, pl.ds(start, span)])
            return acc + jnp.dot(
                jnp.concatenate(blocks, axis=1),
                jnp.concatenate(onehots, axis=0),
                preferred_element_type=jnp.float32,
            )

        total, first = jnp.zeros((cols, span), jnp.float32), 0
        for size in groups:
            left = used - first
            trips = (left + size - 1) // size if size == groups[-1] else left // size
            total = lax.fori_loop(0, trips, lambda i, acc, first=first, size=size: slot_group(first + i * size, size, acc), total)
            first = first + trips * size
        mean = total / used.astype(jnp.float32)
        out_ref[t] = mean.astype(jnp.bfloat16)
        return carry

    lax.fori_loop(0, tiles, tile, 0)


def neighbour_mean(src_tiles, counts, edge_rows, gathered):
    tiles, slots, span = edge_rows.shape
    cols = gathered.shape[1]
    smem = pl.BlockSpec(memory_space=pltpu.SMEM)
    vmem = pl.BlockSpec(memory_space=pltpu.VMEM)
    return pl.pallas_call(
        functools.partial(agg_kernel, groups=GROUPS),
        out_shape=jax.ShapeDtypeStruct((tiles, cols, span), jnp.bfloat16),
        in_specs=[smem, smem, vmem, vmem],
        out_specs=pl.BlockSpec(memory_space=pltpu.VMEM),
        scratch_shapes=[pltpu.VMEM((slots, span), jnp.float32)],
        compiler_params=pltpu.CompilerParams(vmem_limit_bytes=24 * 2**20),
    )(src_tiles, counts, edge_rows, gathered)


def per_device(features, w_self, w_neigh, src_tiles, counts, edge_rows, cotangent):
    feat_t = features.T
    gathered, self_rows, edge_rows, src_tiles, counts = gather(feat_t, edge_rows, src_tiles, counts)
    agg_t = neighbour_mean(src_tiles, counts, edge_rows, gathered)
    activations, grads_t = layer(feat_t, agg_t, self_rows, w_self, w_neigh, cotangent)
    return activations, grads_t.T


def solution(mesh):
    in_specs = (
        P("nodes", "feat"),
        P(),
        P(),
        P("nodes", None),
        P("nodes"),
        P("nodes", None, None),
        P(("nodes", "feat"), None),
    )
    out_specs = (P(("nodes", "feat"), None), P("feat", "nodes"))
    return jax.shard_map(
        per_device, mesh=mesh, in_specs=in_specs, out_specs=out_specs, check_vma=False
    )
```

```python
import functools
import math

import jax
import jax.numpy as jnp
from jax import lax
from jax.experimental import pallas as pl
from jax.experimental.pallas import tpu as pltpu
from jax.sharding import PartitionSpec as P

GROUPS = (32, 16, 8)
MESH = pl.DeviceIdType.MESH
WAYS = {"x+": (1, 0), "x-": (-1, 0), "z+": (0, 1), "z-": (0, -1)}

def plan_gather(zs, seconds, ahead=4.0):
    sends, have = [], {}

    def add(way, block, region, half, passing, get):
        deps = [] if passing is None else [passing]
        if passing is None:
            for h in (0, 1) if half is None else (half,):
                deps += have.get((block, region, h), [])
        sends.append(dict(way=way, block=block, region=region, half=half, relayed=passing is not None,
                          lands=get, deps=sorted(set(deps))))
        if get is not None and get != "sibling":
            for h in (0, 1) if half is None else (half,):
                have[(get, region, h)] = [len(sends) - 1]
        return len(sends) - 1

    def along_z(other, region):
        for d in range(1, zs // 2 + 1):
            for way, s in (("z+", 1), ("z-", -1)):
                half = None if d < zs // 2 else (0 if s == 1 else 1)
                add(way, (other, -s * (d - 1) % zs), region, half, None, (other, -s * d % zs))

    def along_x(dz, region):
        for way, half in (("x+", 0), ("x-", 1)):
            first = add(way, (0, dz), region, half, None, None)
            add(way, (0, dz), region, half, first, (1, dz))

    order = [0]
    for d in range(1, zs // 2):
        order += [d, zs - d]
    order += [zs // 2]
    along_x(0, 0)
    along_z(0, 1)
    along_z(0, 0)
    along_z(1, 0)
    for dz in order:
        along_x(dz, 1)
    for other in (0, 1):
        for dz in order:
            for region in (0, 1):
                add("core", (other, dz), region, None, None, "sibling")

    n = len(sends)
    chain = [0] * n
    for i in reversed(range(n)):
        for d in sends[i]["deps"]:
            chain[d] = max(chain[d], chain[i] + 1)
    free, arrive, starts, todo = {}, {}, {}, set(range(n))
    while todo:
        best = None
        for i in todo:
            if all(d in arrive for d in sends[i]["deps"]):
                ready = max([arrive[d] for d in sends[i]["deps"]], default=0.0)
                at = max(ready, free.get(sends[i]["way"], 0.0))
                key = (at, -chain[i], ready, i)
                best = key if best is None else min(best, key)
        at, _, _, i = best
        todo.remove(i)
        starts[i] = at
        free[sends[i]["way"]] = at + seconds(sends[i])
        arrive[i] = at + seconds(sends[i]) + 1.5
    steps, waited = [], set()
    when = {i: max([arrive[d] for d in sends[i]["deps"]] + [starts[i] - ahead]) for i in range(n)}
    for i in sorted(range(n), key=lambda i: (when[i], starts[i], i)):
        for d in sorted(sends[i]["deps"], key=lambda d: arrive[d]):
            if d not in waited:
                waited.add(d)
                steps.append(("wait", d))
        steps.append(("start", i))
    steps += [("wait", d) for d in sorted(range(n), key=lambda d: arrive[d]) if d not in waited]
    return sends, steps, max(arrive.values())

def gather_kernel(feat_ref, edge_ref, src_ref, count_ref, out_ref, self_ref, edge_out, src_out, count_out,
                  relay_ref, edge_half,
                  send_sem, recv_sem, row_send, row_recv, swap_send, swap_recv, edge_send, edge_recv, own_sem, *, xs, zs, cut, sends, steps, after):
    me = lax.axis_index("nodes")
    f = lax.axis_index("feat")
    feats = lax.axis_size("feat")
    x, z = me // zs, me % zs
    core, parity = f % 2, x % 2
    cols, rows = feat_ref.shape
    own = rows // feats
    sibling = f + 1 - 2 * core
    across = (x + 1 - 2 * parity) * zs + z
    base = (x - parity + core)
    home = base * zs + z
    peers = {w: ((x + dx) % xs) * zs + (z + dz) % zs for w, (dx, dz) in WAYS.items()}

    barrier = pltpu.get_barrier_semaphore()
    for w in peers:
        pl.semaphore_signal(barrier, inc=1, device_id={"nodes": peers[w]}, device_id_type=MESH)
    for d in range(1, feats):
        pl.semaphore_signal(barrier, inc=1, device_id={"feat": (f + d) % feats}, device_id_type=MESH)
    pl.semaphore_signal(barrier, inc=1, device_id={"nodes": across, "feat": sibling}, device_id_type=MESH)
    pl.semaphore_wait(barrier, len(peers) + feats)

    left, right = pl.ds(0, cut), pl.ds(cut, rows - cut)
    moves = ((feat_ref.at[:, left], out_ref.at[home, :, left]), (feat_ref.at[:, right], out_ref.at[home, :, right]),
             (edge_half, edge_out), (src_ref, src_out), (count_ref, count_out))
    theirs = (x + 1 - 2 * parity) - (1 - parity) + (1 - core)
    theirs = theirs * zs + z
    there = (out_ref.at[theirs, :, left], out_ref.at[theirs, :, right], edge_out, src_out, count_out)

    def swap(i):
        return pltpu.make_async_remote_copy(
            src_ref=moves[i][0], dst_ref=there[i], send_sem=swap_send.at[i], recv_sem=swap_recv.at[i],
            device_id={"nodes": across, "feat": sibling}, device_id_type=MESH)
    y, shares = f // 2, feats // 2
    part = edge_ref.shape[0] // shares
    def share(n):
        return pl.ds(n * part, part)
    def across_edges():
        return pltpu.make_async_remote_copy(
            src_ref=edge_half.at[share(y)], dst_ref=edge_out.at[share(y)], send_sem=edge_send.at[0], recv_sem=edge_recv.at[0],
            device_id={"nodes": across, "feat": sibling}, device_id_type=MESH)
    def along_y(d, owner):
        return pltpu.make_async_remote_copy(
            src_ref=edge_out.at[share(owner)], dst_ref=edge_out.at[share(owner)], send_sem=edge_send.at[d],
            recv_sem=edge_recv.at[d], device_id={"feat": (f + 2 * d) % feats}, device_id_type=MESH)
    def keep(i):
        return pltpu.make_async_copy(moves[i][0], moves[i][1], own_sem.at[i])

    def to_owner(d):
        j = (f + d) % feats
        return pltpu.make_async_remote_copy(
            src_ref=feat_ref.at[:, pl.ds(pl.multiple_of(j * own, own), own)], dst_ref=self_ref.at[f],
            send_sem=row_send.at[d], recv_sem=row_recv.at[d], device_id={"feat": j}, device_id_type=MESH)

    @pl.when(parity != core)
    def _():
        for i in (0, 1):
            swap(i).start()
    @pl.when(parity == core)
    def _():
        for i in (0, 1):
            keep(i).start()
    mine = pltpu.make_async_copy(feat_ref.at[:, pl.ds(pl.multiple_of(f * own, own), own)], self_ref.at[f], own_sem.at[5])
    mine.start()
    @pl.when(parity != core)
    def _():
        for i in (0, 1):
            swap(i).wait_recv()
    @pl.when(parity == core)
    def _():
        for i in (0, 1):
            keep(i).wait()

    def later():
        def narrow(t, carry):
            edge_half[t] = edge_ref[t].astype(jnp.float32).astype(jnp.bfloat16)
            return carry
        lax.fori_loop(0, edge_ref.shape[0], narrow, 0)
        for d in range(1, feats):
            to_owner(d).start()
        @pl.when(parity != core)
        def _():
            across_edges().start()
            for i in (3, 4):
                swap(i).start()
        @pl.when(parity == core)
        def _():
            for i in (2, 3, 4):
                keep(i).start()

    def latest():
        @pl.when(parity != core)
        def _():
            across_edges().wait_recv()
            for d in range(1, shares):
                along_y(d, y).start()

    def refs(s, block, relay, b):
        other, dz = block
        c = left if s["region"] == 0 else right
        r = pl.ds(0, cols) if s["half"] is None else pl.ds(s["half"] * (cols // 2), cols // 2)
        if relay:
            return relay_ref.at[dz, r, c]
        return out_ref.at[((b + 2 * other) % xs) * zs + (z + dz) % zs, r, c]

    def copy(i):
        s = sends[i]
        src = refs(s, s["block"], s["relayed"], base)
        wx, wz = WAYS.get(s["way"], (0, 0))
        if s["lands"] == "sibling":
            dst = src
            where = {"feat": sibling}
        else:
            where = {"nodes": peers[s["way"]]}
            if s["lands"] is None:
                dst = refs(s, s["block"], True, base)
            elif s["relayed"]:
                b = (x + wx) % xs
                b = b - b % 2 + core
                dst = relay_dst(s, b)
            else:
                dst = src
        return pltpu.make_async_remote_copy(src_ref=src, dst_ref=dst, send_sem=send_sem.at[i], recv_sem=recv_sem.at[i],
                                            device_id=where, device_id_type=MESH)

    def relay_dst(s, b):
        return refs(s, (1, s["block"][1]), False, b)

    def arrival(i):
        s = sends[i]
        if s["lands"] == "sibling":
            b = x - parity + 1 - core
            dst = refs(s, s["block"], False, b)
            where = {"feat": sibling}
        else:
            where = {"nodes": peers[s["way"]]}
            dst = refs(s, s["block"], True, base) if s["lands"] is None else refs(s, s["lands"], False, base)
        return pltpu.make_async_remote_copy(src_ref=dst, dst_ref=dst, send_sem=send_sem.at[i], recv_sem=recv_sem.at[i],
                                            device_id=where, device_id_type=MESH)

    for n, (what, i) in enumerate(steps):
        if n == steps.index(("wait", next(j for w, j in steps if w == "wait"))) + after:
            later()
        if n == len(steps) // 3:
            latest()
        if what == "start":
            copy(i).start()
        else:
            arrival(i).wait_recv()
    for i in range(len(sends)):
        copy(i).wait_send()
    for d in range(1, feats):
        to_owner(d).wait()
    mine.wait()
    @pl.when(parity != core)
    def _():
        for i in range(2):
            swap(i).wait_send()
        for i in (3, 4):
            swap(i).wait()
        across_edges().wait_send()
        for d in range(1, shares):
            along_y(d, y).wait_send()
            along_y(d, (y + shares - d) % shares).wait_recv()
    @pl.when(parity == core)
    def _():
        for i in (2, 3, 4):
            keep(i).wait()

def gather(feat_t, edge_rows, src_tiles, counts, xs=4, zs=8, feats=8, cut=896, after=0, ahead=2.0, cid=1):
    cols, rows = feat_t.shape
    def seconds(s):
        n = cols * (cut if s["region"] == 0 else rows - cut) * 2 / (1 if s["half"] is None else 2)
        return n / 300e3 if s["way"] == "core" else 2 * n / 94e3
    sends, steps, end = plan_gather(zs, seconds, ahead)
    anywhere = pl.BlockSpec(memory_space=pl.ANY)
    vmem = pl.BlockSpec(memory_space=pltpu.VMEM)
    dma = pltpu.SemaphoreType.DMA
    shape = jax.ShapeDtypeStruct
    return pl.pallas_call(
        functools.partial(gather_kernel, xs=xs, zs=zs, cut=cut, sends=sends, steps=steps, after=after),
        out_shape=(shape((xs * zs, cols, rows), feat_t.dtype),
                   shape((feats, cols, rows // feats), feat_t.dtype), shape(edge_rows.shape, jnp.bfloat16),
                   shape(src_tiles.shape, src_tiles.dtype), shape(counts.shape, counts.dtype)),
        in_specs=[vmem, vmem, anywhere, anywhere],
        out_specs=(vmem,) * 3 + (anywhere,) * 2,
        scratch_shapes=[pltpu.VMEM((zs, cols, rows), feat_t.dtype), pltpu.VMEM(edge_rows.shape, jnp.bfloat16),
                        dma((len(sends),)), dma((len(sends),)), dma((feats,)), dma((feats,)), dma((5,)), dma((5,)), dma((feats // 2,)), dma((feats // 2,)), dma((7,))],
        compiler_params=pltpu.CompilerParams(collective_id=cid, has_side_effects=True, vmem_limit_bytes=24 * 2**20),
    )(feat_t, edge_rows, src_tiles, counts)

def layer_kernel(feat_ref, agg_ref, self_ref, ws_ref, wn_ref, cot_ref, act_ref, wg_ref,
                 rows_buf, swapped, lhs, base, left, gz, xout, xbuf, zout, zbuf,
                 a_send, a_recv, y_send, y_recv, x_send, x_recv, z_send, z_recv, s_send, s_recv, *, xs, zs, ys):
    me = lax.axis_index("nodes")
    f = lax.axis_index("feat")
    x, z = me // zs, me % zs
    y, core = f // 2, f % 2
    feats = 2 * ys
    cols = feat_ref.shape[0]
    own = cot_ref.shape[0]
    hidden = ws_ref.shape[1]
    chunks = hidden // 256
    half = hidden // 2

    def remote(src, dst, send, recv, **where):
        return pltpu.make_async_remote_copy(src_ref=src, dst_ref=dst, send_sem=send, recv_sem=recv,
                                            device_id=where, device_id_type=MESH)

    parity = x % 2
    pair = x - parity
    across = (pair + 1 - parity) * zs + z
    shard = 2 * y + parity

    barrier = pltpu.get_barrier_semaphore()
    for d in range(feats):
        j = (f + d) % feats
        if d:
            pl.semaphore_signal(barrier, inc=1, device_id={"feat": j}, device_id_type=MESH)
        pl.semaphore_signal(barrier, inc=1, device_id={"nodes": across, "feat": j}, device_id_type=MESH)
    for other in (x + 2, x + xs - 1 + 2 * parity):
        pl.semaphore_signal(barrier, inc=1, device_id={"nodes": (other % xs) * zs + z}, device_id_type=MESH)
    for d in range(1, zs):
        pl.semaphore_signal(barrier, inc=1, device_id={"nodes": x * zs + (z + d) % zs}, device_id_type=MESH)
    pl.semaphore_wait(barrier, 2 * feats - 1 + 2 + zs - 1)

    def to_owner(d):
        j = (f + d) % feats
        return remote(agg_ref.at[j], rows_buf.at[shard],
                      a_send.at[d], a_recv.at[shard], nodes=(pair + core) * zs + z, feat=j)
    def from_shard(i):
        return remote(rows_buf.at[i], rows_buf.at[i], a_send.at[0], a_recv.at[i],
                      nodes=(pair + i % 2) * zs + z, feat=i - i % 2 + parity)
    def swap():
        return remote(agg_ref, swapped, s_send, s_recv, nodes=across, feat=f + 1 - 2 * core)
    for d in range(1, feats):
        to_owner(d).start()
    @pl.when(parity != core)
    def _():
        to_owner(0).start()
    @pl.when(parity == core)
    def _():
        rows_buf[f] = agg_ref[f]
        for j in range(feats):
            left[cols:, j * own:(j + 1) * own] = agg_ref[j]
    left[0:cols, :] = feat_ref[...]
    lhs[...] = self_ref[...].reshape(feats * cols, own).T
    base[...] = jnp.dot(lhs[...], ws_ref[...], preferred_element_type=jnp.float32)
    for d in range(feats):
        i = (f + d) % feats
        if d:
            from_shard(i).wait_recv()
        else:
            @pl.when(parity != core)
            def _():
                from_shard(i).wait_recv()
    @pl.when(parity != core)
    def _():
        swap().start()
    lhs[...] = rows_buf[...].reshape(feats * cols, own).T

    up, down = (y + 1) % ys, (y + ys - 1) % ys
    far = (y + 2) % ys
    sibling = 2 * y + 1 - core
    hrows = own // 2
    def spread(c, k):
        by = (y, y, y, down, up, down, up, far, far)[k]
        to = (sibling, 2 * up + core, 2 * down + core, 2 * up + core, 2 * down + core) + (sibling,) * 4
        r = {3: pl.ds(0, hrows), 4: pl.ds(hrows, hrows), 7: pl.ds(0, hrows), 8: pl.ds(hrows, hrows)}.get(k, pl.ds(0, own))
        ref = gz.at[c, 2 * by + core, r]
        return remote(ref, ref, y_send.at[c, k], y_recv.at[c, k], feat=to[k])

    def columns(ref, c):
        return jnp.concatenate([ref[:, pl.ds(pl.multiple_of(c * 128, 128), 128)],
                                ref[:, pl.ds(pl.multiple_of(half + c * 128, 128), 128)]], axis=1)

    def layer(c, carry):
        v = columns(base, c) + jnp.dot(lhs[...], columns(wn_ref, c), preferred_element_type=jnp.float32)
        s = math.sqrt(2 / math.pi)
        v2 = v * v
        t = jnp.tanh(s * (v + 0.044715 * (v2 * v)))
        cdf = 0.5 * (1.0 + t)
        out = (v * cdf).astype(jnp.bfloat16)
        act_ref[:, pl.ds(pl.multiple_of(c * 128, 128), 128)] = out[:, :128]
        act_ref[:, pl.ds(pl.multiple_of(half + c * 128, 128), 128)] = out[:, 128:]
        slope = cdf + (0.5 * s) * v * (1.0 - t * t) * (1.0 + (3 * 0.044715) * v2)
        gz[c, f] = (columns(cot_ref, c).astype(jnp.float32) * slope).astype(jnp.bfloat16)
        for k in (1, 2, 0):
            spread(c, k).start()
        return carry
    lax.fori_loop(0, 2, layer, 0)

    def xcopy(c, d):
        to = (x + d) % xs
        return remote(xout.at[c, to], xbuf.at[c, d], x_send.at[c, d], x_recv.at[c, d], nodes=to * zs + z)
    def zcopy(c, p, zto):
        return remote(zout.at[c, p], zbuf.at[z], z_send.at[c, p], z_recv.at[z], nodes=x * zs + zto)

    def relay(c, carry):
        spread(c, 1).wait_recv()
        spread(c, 3).start()
        spread(c, 5).start()
        spread(c, 2).wait_recv()
        spread(c, 4).start()
        spread(c, 6).start()
        return carry
    def terms(c, carry):
        for k in (3, 4):
            spread(c, k).wait_recv()
            spread(c, k + 4).start()
        for k in (0, 5, 6, 7, 8):
            spread(c, k).wait_recv()
        g = gz[c].reshape(feats * own, 256)
        term = jnp.dot(left[...], g, preferred_element_type=jnp.float32)
        for q in range(4):
            piece = term[(q // 2) * cols:(q // 2 + 1) * cols, (q % 2) * 128:(q % 2) * 128 + 128]
            xout[c, q] = piece
        for d in range(1, xs):
            xcopy(c, d).start()
        return carry
    def sums(c, carry):
        for d in range(1, xs):
            xcopy(c, d).wait_recv()
        total = xout[c, x] + xbuf[c, 1] + xbuf[c, 2] + xbuf[c, 3]
        for p in range(2):
            zto = 2 * c + p
            piece = jnp.concatenate([total[:cols // 2, 64 * p:64 * p + 64], total[cols // 2:, 64 * p:64 * p + 64]], axis=1)
            zout[c, p] = piece
            @pl.when(zto != z)
            def _():
                zcopy(c, p, zto).start()
            @pl.when(zto == z)
            def _():
                zbuf[z] = piece
        return carry
    def stage(s, carry):
        @pl.when(s < chunks)
        def _():
            relay(s, 0)
        @pl.when(s < chunks - 2)
        def _():
            layer(s + 2, 0)
        @pl.when((s >= 1) & (s <= chunks))
        def _():
            terms(s - 1, 0)
        @pl.when(s >= 2)
        def _():
            sums(s - 2, 0)
        return carry
    @pl.when(parity != core)
    def _():
        swap().wait_recv()
        for j in range(feats):
            left[cols:, j * own:(j + 1) * own] = swapped[j]
    lax.fori_loop(0, chunks + 2, stage, 0)
    def arrived(i, carry):
        @pl.when(i != z)
        def _():
            remote(zout.at[0, 0], zbuf.at[i], z_send.at[0, 0], z_recv.at[i], nodes=x * zs + i).wait_recv()
        return carry
    lax.fori_loop(0, zs, arrived, 0)
    done = jnp.sum(zbuf[...], axis=0)
    done = jnp.concatenate([done[:, :64], done[:, 64:]], axis=0)
    done = jnp.concatenate([done, jnp.zeros_like(done)], axis=1)
    done = jnp.concatenate([done, jnp.zeros((128 - cols, 128), jnp.float32)], axis=0)
    wg_ref[...] = done.T[:64, :cols]

    def finish(c, carry):
        for k in range(9):
            spread(c, k).wait_send()
        for d in range(1, xs):
            xcopy(c, d).wait_send()
        for p in range(2):
            @pl.when(2 * c + p != z)
            def _():
                zcopy(c, p, 2 * c + p).wait_send()
        return carry
    lax.fori_loop(0, chunks, finish, 0)
    for d in range(1, feats):
        to_owner(d).wait_send()
    @pl.when(parity != core)
    def _():
        to_owner(0).wait_send()
        swap().wait_send()

def layer(feat_t, agg_t, self_rows, w_self, w_neigh, cot, xs=4, zs=8, ys=4, cid=2):
    cols, rows = feat_t.shape
    own, hidden = cot.shape
    feats, chunks = 2 * ys, hidden // 256
    v = pl.BlockSpec(memory_space=pltpu.VMEM)
    dma = pltpu.SemaphoreType.DMA
    f32, bf16 = jnp.float32, jnp.bfloat16
    return pl.pallas_call(
        functools.partial(layer_kernel, xs=xs, zs=zs, ys=ys),
        out_shape=(jax.ShapeDtypeStruct((own, hidden), bf16), jax.ShapeDtypeStruct((hidden // (xs * zs) * 2, cols), f32)),
        in_specs=[v] * 6,
        out_specs=(v, v),
        scratch_shapes=[
            pltpu.VMEM((feats, cols, own), bf16), pltpu.VMEM((feats, cols, own), bf16), pltpu.VMEM((own, feats * cols), bf16), pltpu.VMEM((own, hidden), f32),
            pltpu.VMEM((2 * cols, rows), bf16), pltpu.VMEM((chunks, feats, own, 256), bf16),
            pltpu.VMEM((chunks, 4, cols, 128), f32), pltpu.VMEM((chunks, xs, cols, 128), f32),
            pltpu.VMEM((chunks, 2, cols // 2, 128), f32), pltpu.VMEM((zs, cols // 2, 128), f32),
            dma((feats,)), dma((feats,)), dma((chunks, 9)), dma((chunks, 9)),
            dma((chunks, xs)), dma((chunks, xs)), dma((chunks, 2)), dma((zs,)), dma, dma,
        ],
        compiler_params=pltpu.CompilerParams(collective_id=cid, has_side_effects=True, vmem_limit_bytes=48 * 2**20),
    )(feat_t, agg_t, self_rows, w_self, w_neigh, cot)


def agg_kernel(src_ref, count_ref, rows_ref, g_ref, out_ref, picks_ref, *, groups):
    tiles, slots, span = rows_ref.shape
    cols = g_ref.shape[1]
    per_block = g_ref.shape[2] // span
    iota = lax.broadcasted_iota(jnp.int32, (span, span), 0).astype(jnp.float32).astype(jnp.bfloat16)
    one = jnp.ones((span, span), jnp.bfloat16)
    zero = jnp.zeros((span, span), jnp.bfloat16)
    slot_ids = lax.broadcasted_iota(jnp.int32, (slots, span), 0)

    def tile(t, carry):
        used = count_ref[t]
        picks_ref[...] = jnp.where(slot_ids < used, rows_ref[t].astype(jnp.float32), -1.0)

        def slot_group(first, size, acc):
            onehots, blocks = [], []
            for u in range(size):
                k = first + u
                pick = jnp.broadcast_to(picks_ref[pl.ds(k, 1), :], (16, span)).astype(jnp.bfloat16)
                pick = jnp.concatenate([pick] * (span // 16), axis=0)
                onehots.append(jnp.where(pick == iota, one, zero))
                s = src_ref[t, k]
                start = pl.multiple_of((s % per_block) * span, span)
                blocks.append(g_ref[s // per_block, :, pl.ds(start, span)])
            return acc + jnp.dot(
                jnp.concatenate(blocks, axis=1),
                jnp.concatenate(onehots, axis=0),
                preferred_element_type=jnp.float32,
            )

        total, first = jnp.zeros((cols, span), jnp.float32), 0
        for size in groups:
            left = used - first
            trips = (left + size - 1) // size if size == groups[-1] else left // size
            total = lax.fori_loop(0, trips, lambda i, acc, first=first, size=size: slot_group(first + i * size, size, acc), total)
            first = first + trips * size
        mean = total / used.astype(jnp.float32)
        out_ref[t] = mean.astype(jnp.bfloat16)
        return carry

    lax.fori_loop(0, tiles, tile, 0)


def neighbour_mean(src_tiles, counts, edge_rows, gathered):
    tiles, slots, span = edge_rows.shape
    cols = gathered.shape[1]
    smem = pl.BlockSpec(memory_space=pltpu.SMEM)
    vmem = pl.BlockSpec(memory_space=pltpu.VMEM)
    return pl.pallas_call(
        functools.partial(agg_kernel, groups=GROUPS),
        out_shape=jax.ShapeDtypeStruct((tiles, cols, span), jnp.bfloat16),
        in_specs=[smem, smem, vmem, vmem],
        out_specs=pl.BlockSpec(memory_space=pltpu.VMEM),
        scratch_shapes=[pltpu.VMEM((slots, span), jnp.float32)],
        compiler_params=pltpu.CompilerParams(vmem_limit_bytes=24 * 2**20),
    )(src_tiles, counts, edge_rows, gathered)


def per_device(features, w_self, w_neigh, src_tiles, counts, edge_rows, cotangent):
    feat_t = features.T
    gathered, self_rows, edge_rows, src_tiles, counts = gather(feat_t, edge_rows, src_tiles, counts)
    agg_t = neighbour_mean(src_tiles, counts, edge_rows, gathered)
    activations, grads_t = layer(feat_t, agg_t, self_rows, w_self, w_neigh, cotangent)
    return activations, grads_t.T


def solution(mesh):
    in_specs = (
        P("nodes", "feat"),
        P(),
        P(),
        P("nodes", None),
        P("nodes"),
        P("nodes", None, None),
        P(("nodes", "feat"), None),
    )
    out_specs = (P(("nodes", "feat"), None), P("feat", "nodes"))
    return jax.shard_map(
        per_device, mesh=mesh, in_specs=in_specs, out_specs=out_specs, check_vma=False
    )
```

```python
import functools
import math

import jax
import jax.numpy as jnp
from jax import lax
from jax.experimental import pallas as pl
from jax.experimental.pallas import tpu as pltpu
from jax.sharding import PartitionSpec as P

GROUPS = (64, 32, 16, 8)
MESH = pl.DeviceIdType.MESH
WAYS = {"x+": (1, 0), "x-": (-1, 0), "z+": (0, 1), "z-": (0, -1)}

def plan_gather(zs, seconds, ahead=4.0):
    sends, have = [], {}

    def add(way, block, region, half, passing, get):
        deps = [] if passing is None else [passing]
        if passing is None:
            for h in (0, 1) if half is None else (half,):
                deps += have.get((block, region, h), [])
        sends.append(dict(way=way, block=block, region=region, half=half, relayed=passing is not None,
                          lands=get, deps=sorted(set(deps))))
        if get is not None and get != "sibling":
            for h in (0, 1) if half is None else (half,):
                have[(get, region, h)] = [len(sends) - 1]
        return len(sends) - 1

    def along_z(other, region):
        for d in range(1, zs // 2 + 1):
            for way, s in (("z+", 1), ("z-", -1)):
                half = None if d < zs // 2 else (0 if s == 1 else 1)
                add(way, (other, -s * (d - 1) % zs), region, half, None, (other, -s * d % zs))

    def along_x(dz, region):
        for way, half in (("x+", 0), ("x-", 1)):
            first = add(way, (0, dz), region, half, None, None)
            add(way, (0, dz), region, half, first, (1, dz))

    order = [0]
    for d in range(1, zs // 2):
        order += [d, zs - d]
    order += [zs // 2]
    along_x(0, 0)
    along_z(0, 1)
    along_z(0, 0)
    along_z(1, 0)
    for dz in order:
        along_x(dz, 1)
    for other in (0, 1):
        for dz in order:
            for region in (0, 1):
                add("core", (other, dz), region, None, None, "sibling")

    n = len(sends)
    chain = [0] * n
    for i in reversed(range(n)):
        for d in sends[i]["deps"]:
            chain[d] = max(chain[d], chain[i] + 1)
    free, arrive, starts, todo = {}, {}, {}, set(range(n))
    while todo:
        best = None
        for i in todo:
            if all(d in arrive for d in sends[i]["deps"]):
                ready = max([arrive[d] for d in sends[i]["deps"]], default=0.0)
                at = max(ready, free.get(sends[i]["way"], 0.0))
                key = (at, -chain[i], ready, i)
                best = key if best is None else min(best, key)
        at, _, _, i = best
        todo.remove(i)
        starts[i] = at
        free[sends[i]["way"]] = at + seconds(sends[i])
        arrive[i] = at + seconds(sends[i]) + 1.5
    steps, waited = [], set()
    when = {i: max([arrive[d] for d in sends[i]["deps"]] + [starts[i] - ahead]) for i in range(n)}
    for i in sorted(range(n), key=lambda i: (when[i], starts[i], i)):
        for d in sorted(sends[i]["deps"], key=lambda d: arrive[d]):
            if d not in waited:
                waited.add(d)
                steps.append(("wait", d))
        steps.append(("start", i))
    steps += [("wait", d) for d in sorted(range(n), key=lambda d: arrive[d]) if d not in waited]
    return sends, steps, max(arrive.values())

def gather_kernel(feat_ref, edge_ref, src_ref, count_ref, out_ref, self_ref, edge_out, src_out, count_out,
                  relay_ref, edge_half,
                  send_sem, recv_sem, row_send, row_recv, swap_send, swap_recv, edge_send, edge_recv, own_sem, *, xs, zs, cut, sends, steps, after):
    me = lax.axis_index("nodes")
    f = lax.axis_index("feat")
    feats = lax.axis_size("feat")
    x, z = me // zs, me % zs
    core, parity = f % 2, x % 2
    cols, rows = feat_ref.shape
    own = rows // feats
    sibling = f + 1 - 2 * core
    across = (x + 1 - 2 * parity) * zs + z
    base = (x - parity + core)
    home = base * zs + z
    peers = {w: ((x + dx) % xs) * zs + (z + dz) % zs for w, (dx, dz) in WAYS.items()}

    barrier = pltpu.get_barrier_semaphore()
    for w in peers:
        pl.semaphore_signal(barrier, inc=1, device_id={"nodes": peers[w]}, device_id_type=MESH)
    for d in range(1, feats):
        pl.semaphore_signal(barrier, inc=1, device_id={"feat": (f + d) % feats}, device_id_type=MESH)
    pl.semaphore_signal(barrier, inc=1, device_id={"nodes": across, "feat": sibling}, device_id_type=MESH)
    pl.semaphore_wait(barrier, len(peers) + feats)

    left, right = pl.ds(0, cut), pl.ds(cut, rows - cut)
    moves = ((feat_ref.at[:, left], out_ref.at[home, :, left]), (feat_ref.at[:, right], out_ref.at[home, :, right]),
             (edge_half, edge_out), (src_ref, src_out), (count_ref, count_out))
    theirs = (x + 1 - 2 * parity) - (1 - parity) + (1 - core)
    theirs = theirs * zs + z
    there = (out_ref.at[theirs, :, left], out_ref.at[theirs, :, right], edge_out, src_out, count_out)

    def swap(i):
        return pltpu.make_async_remote_copy(
            src_ref=moves[i][0], dst_ref=there[i], send_sem=swap_send.at[i], recv_sem=swap_recv.at[i],
            device_id={"nodes": across, "feat": sibling}, device_id_type=MESH)
    y, shares = f // 2, feats // 2
    part = edge_ref.shape[0] // shares
    def share(n):
        return pl.ds(n * part, part)
    def across_edges():
        return pltpu.make_async_remote_copy(
            src_ref=edge_half.at[share(y)], dst_ref=edge_out.at[share(y)], send_sem=edge_send.at[0], recv_sem=edge_recv.at[0],
            device_id={"nodes": across, "feat": sibling}, device_id_type=MESH)
    def along_y(d, owner):
        return pltpu.make_async_remote_copy(
            src_ref=edge_out.at[share(owner)], dst_ref=edge_out.at[share(owner)], send_sem=edge_send.at[d],
            recv_sem=edge_recv.at[d], device_id={"feat": (f + 2 * d) % feats}, device_id_type=MESH)
    def keep(i):
        return pltpu.make_async_copy(moves[i][0], moves[i][1], own_sem.at[i])

    def to_owner(d):
        j = (f + d) % feats
        return pltpu.make_async_remote_copy(
            src_ref=feat_ref.at[:, pl.ds(pl.multiple_of(j * own, own), own)], dst_ref=self_ref.at[f],
            send_sem=row_send.at[d], recv_sem=row_recv.at[d], device_id={"feat": j}, device_id_type=MESH)

    @pl.when(parity != core)
    def _():
        for i in (0, 1):
            swap(i).start()
    @pl.when(parity == core)
    def _():
        for i in (0, 1):
            keep(i).start()
    mine = pltpu.make_async_copy(feat_ref.at[:, pl.ds(pl.multiple_of(f * own, own), own)], self_ref.at[f], own_sem.at[5])
    mine.start()
    @pl.when(parity != core)
    def _():
        for i in (0, 1):
            swap(i).wait_recv()
    @pl.when(parity == core)
    def _():
        for i in (0, 1):
            keep(i).wait()

    def later():
        def narrow(t, carry):
            edge_half[t] = edge_ref[t].astype(jnp.float32).astype(jnp.bfloat16)
            return carry
        lax.fori_loop(0, edge_ref.shape[0], narrow, 0)
        for d in range(1, feats):
            to_owner(d).start()
        @pl.when(parity != core)
        def _():
            across_edges().start()
            for i in (3, 4):
                swap(i).start()
        @pl.when(parity == core)
        def _():
            for i in (2, 3, 4):
                keep(i).start()

    def latest():
        @pl.when(parity != core)
        def _():
            across_edges().wait_recv()
            for d in range(1, shares):
                along_y(d, y).start()

    def refs(s, block, relay, b):
        other, dz = block
        c = left if s["region"] == 0 else right
        r = pl.ds(0, cols) if s["half"] is None else pl.ds(s["half"] * (cols // 2), cols // 2)
        if relay:
            return relay_ref.at[dz, r, c]
        return out_ref.at[((b + 2 * other) % xs) * zs + (z + dz) % zs, r, c]

    def copy(i):
        s = sends[i]
        src = refs(s, s["block"], s["relayed"], base)
        wx, wz = WAYS.get(s["way"], (0, 0))
        if s["lands"] == "sibling":
            dst = src
            where = {"feat": sibling}
        else:
            where = {"nodes": peers[s["way"]]}
            if s["lands"] is None:
                dst = refs(s, s["block"], True, base)
            elif s["relayed"]:
                b = (x + wx) % xs
                b = b - b % 2 + core
                dst = relay_dst(s, b)
            else:
                dst = src
        return pltpu.make_async_remote_copy(src_ref=src, dst_ref=dst, send_sem=send_sem.at[i], recv_sem=recv_sem.at[i],
                                            device_id=where, device_id_type=MESH)

    def relay_dst(s, b):
        return refs(s, (1, s["block"][1]), False, b)

    def arrival(i):
        s = sends[i]
        if s["lands"] == "sibling":
            b = x - parity + 1 - core
            dst = refs(s, s["block"], False, b)
            where = {"feat": sibling}
        else:
            where = {"nodes": peers[s["way"]]}
            dst = refs(s, s["block"], True, base) if s["lands"] is None else refs(s, s["lands"], False, base)
        return pltpu.make_async_remote_copy(src_ref=dst, dst_ref=dst, send_sem=send_sem.at[i], recv_sem=recv_sem.at[i],
                                            device_id=where, device_id_type=MESH)

    for n, (what, i) in enumerate(steps):
        if n == steps.index(("wait", next(j for w, j in steps if w == "wait"))) + after:
            later()
        if n == len(steps) // 3:
            latest()
        if what == "start":
            copy(i).start()
        else:
            arrival(i).wait_recv()
    for i in range(len(sends)):
        copy(i).wait_send()
    for d in range(1, feats):
        to_owner(d).wait()
    mine.wait()
    @pl.when(parity != core)
    def _():
        for i in range(2):
            swap(i).wait_send()
        for i in (3, 4):
            swap(i).wait()
        across_edges().wait_send()
        for d in range(1, shares):
            along_y(d, y).wait_send()
            along_y(d, (y + shares - d) % shares).wait_recv()
    @pl.when(parity == core)
    def _():
        for i in (2, 3, 4):
            keep(i).wait()

def gather(feat_t, edge_rows, src_tiles, counts, xs=4, zs=8, feats=8, cut=896, after=0, ahead=2.0, cid=1):
    cols, rows = feat_t.shape
    def seconds(s):
        n = cols * (cut if s["region"] == 0 else rows - cut) * 2 / (1 if s["half"] is None else 2)
        return n / 300e3 if s["way"] == "core" else 2 * n / 94e3
    sends, steps, end = plan_gather(zs, seconds, ahead)
    anywhere = pl.BlockSpec(memory_space=pl.ANY)
    vmem = pl.BlockSpec(memory_space=pltpu.VMEM)
    dma = pltpu.SemaphoreType.DMA
    shape = jax.ShapeDtypeStruct
    return pl.pallas_call(
        functools.partial(gather_kernel, xs=xs, zs=zs, cut=cut, sends=sends, steps=steps, after=after),
        out_shape=(shape((xs * zs, cols, rows), feat_t.dtype),
                   shape((feats, cols, rows // feats), feat_t.dtype), shape(edge_rows.shape, jnp.bfloat16),
                   shape(src_tiles.shape, src_tiles.dtype), shape(counts.shape, counts.dtype)),
        in_specs=[vmem, vmem, anywhere, anywhere],
        out_specs=(vmem,) * 3 + (anywhere,) * 2,
        scratch_shapes=[pltpu.VMEM((zs, cols, rows), feat_t.dtype), pltpu.VMEM(edge_rows.shape, jnp.bfloat16),
                        dma((len(sends),)), dma((len(sends),)), dma((feats,)), dma((feats,)), dma((5,)), dma((5,)), dma((feats // 2,)), dma((feats // 2,)), dma((7,))],
        compiler_params=pltpu.CompilerParams(collective_id=cid, has_side_effects=True, vmem_limit_bytes=24 * 2**20),
    )(feat_t, edge_rows, src_tiles, counts)

def layer_kernel(feat_ref, agg_ref, self_ref, ws_ref, wn_ref, cot_ref, act_ref, wg_ref,
                 rows_buf, swapped, lhs, base, left, gz, xout, xbuf, zout, zbuf,
                 a_send, a_recv, y_send, y_recv, x_send, x_recv, z_send, z_recv, s_send, s_recv, *, xs, zs, ys):
    me = lax.axis_index("nodes")
    f = lax.axis_index("feat")
    x, z = me // zs, me % zs
    y, core = f // 2, f % 2
    feats = 2 * ys
    cols = feat_ref.shape[0]
    own = cot_ref.shape[0]
    hidden = ws_ref.shape[1]
    chunks = hidden // 256
    half = hidden // 2

    def remote(src, dst, send, recv, **where):
        return pltpu.make_async_remote_copy(src_ref=src, dst_ref=dst, send_sem=send, recv_sem=recv,
                                            device_id=where, device_id_type=MESH)

    parity = x % 2
    pair = x - parity
    across = (pair + 1 - parity) * zs + z
    shard = 2 * y + parity

    barrier = pltpu.get_barrier_semaphore()
    for d in range(feats):
        j = (f + d) % feats
        if d:
            pl.semaphore_signal(barrier, inc=1, device_id={"feat": j}, device_id_type=MESH)
        pl.semaphore_signal(barrier, inc=1, device_id={"nodes": across, "feat": j}, device_id_type=MESH)
    for other in (x + 2, x + xs - 1 + 2 * parity):
        pl.semaphore_signal(barrier, inc=1, device_id={"nodes": (other % xs) * zs + z}, device_id_type=MESH)
    for d in range(1, zs):
        pl.semaphore_signal(barrier, inc=1, device_id={"nodes": x * zs + (z + d) % zs}, device_id_type=MESH)
    pl.semaphore_wait(barrier, 2 * feats - 1 + 2 + zs - 1)

    def to_owner(d):
        j = (f + d) % feats
        return remote(agg_ref.at[j], rows_buf.at[shard],
                      a_send.at[d], a_recv.at[shard], nodes=(pair + core) * zs + z, feat=j)
    def from_shard(i):
        return remote(rows_buf.at[i], rows_buf.at[i], a_send.at[0], a_recv.at[i],
                      nodes=(pair + i % 2) * zs + z, feat=i - i % 2 + parity)
    def swap():
        return remote(agg_ref, swapped, s_send, s_recv, nodes=across, feat=f + 1 - 2 * core)
    for d in range(1, feats):
        to_owner(d).start()
    @pl.when(parity != core)
    def _():
        to_owner(0).start()
    @pl.when(parity == core)
    def _():
        rows_buf[f] = agg_ref[f]
        for j in range(feats):
            left[cols:, j * own:(j + 1) * own] = agg_ref[j]
    left[0:cols, :] = feat_ref[...]
    lhs[...] = self_ref[...].reshape(feats * cols, own).T
    base[...] = jnp.dot(lhs[...], ws_ref[...], preferred_element_type=jnp.float32)
    for d in range(feats):
        i = (f + d) % feats
        if d:
            from_shard(i).wait_recv()
        else:
            @pl.when(parity != core)
            def _():
                from_shard(i).wait_recv()
    @pl.when(parity != core)
    def _():
        swap().start()
    lhs[...] = rows_buf[...].reshape(feats * cols, own).T

    up, down = (y + 1) % ys, (y + ys - 1) % ys
    far = (y + 2) % ys
    sibling = 2 * y + 1 - core
    hrows = own // 2
    def spread(c, k):
        by = (y, y, y, down, up, down, up, far, far)[k]
        to = (sibling, 2 * up + core, 2 * down + core, 2 * up + core, 2 * down + core) + (sibling,) * 4
        r = {3: pl.ds(0, hrows), 4: pl.ds(hrows, hrows), 7: pl.ds(0, hrows), 8: pl.ds(hrows, hrows)}.get(k, pl.ds(0, own))
        ref = gz.at[c, 2 * by + core, r]
        return remote(ref, ref, y_send.at[c, k], y_recv.at[c, k], feat=to[k])

    def columns(ref, c):
        return jnp.concatenate([ref[:, pl.ds(pl.multiple_of(c * 128, 128), 128)],
                                ref[:, pl.ds(pl.multiple_of(half + c * 128, 128), 128)]], axis=1)

    def layer(c, carry):
        v = columns(base, c) + jnp.dot(lhs[...], columns(wn_ref, c), preferred_element_type=jnp.float32)
        s = math.sqrt(2 / math.pi)
        v2 = v * v
        t = jnp.tanh(s * (v + 0.044715 * (v2 * v)))
        cdf = 0.5 * (1.0 + t)
        out = (v * cdf).astype(jnp.bfloat16)
        act_ref[:, pl.ds(pl.multiple_of(c * 128, 128), 128)] = out[:, :128]
        act_ref[:, pl.ds(pl.multiple_of(half + c * 128, 128), 128)] = out[:, 128:]
        slope = cdf + (0.5 * s) * v * (1.0 - t * t) * (1.0 + (3 * 0.044715) * v2)
        gz[c, f] = (columns(cot_ref, c).astype(jnp.float32) * slope).astype(jnp.bfloat16)
        for k in (1, 2, 0):
            spread(c, k).start()
        return carry
    lax.fori_loop(0, 2, layer, 0)

    def xcopy(c, d):
        to = (x + d) % xs
        return remote(xout.at[c, to], xbuf.at[c, d], x_send.at[c, d], x_recv.at[c, d], nodes=to * zs + z)
    def zcopy(c, p, zto):
        return remote(zout.at[c, p], zbuf.at[z], z_send.at[c, p], z_recv.at[z], nodes=x * zs + zto)

    def relay(c, carry):
        spread(c, 1).wait_recv()
        spread(c, 3).start()
        spread(c, 5).start()
        spread(c, 2).wait_recv()
        spread(c, 4).start()
        spread(c, 6).start()
        return carry
    def terms(c, carry):
        for k in (3, 4):
            spread(c, k).wait_recv()
            spread(c, k + 4).start()
        for k in (0, 5, 6, 7, 8):
            spread(c, k).wait_recv()
        g = gz[c].reshape(feats * own, 256)
        term = jnp.dot(left[...], g, preferred_element_type=jnp.float32)
        for q in range(4):
            piece = term[(q // 2) * cols:(q // 2 + 1) * cols, (q % 2) * 128:(q % 2) * 128 + 128]
            xout[c, q] = piece
        for d in range(1, xs):
            xcopy(c, d).start()
        return carry
    def sums(c, carry):
        for d in range(1, xs):
            xcopy(c, d).wait_recv()
        total = xout[c, x] + xbuf[c, 1] + xbuf[c, 2] + xbuf[c, 3]
        for p in range(2):
            zto = 2 * c + p
            piece = jnp.concatenate([total[:cols // 2, 64 * p:64 * p + 64], total[cols // 2:, 64 * p:64 * p + 64]], axis=1)
            zout[c, p] = piece
            @pl.when(zto != z)
            def _():
                zcopy(c, p, zto).start()
            @pl.when(zto == z)
            def _():
                zbuf[z] = piece
        return carry
    def stage(s, carry):
        @pl.when(s < chunks)
        def _():
            relay(s, 0)
        @pl.when(s < chunks - 2)
        def _():
            layer(s + 2, 0)
        @pl.when((s >= 1) & (s <= chunks))
        def _():
            terms(s - 1, 0)
        @pl.when(s >= 2)
        def _():
            sums(s - 2, 0)
        return carry
    @pl.when(parity != core)
    def _():
        swap().wait_recv()
        for j in range(feats):
            left[cols:, j * own:(j + 1) * own] = swapped[j]
    lax.fori_loop(0, chunks + 2, stage, 0)
    def arrived(i, carry):
        @pl.when(i != z)
        def _():
            remote(zout.at[0, 0], zbuf.at[i], z_send.at[0, 0], z_recv.at[i], nodes=x * zs + i).wait_recv()
        return carry
    lax.fori_loop(0, zs, arrived, 0)
    done = jnp.sum(zbuf[...], axis=0)
    done = jnp.concatenate([done[:, :64], done[:, 64:]], axis=0)
    done = jnp.concatenate([done, jnp.zeros_like(done)], axis=1)
    done = jnp.concatenate([done, jnp.zeros((128 - cols, 128), jnp.float32)], axis=0)
    wg_ref[...] = done.T[:64, :cols]

    def finish(c, carry):
        for k in range(9):
            spread(c, k).wait_send()
        for d in range(1, xs):
            xcopy(c, d).wait_send()
        for p in range(2):
            @pl.when(2 * c + p != z)
            def _():
                zcopy(c, p, 2 * c + p).wait_send()
        return carry
    lax.fori_loop(0, chunks, finish, 0)
    for d in range(1, feats):
        to_owner(d).wait_send()
    @pl.when(parity != core)
    def _():
        to_owner(0).wait_send()
        swap().wait_send()

def layer(feat_t, agg_t, self_rows, w_self, w_neigh, cot, xs=4, zs=8, ys=4, cid=2):
    cols, rows = feat_t.shape
    own, hidden = cot.shape
    feats, chunks = 2 * ys, hidden // 256
    v = pl.BlockSpec(memory_space=pltpu.VMEM)
    dma = pltpu.SemaphoreType.DMA
    f32, bf16 = jnp.float32, jnp.bfloat16
    return pl.pallas_call(
        functools.partial(layer_kernel, xs=xs, zs=zs, ys=ys),
        out_shape=(jax.ShapeDtypeStruct((own, hidden), bf16), jax.ShapeDtypeStruct((hidden // (xs * zs) * 2, cols), f32)),
        in_specs=[v] * 6,
        out_specs=(v, v),
        scratch_shapes=[
            pltpu.VMEM((feats, cols, own), bf16), pltpu.VMEM((feats, cols, own), bf16), pltpu.VMEM((own, feats * cols), bf16), pltpu.VMEM((own, hidden), f32),
            pltpu.VMEM((2 * cols, rows), bf16), pltpu.VMEM((chunks, feats, own, 256), bf16),
            pltpu.VMEM((chunks, 4, cols, 128), f32), pltpu.VMEM((chunks, xs, cols, 128), f32),
            pltpu.VMEM((chunks, 2, cols // 2, 128), f32), pltpu.VMEM((zs, cols // 2, 128), f32),
            dma((feats,)), dma((feats,)), dma((chunks, 9)), dma((chunks, 9)),
            dma((chunks, xs)), dma((chunks, xs)), dma((chunks, 2)), dma((zs,)), dma, dma,
        ],
        compiler_params=pltpu.CompilerParams(collective_id=cid, has_side_effects=True, vmem_limit_bytes=48 * 2**20),
    )(feat_t, agg_t, self_rows, w_self, w_neigh, cot)


def agg_kernel(src_ref, count_ref, rows_ref, g_ref, out_ref, picks_ref, *, groups):
    tiles, slots, span = rows_ref.shape
    cols = g_ref.shape[1]
    per_block = g_ref.shape[2] // span
    iota = lax.broadcasted_iota(jnp.int32, (span, span), 0).astype(jnp.float32).astype(jnp.bfloat16)
    one = jnp.ones((span, span), jnp.bfloat16)
    zero = jnp.zeros((span, span), jnp.bfloat16)
    slot_ids = lax.broadcasted_iota(jnp.int32, (slots, span), 0)

    def tile(t, carry):
        used = count_ref[t]
        picks_ref[...] = jnp.where(slot_ids < used, rows_ref[t].astype(jnp.float32), -1.0)

        def slot_group(first, size, acc):
            onehots, blocks = [], []
            for u in range(size):
                k = first + u
                pick = jnp.broadcast_to(picks_ref[pl.ds(k, 1), :], (16, span)).astype(jnp.bfloat16)
                pick = jnp.concatenate([pick] * (span // 16), axis=0)
                onehots.append(jnp.where(pick == iota, one, zero))
                s = src_ref[t, k]
                start = pl.multiple_of((s % per_block) * span, span)
                blocks.append(g_ref[s // per_block, :, pl.ds(start, span)])
            return acc + jnp.dot(
                jnp.concatenate(blocks, axis=1),
                jnp.concatenate(onehots, axis=0),
                preferred_element_type=jnp.float32,
            )

        total, first = jnp.zeros((cols, span), jnp.float32), 0
        for size in groups:
            left = used - first
            trips = (left + size - 1) // size if size == groups[-1] else left // size
            total = lax.fori_loop(0, trips, lambda i, acc, first=first, size=size: slot_group(first + i * size, size, acc), total)
            first = first + trips * size
        mean = total / used.astype(jnp.float32)
        out_ref[t] = mean.astype(jnp.bfloat16)
        return carry

    lax.fori_loop(0, tiles, tile, 0)


def neighbour_mean(src_tiles, counts, edge_rows, gathered):
    tiles, slots, span = edge_rows.shape
    cols = gathered.shape[1]
    smem = pl.BlockSpec(memory_space=pltpu.SMEM)
    vmem = pl.BlockSpec(memory_space=pltpu.VMEM)
    return pl.pallas_call(
        functools.partial(agg_kernel, groups=GROUPS),
        out_shape=jax.ShapeDtypeStruct((tiles, cols, span), jnp.bfloat16),
        in_specs=[smem, smem, vmem, vmem],
        out_specs=pl.BlockSpec(memory_space=pltpu.VMEM),
        scratch_shapes=[pltpu.VMEM((slots, span), jnp.float32)],
        compiler_params=pltpu.CompilerParams(vmem_limit_bytes=24 * 2**20),
    )(src_tiles, counts, edge_rows, gathered)


def per_device(features, w_self, w_neigh, src_tiles, counts, edge_rows, cotangent):
    feat_t = features.T
    gathered, self_rows, edge_rows, src_tiles, counts = gather(feat_t, edge_rows, src_tiles, counts)
    agg_t = neighbour_mean(src_tiles, counts, edge_rows, gathered)
    activations, grads_t = layer(feat_t, agg_t, self_rows, w_self, w_neigh, cotangent)
    return activations, grads_t.T


def solution(mesh):
    in_specs = (
        P("nodes", "feat"),
        P(),
        P(),
        P("nodes", None),
        P("nodes"),
        P("nodes", None, None),
        P(("nodes", "feat"), None),
    )
    out_specs = (P(("nodes", "feat"), None), P("feat", "nodes"))
    return jax.shard_map(
        per_device, mesh=mesh, in_specs=in_specs, out_specs=out_specs, check_vma=False
    )
```
